32 devices in a mesh: ctx: 8 (over z, y), fsdp: 4 (over x, core).
Axes of the slice: x: 2, y: 2, z: 4, core: 2. Of those that a mesh axis runs over, the one named last changes fastest.
Arguments:
- residual_in: bfloat16 [4, 1024, 768], P('fsdp', 'ctx'), may hold values from -6 to 6
- cotangent: float32 [4, 1024, 768], P('fsdp', 'ctx'), may hold values from -6 to 6
- group_order: int32 [16], replicated, may hold values from 0 to 15, each once
- gain_first: float32 [768], P('fsdp'), may hold values from 0.5 to 1.5
- shift_first: float32 [768], P('fsdp'), may hold values from -3 to 3
- gain_second: float32 [768], P('fsdp'), may hold values from 0.5 to 1.5
- shift_second: float32 [768], P('fsdp'), may hold values from -3 to 3
- heads_weight: float32 [768, 2304], P('fsdp')
- heads_bias: float32 [2304], P('fsdp'), may hold values from -3 to 3
- output_weight: float32 [768, 768], P('fsdp'), may hold values from -6 to 6
- output_bias: float32 [768], P('fsdp'), may hold values from -3 to 3
- up_weight: float32 [768, 3072], P('fsdp'), may hold values from -0.21875 to 0.21875
- up_bias: float32 [3072], P('fsdp'), may hold values from -3 to 3
- down_weight: float32 [768, 3072], P('fsdp'), may hold values from -0.109375 to 0.109375
- down_bias: float32 [768], P('fsdp'), may hold values from -3 to 3
- heads_moment: float32 [768, 2304], P('fsdp')
- output_moment: float32 [768, 768], P('fsdp')
- up_moment: float32 [768, 3072], P('fsdp')
- down_moment: float32 [768, 3072], P('fsdp')
Outputs:
- block_out: bfloat16 [4, 1024, 768], P('fsdp', 'ctx')
- input_grad: float32 [4, 1024, 768], P('fsdp', 'ctx')
- grad_gain_first: float32 [768], P('fsdp')
- grad_shift_first: float32 [768], P('fsdp')
- grad_gain_second: float32 [768], P('fsdp')
- grad_shift_second: float32 [768], P('fsdp')
- grad_heads_weight: float32 [768, 2304], P('fsdp')
- grad_heads_bias: float32 [2304], P('fsdp')
- grad_output_weight: float32 [768, 768], P('fsdp')
- grad_output_bias: float32 [768], P('fsdp')
- grad_up_weight: float32 [768, 3072], P('fsdp')
- grad_up_bias: float32 [3072], P('fsdp')
- grad_down_weight: float32 [768, 3072], P('fsdp')
- grad_down_bias: float32 [768], P('fsdp')
- new_gain_first: float32 [768], P('fsdp')
- new_shift_first: float32 [768], P('fsdp')
- new_gain_second: float32 [768], P('fsdp')
- new_shift_second: float32 [768], P('fsdp')
- new_heads_weight: float32 [768, 2304], P('fsdp')
- new_heads_bias: float32 [2304], P('fsdp')
- new_output_weight: float32 [768, 768], P('fsdp')
- new_output_bias: float32 [768], P('fsdp')
- new_up_weight: float32 [768, 3072], P('fsdp')
- new_up_bias: float32 [3072], P('fsdp')
- new_down_weight: float32 [768, 3072], P('fsdp')
- new_down_bias: float32 [768], P('fsdp')
- new_heads_moment: float32 [768, 2304], P('fsdp')
- new_output_moment: float32 [768, 768], P('fsdp')
- new_up_moment: float32 [768, 3072], P('fsdp')
- new_down_moment: float32 [768, 3072], P('fsdp')
The draws below stay inside these ranges and needn't reach their ends.
Inputs may be any that keep to these rules, and one draw needn't show every extreme that they name: Storage slot s of every sequence, rows s * 64 to (s + 1) * 64 - 1, holds group group_order[s] of the sequence; each group once.
All inputs are finite; a program needn't handle non-finite values.
Results may differ from the reference program's by a relative error of at most 0.035.
Values may be sent and summed in bfloat16 or wider, within the bound.
No kernel may reach another device: no remote copies, remote signals or barrier semaphores. Data moves between devices by JAX's collectives and lax.ppermute only.
A program may use at most 192 MiB of HBM per device.

```python
import math
import jax
import jax.numpy as jnp
from jax import lax

D = 768
HEADS = 12
HD = 64
ROT = 16
FF = 3072
NS_ITERS = 5
GROUP = 64
LEN = 1024
SEQS = 4
TOKENS = 4096
N_CTX = 8


def draw_heads_weight(key, part):
    first = jax.random.fold_in(jax.random.fold_in(key, 11), 0)
    base = jnp.clip(jax.random.normal(first, (D, 3 * D), jnp.float32), -6.0, 6.0) / jnp.sqrt(jnp.float32(D))
    return base


def moment_draw(key, rows, cols, factor):
    noise = jnp.clip(jax.random.normal(key, (rows, cols), jnp.float32), -6.0, 6.0)
    return factor * jnp.sqrt(jnp.float32(TOKENS)) * noise


def draw_heads_moment(key, part):
    return moment_draw(jax.random.fold_in(key, 21), D, 3 * D, 1.5)


def draw_output_moment(key, part):
    return moment_draw(jax.random.fold_in(key, 22), D, D, 0.045)


def draw_up_moment(key, part):
    return moment_draw(jax.random.fold_in(key, 23), D, FF, 0.15)


def draw_down_moment(key, part):
    return moment_draw(jax.random.fold_in(key, 24), D, FF, 0.3)


def levels(key, extent, cuts, low, largest):
    level = 1.0
    for position, shards_of in cuts:
        heights = jax.random.uniform(jax.random.fold_in(jax.random.fold_in(key, 6), position), (shards_of,), jnp.float32, low / len(cuts), largest / len(cuts))
        level = level * jnp.repeat(jnp.exp(heights), extent[position] // shards_of).reshape((-1,) + (1,) * (len(extent) - 1 - position))
    return level


def scatter_about(own_key, dims, scale, bound, shards=(), kind=jnp.bfloat16):
    drawn = jax.random.normal(own_key, dims, jnp.float32) * scale
    if len(shards) > 0:
        drawn = levels(own_key, dims, shards, -0.22, 0.18) * drawn
    return jnp.clip(drawn, min=-bound, max=bound).astype(kind)


def setup_inputs(seed: int = 0) -> dict:
    seeds = jax.random.split(jax.random.key(seed), 20)
    return {
        "residual_in": scatter_about(seeds[0], (SEQS, LEN, D), 1.0, 6.0, ((0, 4), (1, 8))),
        "cotangent": scatter_about(seeds[1], (SEQS, LEN, D), 1.0, 6.0, ((0, 4), (1, 8)), jnp.float32),
        "group_order": jax.random.permutation(seeds[2], 2 * N_CTX).astype(jnp.int32),
        "gain_first": jnp.clip(1.0 + 0.1 * jax.random.normal(seeds[3], (D,), jnp.float32), 0.5, 1.5),
        "shift_first": scatter_about(seeds[4], (D,), 0.3, 3.0, ((0, 4),), jnp.float32),
        "gain_second": jnp.clip(1.0 + 0.1 * jax.random.normal(seeds[5], (D,), jnp.float32), 0.5, 1.5),
        "shift_second": scatter_about(seeds[6], (D,), 0.3, 3.0, ((0, 4),), jnp.float32),
        "heads_weight": draw_heads_weight(jax.random.fold_in(seeds[19], 71), 0),
        "heads_bias": scatter_about(seeds[8], (3 * D,), 0.3, 3.0, ((0, 4),), jnp.float32),
        "output_weight": scatter_about(seeds[9], (D, D), 1 ** -0.5, 6.0, ((0, 4),), jnp.float32),
        "output_bias": scatter_about(seeds[10], (D,), 0.3, 3.0, ((0, 4),), jnp.float32),
        "up_weight": scatter_about(seeds[11], (D, FF), D ** -0.5, 0.21875, ((0, 4),), jnp.float32),
        "up_bias": scatter_about(seeds[12], (FF,), 0.3, 3.0, ((0, 4),), jnp.float32),
        "down_weight": scatter_about(seeds[13], (D, FF), FF ** -0.5, 0.109375, ((0, 4),), jnp.float32),
        "down_bias": scatter_about(seeds[14], (D,), 0.3, 3.0, ((0, 4),), jnp.float32),
        "heads_moment": draw_heads_moment(jax.random.fold_in(seeds[19], 71), 0),
        "output_moment": draw_output_moment(jax.random.fold_in(seeds[19], 71), 0),
        "up_moment": draw_up_moment(jax.random.fold_in(seeds[19], 71), 0),
        "down_moment": draw_down_moment(jax.random.fold_in(seeds[19], 71), 0),
    }


mom_rate = 0.95
schulz_coeffs = (3.4445, -4.775, 2.0315)
step_rates = (0.04, 0.3, 0.04, 0.04)
vector_rate = 0.3
norm_eps = 1e-05
neg_large = -1e+30

def to_half(value):
    return lax.optimization_barrier(value.astype(jnp.bfloat16))

def layer_norm(inputs, gain, shift):
    average = lax.optimization_barrier(jnp.mean(inputs, axis=-1, keepdims=True))
    centred = inputs - average
    variance = lax.optimization_barrier(jnp.mean(centred * centred, axis=-1, keepdims=True))
    inverse = lax.rsqrt(variance + norm_eps)
    normed = centred * inverse
    return (normed, inverse, normed * gain + shift)

def norm_back(delta, normed, inverse, gain):
    scaled = delta * gain
    first = lax.optimization_barrier(jnp.mean(scaled, axis=-1, keepdims=True))
    second = lax.optimization_barrier(jnp.mean(scaled * normed, axis=-1, keepdims=True))
    return inverse * (scaled - first - normed * second)

def gelu_value(pre):
    return 0.5 * pre * (1.0 + lax.erf(pre / math.sqrt(2.0)))

def gelu_slope(pre):
    return 0.5 * (1.0 + lax.erf(pre / math.sqrt(2.0))) + pre * jnp.exp(-0.5 * pre * pre) / math.sqrt(2.0 * math.pi)

def slot_places(group_order, first_row, count, group):
    positions = first_row + jnp.arange(count, dtype=jnp.int32)
    slots = positions // group
    table = jnp.arange(group_order.shape[0], dtype=jnp.int32)
    picked = lax.optimization_barrier(jnp.sum(jnp.where(slots[:, None] == table[None, :], group_order[None, :], 0), axis=1))
    return (picked * group + positions % group).astype(jnp.int32)

def rotary_tables(places):
    halfway = ROT // 2
    rates = 10000.0 ** (-2.0 * jnp.arange(halfway, dtype=jnp.float32) / ROT)
    angle = places.astype(jnp.float32)[:, None] * rates[None, :]
    return (jnp.cos(angle), jnp.sin(angle))

def rotate(heads, cosine, sine, sign):
    halfway = ROT // 2
    first = heads[..., :halfway]
    second = heads[..., halfway:ROT]
    cosine = cosine[:, None, :]
    sine = sign * sine[:, None, :]
    return jnp.concatenate([first * cosine - second * sine, second * cosine + first * sine, heads[..., ROT:]], axis=-1)

def orthogonalize(nest, blocks):
    rows, cols = nest.shape
    norm = jnp.sqrt(jnp.sum(nest * nest))
    ortho = (nest / (norm + 1e-07)).astype(jnp.bfloat16)
    for turn in range(NS_ITERS):
        parts = ortho.astype(jnp.float32).reshape(rows, blocks, cols // blocks)
        partial_value = jnp.einsum('rbw,sbw->brs', parts, parts)
        gram = lax.optimization_barrier(jnp.sum(to_half(partial_value).astype(jnp.float32), axis=0)).astype(jnp.bfloat16)
        square = jnp.dot(gram, gram, preferred_element_type=jnp.float32)
        mix = (schulz_coeffs[1] * gram.astype(jnp.float32) + schulz_coeffs[2] * square).astype(jnp.bfloat16)
        ortho = (schulz_coeffs[0] * ortho.astype(jnp.float32) + jnp.dot(mix, ortho, preferred_element_type=jnp.float32)).astype(jnp.bfloat16)
    return ortho

def reference(residual_in, cotangent, group_order, gain_first, shift_first, gain_second, shift_second, heads_weight, heads_bias, output_weight, output_bias, up_weight, up_bias, down_weight, down_bias, heads_moment, output_moment, up_moment, down_moment):
    single = jnp.float32
    half = jnp.bfloat16
    heads_copy = heads_weight.astype(half)
    output_copy = output_weight.astype(half)
    up_copy = up_weight.astype(half)
    down_copy = down_weight.astype(half)
    gain_one = to_half(gain_first).astype(single)
    shift_one = to_half(shift_first).astype(single)
    gain_two = to_half(gain_second).astype(single)
    shift_two = to_half(shift_second).astype(single)
    heads_shift = to_half(heads_bias).astype(single)
    output_shift = to_half(output_bias).astype(single)
    up_shift = to_half(up_bias).astype(single)
    down_shift = to_half(down_bias).astype(single)
    places = slot_places(group_order, 0, LEN, GROUP)
    cosine, sine = rotary_tables(places)
    scale = 1.0 / math.sqrt(HD)
    block = math.gcd(LEN, 512)
    count = LEN // block
    place_blocks = places.reshape(count, block)

    def one_sequence(carry, data):
        inputs_half, grad_out = data
        inputs = inputs_half.astype(single)
        first_hat, first_inv, first_norm = layer_norm(inputs, gain_one, shift_one)
        second_hat, second_inv, second_norm = layer_norm(inputs, gain_two, shift_two)
        first_in = first_norm.astype(half)
        second_in = second_norm.astype(half)
        projected = jnp.dot(first_in, heads_copy, preferred_element_type=single) + heads_shift
        split = projected.reshape(LEN, 3, HEADS, HD)
        query = rotate(split[:, 0], cosine, sine, 1.0).astype(half)
        keys = rotate(split[:, 1], cosine, sine, 1.0).astype(half)
        values = split[:, 2].astype(half)
        keys_wide = keys.astype(single)
        values_wide = values.astype(single)
        query_blocks = query.reshape(count, block, HEADS, HD)

        def forward_block(args):
            query_block, place_block = args
            score = jnp.einsum('qhd,khd->hqk', query_block.astype(single), keys_wide) * scale
            allowed = places[None, None, :] <= place_block[None, :, None]
            peak = lax.optimization_barrier(jnp.max(jnp.where(allowed, score, neg_large), axis=-1))
            total = lax.optimization_barrier(jnp.sum(jnp.where(allowed, jnp.exp(score - peak[..., None]), 0.0), axis=-1))
            lse_block = peak + jnp.log(total)
            prob = to_half(jnp.where(allowed, jnp.exp(score - lse_block[..., None]), 0.0)).astype(single)
            return (jnp.einsum('hqk,khd->qhd', prob, values_wide), lse_block)
        mixed, lse = lax.map(forward_block, (query_blocks, place_blocks))
        attn = mixed.reshape(LEN, D).astype(half)
        output_part = jnp.dot(attn, output_copy, preferred_element_type=single) + output_shift
        up_pre = jnp.dot(second_in, up_copy, preferred_element_type=single) + up_shift
        active = gelu_value(up_pre).astype(half)
        mlp_part = jnp.dot(active, down_copy.T, preferred_element_type=single) + down_shift
        block_out = (inputs + output_part + mlp_part).astype(half)
        grad_half = grad_out.astype(half)
        down_local = jnp.dot(grad_half.T, active, preferred_element_type=single)
        up_delta = jnp.dot(grad_half, down_copy, preferred_element_type=single) * gelu_slope(up_pre)
        up_half = up_delta.astype(half)
        up_local = jnp.dot(second_in.T, up_half, preferred_element_type=single)
        second_delta = jnp.dot(up_half, up_copy.T, preferred_element_type=single)
        output_local = jnp.dot(attn.T, grad_half, preferred_element_type=single)
        attn_delta = jnp.dot(grad_half, output_copy.T, preferred_element_type=single).astype(half)
        attn_heads = attn_delta.reshape(LEN, HEADS, HD)
        delta = lax.optimization_barrier(jnp.sum(attn_heads.astype(single) * attn.reshape(LEN, HEADS, HD).astype(single), axis=-1))
        delta_blocks = jnp.transpose(delta.reshape(count, block, HEADS), (0, 2, 1))
        dout_blocks = attn_heads.reshape(count, block, HEADS, HD)

        def back_block(sums, args):
            key_sum, value_sum = sums
            query_block, place_block, lse_block, delta_block, dout_block = args
            score = jnp.einsum('qhd,khd->hqk', query_block.astype(single), keys_wide) * scale
            allowed = places[None, None, :] <= place_block[None, :, None]
            prob = jnp.where(allowed, jnp.exp(score - lse_block[..., None]), 0.0)
            prob_half = to_half(prob).astype(single)
            prob_grad = jnp.einsum('qhd,khd->hqk', dout_block.astype(single), values_wide)
            score_delta = to_half(prob * (prob_grad - delta_block[..., None])).astype(single)
            query_grad = jnp.einsum('hqk,khd->qhd', score_delta, keys_wide) * scale
            key_sum = key_sum + jnp.einsum('hqk,qhd->khd', score_delta, query_block.astype(single)) * scale
            value_sum = value_sum + jnp.einsum('hqk,qhd->khd', prob_half, dout_block.astype(single))
            return ((key_sum, value_sum), query_grad)
        start_sums = (jnp.zeros((LEN, HEADS, HD), single), jnp.zeros((LEN, HEADS, HD), single))
        (key_sum, value_sum), query_grads = lax.scan(back_block, start_sums, (query_blocks, place_blocks, lse, delta_blocks, dout_blocks))
        query_delta = rotate(query_grads.reshape(LEN, HEADS, HD), cosine, sine, -1.0)
        key_delta = rotate(key_sum, cosine, sine, -1.0)
        heads_delta = jnp.concatenate([query_delta.reshape(LEN, D), key_delta.reshape(LEN, D), value_sum.reshape(LEN, D)], axis=1)
        heads_half = heads_delta.astype(half)
        heads_local = jnp.dot(first_in.T, heads_half, preferred_element_type=single)
        first_delta = jnp.dot(heads_half, heads_copy.T, preferred_element_type=single)
        input_grad = grad_out + norm_back(first_delta, first_hat, first_inv, gain_one) + norm_back(second_delta, second_hat, second_inv, gain_two)
        terms = (heads_local, output_local, up_local, down_local, lax.optimization_barrier(jnp.sum(first_delta * first_hat, axis=0)), lax.optimization_barrier(jnp.sum(first_delta, axis=0)), lax.optimization_barrier(jnp.sum(second_delta * second_hat, axis=0)), lax.optimization_barrier(jnp.sum(second_delta, axis=0)), lax.optimization_barrier(jnp.sum(heads_delta, axis=0)), lax.optimization_barrier(jnp.sum(grad_out, axis=0)), lax.optimization_barrier(jnp.sum(up_delta, axis=0)))
        new_carry = tuple((old + new for old, new in zip(carry, terms)))
        return (new_carry, (block_out, input_grad))
    start = (jnp.zeros((D, 3 * D), single), jnp.zeros((D, D), single), jnp.zeros((D, FF), single), jnp.zeros((D, FF), single), jnp.zeros((D,), single), jnp.zeros((D,), single), jnp.zeros((D,), single), jnp.zeros((D,), single), jnp.zeros((3 * D,), single), jnp.zeros((D,), single), jnp.zeros((FF,), single))
    sums, (block_out, input_grad) = lax.scan(one_sequence, start, (residual_in, cotangent))
    matrix_grads = sums[0:4]
    weights = (heads_weight, output_weight, up_weight, down_weight)
    moments = (heads_moment, output_moment, up_moment, down_moment)
    new_weights = []
    new_moments = []
    for which in range(4):
        moment = mom_rate * moments[which] + matrix_grads[which]
        nest = matrix_grads[which] + mom_rate * moment
        ortho = orthogonalize(nest, N_CTX)
        new_weights.append(weights[which] - step_rates[which] * math.sqrt(nest.shape[1]) * ortho.astype(single))
        new_moments.append(moment)
    vector_values = (gain_first, shift_first, gain_second, shift_second, heads_bias, output_bias, up_bias, down_bias)
    vector_grads = (sums[4], sums[5], sums[6], sums[7], sums[8], sums[9], sums[10], sums[9])
    new_vectors = []
    for which in range(8):
        grad = vector_grads[which]
        new_vectors.append(vector_values[which] - vector_rate * grad * lax.rsqrt(jnp.mean(grad * grad) + norm_eps))
    return (block_out, input_grad, vector_grads[0], vector_grads[1], vector_grads[2], vector_grads[3], matrix_grads[0], vector_grads[4], matrix_grads[1], vector_grads[5], matrix_grads[2], vector_grads[6], matrix_grads[3], vector_grads[7], new_vectors[0], new_vectors[1], new_vectors[2], new_vectors[3], new_weights[0], new_vectors[4], new_weights[1], new_vectors[5], new_weights[2], new_vectors[6], new_weights[3], new_vectors[7], new_moments[0], new_moments[1], new_moments[2], new_moments[3])
```

```python
import math

import jax
import jax.numpy as jnp
from jax import lax
from jax.experimental import pallas as pl
from jax.experimental.pallas import tpu as pltpu
from jax.sharding import PartitionSpec as P

HEADS = 12
HD = 64
ROT = 16
NS_ITERS = 5


mom_rate = 0.95
schulz_coeffs = (3.4445, -4.775, 2.0315)
step_rates = (0.04, 0.3, 0.04, 0.04)
vector_rate = 0.3
norm_eps = 1e-05
neg_large = -1e30


def broadcast(x, axis, root):
    mine = lax.axis_index(axis) == root
    return lax.psum(jnp.where(mine, x, jnp.zeros_like(x)), axis)


def layer_norm(inputs, gain, shift):
    average = jnp.mean(inputs, axis=-1, keepdims=True)
    centred = inputs - average
    variance = jnp.mean(centred * centred, axis=-1, keepdims=True)
    inverse = lax.rsqrt(variance + norm_eps)
    normed = centred * inverse
    return (normed, inverse, normed * gain + shift)


def norm_back(delta, normed, inverse, gain):
    scaled = delta * gain
    first = jnp.mean(scaled, axis=-1, keepdims=True)
    second = jnp.mean(scaled * normed, axis=-1, keepdims=True)
    return inverse * (scaled - first - normed * second)


def gelu_value(pre):
    return 0.5 * pre * (1.0 + lax.erf(pre / math.sqrt(2.0)))


def gelu_slope(pre):
    return 0.5 * (1.0 + lax.erf(pre / math.sqrt(2.0))) + pre * jnp.exp(
        -0.5 * pre * pre
    ) / math.sqrt(2.0 * math.pi)


def slot_places(group_order, first_row, count, group):
    positions = first_row + jnp.arange(count, dtype=jnp.int32)
    slots = positions // group
    table = jnp.arange(group_order.shape[0], dtype=jnp.int32)
    picked = jnp.sum(jnp.where(slots[:, None] == table[None, :], group_order[None, :], 0), axis=1)
    return picked * group + positions % group


def rotary_tables(places):
    halfway = ROT // 2
    rates = 10000.0 ** (-2.0 * jnp.arange(halfway, dtype=jnp.float32) / ROT)
    angle = places.astype(jnp.float32)[:, None] * rates[None, :]
    return (jnp.cos(angle), jnp.sin(angle))


def rotate(heads, cosine, sine, sign):
    halfway = ROT // 2
    first = heads[..., :halfway]
    second = heads[..., halfway:ROT]
    cosine = cosine[:, None, :]
    sine = sign * sine[:, None, :]
    return jnp.concatenate(
        [first * cosine - second * sine, second * cosine + first * sine, heads[..., ROT:]], axis=-1
    )


def local_general(
    residual_in,
    cotangent,
    group_order,
    gain_first,
    shift_first,
    gain_second,
    shift_second,
    heads_weight,
    heads_bias,
    output_weight,
    output_bias,
    up_weight,
    up_bias,
    down_weight,
    down_bias,
    heads_moment,
    output_moment,
    up_moment,
    down_moment,
):
    single = jnp.float32
    half = jnp.bfloat16
    ctx_count = lax.axis_size("ctx")
    shard_count = lax.axis_size("fsdp")
    ctx_place = lax.axis_index("ctx")
    shard_place = lax.axis_index("fsdp")
    seqs, rows, width = residual_in.shape
    length = rows * ctx_count
    group = rows // 2
    scale = 1.0 / math.sqrt(HD)
    query_places = slot_places(group_order, ctx_place * rows, rows, group)
    key_places = slot_places(group_order, 0, length, group)
    copies = (
        lax.all_gather(heads_weight.astype(half), "fsdp", axis=0, tiled=True),
        lax.all_gather(output_weight.astype(half), "fsdp", axis=0, tiled=True),
        lax.all_gather(up_weight.astype(half), "fsdp", axis=0, tiled=True),
        lax.all_gather(down_weight.astype(half), "fsdp", axis=0, tiled=True),
        lax.all_gather(gain_first.astype(half), "fsdp", axis=0, tiled=True),
        lax.all_gather(shift_first.astype(half), "fsdp", axis=0, tiled=True),
        lax.all_gather(gain_second.astype(half), "fsdp", axis=0, tiled=True),
        lax.all_gather(shift_second.astype(half), "fsdp", axis=0, tiled=True),
        lax.all_gather(heads_bias.astype(half), "fsdp", axis=0, tiled=True),
        lax.all_gather(output_bias.astype(half), "fsdp", axis=0, tiled=True),
        lax.all_gather(up_bias.astype(half), "fsdp", axis=0, tiled=True),
        lax.all_gather(down_bias.astype(half), "fsdp", axis=0, tiled=True),
    )
    heads_copy, output_copy, up_copy, down_copy = (copies[0], copies[1], copies[2], copies[3])
    gain_one, shift_one, gain_two, shift_two, heads_shift, output_shift, up_shift, down_shift = [
        piece.astype(single) for piece in copies[4:]
    ]
    inputs = residual_in.astype(single)
    first_hat, first_inv, first_norm = layer_norm(inputs, gain_one, shift_one)
    second_hat, second_inv, second_norm = layer_norm(inputs, gain_two, shift_two)
    first_in = first_norm.astype(half)
    second_in = second_norm.astype(half)
    projected = (
        jnp.einsum("std,de->ste", first_in, heads_copy, preferred_element_type=single) + heads_shift
    )
    cosine, sine = rotary_tables(query_places)
    split = projected.reshape(seqs, rows, 3, HEADS, HD)
    query = rotate(split[:, :, 0], cosine, sine, 1.0).astype(half)
    keys = rotate(split[:, :, 1], cosine, sine, 1.0).astype(half).reshape(seqs, rows, width)
    values = split[:, :, 2].astype(half).reshape(seqs, rows, width)
    peak = jnp.full((seqs, HEADS, rows), neg_large, single)
    key_piece = lax.all_gather(keys, "ctx", axis=1, tiled=True)
    value_piece = lax.all_gather(values, "ctx", axis=1, tiled=True)
    count = key_piece.shape[1]
    places = slot_places(group_order, jnp.int32(0), count, group)
    key_heads = key_piece.reshape(seqs, count, HEADS, HD)
    value_heads = value_piece.reshape(seqs, count, HEADS, HD)
    score = jnp.einsum("sqhd,skhd->shqk", query, key_heads, preferred_element_type=single) * scale
    allowed = (places[None, :] <= query_places[:, None])[None, None]
    new_peak = jnp.maximum(peak, jnp.max(jnp.where(allowed, score, neg_large), axis=-1))
    weights = jnp.where(allowed, jnp.exp(score - new_peak[..., None]), 0.0)
    total = jnp.sum(weights, axis=-1)
    mixed = jnp.einsum(
        "shqk,skhd->shqd", weights.astype(half), value_heads, preferred_element_type=single
    )
    state = (new_peak, total, mixed)
    peak, total, mixed = state
    lse = peak + jnp.log(total)
    attn = (
        jnp.transpose(mixed / total[..., None], (0, 2, 1, 3))
        .reshape(seqs, rows, width)
        .astype(half)
    )
    output_part = (
        jnp.einsum("std,de->ste", attn, output_copy, preferred_element_type=single) + output_shift
    )
    up_pre = jnp.einsum("std,df->stf", second_in, up_copy, preferred_element_type=single) + up_shift
    active = gelu_value(up_pre).astype(half)
    mlp_part = (
        jnp.einsum("stf,df->std", active, down_copy, preferred_element_type=single) + down_shift
    )
    block_out = (inputs + output_part + mlp_part).astype(half)
    grad_half = cotangent.astype(half)
    down_local = jnp.einsum("std,stf->df", grad_half, active, preferred_element_type=single)
    up_delta = jnp.einsum(
        "std,df->stf", grad_half, down_copy, preferred_element_type=single
    ) * gelu_slope(up_pre)
    up_half = up_delta.astype(half)
    up_local = jnp.einsum("std,stf->df", second_in, up_half, preferred_element_type=single)
    second_delta = jnp.einsum("stf,df->std", up_half, up_copy, preferred_element_type=single)
    output_local = jnp.einsum("std,ste->de", attn, grad_half, preferred_element_type=single)
    attn_delta = jnp.einsum(
        "ste,de->std", grad_half, output_copy, preferred_element_type=single
    ).astype(half)
    attn_heads = attn_delta.reshape(seqs, rows, HEADS, HD)
    delta = jnp.transpose(
        jnp.sum(
            attn_heads.astype(single) * attn.reshape(seqs, rows, HEADS, HD).astype(single), axis=-1
        ),
        (0, 2, 1),
    )
    every_key, every_value = (
        lax.all_gather(keys, "ctx", axis=1, tiled=True),
        lax.all_gather(values, "ctx", axis=1, tiled=True),
    )
    block = math.gcd(length, 512)
    count = length // block
    key_blocks = jnp.moveaxis(every_key.reshape(seqs, count, block, HEADS, HD), 1, 0)
    value_blocks = jnp.moveaxis(every_value.reshape(seqs, count, block, HEADS, HD), 1, 0)
    place_blocks = key_places.reshape(count, block)

    def back_block(query_grad, data):
        key_block, value_block, place_block = data
        score = (
            jnp.einsum("sqhd,skhd->shqk", query, key_block, preferred_element_type=single) * scale
        )
        allowed = (place_block[None, :] <= query_places[:, None])[None, None]
        prob = jnp.where(allowed, jnp.exp(score - lse[..., None]), 0.0)
        prob_half = prob.astype(half)
        prob_grad = jnp.einsum(
            "sqhd,skhd->shqk", attn_heads, value_block, preferred_element_type=single
        )
        score_delta = (prob * (prob_grad - delta[..., None])).astype(half)
        query_grad = (
            query_grad
            + jnp.einsum("shqk,skhd->sqhd", score_delta, key_block, preferred_element_type=single)
            * scale
        )
        key_grad = (
            jnp.einsum("shqk,sqhd->skhd", score_delta, query, preferred_element_type=single) * scale
        )
        value_grad = jnp.einsum(
            "shqk,sqhd->skhd", prob_half, attn_heads, preferred_element_type=single
        )
        joined = jnp.concatenate(
            [key_grad.reshape(seqs, block, width), value_grad.reshape(seqs, block, width)], axis=-1
        )
        return (query_grad, joined)

    query_grad, stacked = lax.scan(
        back_block,
        jnp.zeros((seqs, rows, HEADS, HD), single),
        (key_blocks, value_blocks, place_blocks),
    )
    key_grads = jnp.moveaxis(stacked, 0, 1).reshape(seqs, length, 2 * width)
    home = lax.psum_scatter(key_grads, "ctx", scatter_dimension=1, tiled=True)
    key_delta = rotate(home[..., :width].reshape(seqs, rows, HEADS, HD), cosine, sine, -1.0)
    query_delta = rotate(query_grad, cosine, sine, -1.0)
    heads_delta = jnp.concatenate(
        [
            query_delta.reshape(seqs, rows, width),
            key_delta.reshape(seqs, rows, width),
            home[..., width:],
        ],
        axis=-1,
    )
    heads_half = heads_delta.astype(half)
    heads_local = jnp.einsum("std,ste->de", first_in, heads_half, preferred_element_type=single)
    first_delta = jnp.einsum("ste,de->std", heads_half, heads_copy, preferred_element_type=single)
    input_grad = (
        cotangent
        + norm_back(first_delta, first_hat, first_inv, gain_one)
        + norm_back(second_delta, second_hat, second_inv, gain_two)
    )
    columns = (
        lax.psum_scatter(heads_local, "ctx", scatter_dimension=1, tiled=True),
        lax.psum_scatter(output_local, "ctx", scatter_dimension=1, tiled=True),
        lax.psum_scatter(up_local, "ctx", scatter_dimension=1, tiled=True),
        lax.psum_scatter(down_local, "ctx", scatter_dimension=1, tiled=True),
    )
    parts = (
        lax.psum_scatter(columns[0], "fsdp", scatter_dimension=0, tiled=True),
        lax.psum_scatter(columns[1], "fsdp", scatter_dimension=0, tiled=True),
        lax.psum_scatter(columns[2], "fsdp", scatter_dimension=0, tiled=True),
        lax.psum_scatter(columns[3], "fsdp", scatter_dimension=0, tiled=True),
    )
    full_grads = (
        lax.all_gather(parts[0], "ctx", axis=1, tiled=True),
        lax.all_gather(parts[1], "ctx", axis=1, tiled=True),
        lax.all_gather(parts[2], "ctx", axis=1, tiled=True),
        lax.all_gather(parts[3], "ctx", axis=1, tiled=True),
    )
    weights_all = (heads_weight, output_weight, up_weight, down_weight)
    moments_all = (heads_moment, output_moment, up_moment, down_moment)
    new_moments = []
    nest_blocks = []
    for which in range(4):
        moment = mom_rate * moments_all[which] + full_grads[which]
        nest = full_grads[which] + mom_rate * moment
        cols = nest.shape[1] // ctx_count
        new_moments.append(moment)
        nest_blocks.append(lax.dynamic_slice_in_dim(nest, ctx_place * cols, cols, 1))
    sums = lax.psum(
        (
            jnp.sum(first_delta * first_hat, axis=(0, 1)),
            jnp.sum(first_delta, axis=(0, 1)),
            jnp.sum(second_delta * second_hat, axis=(0, 1)),
            jnp.sum(second_delta, axis=(0, 1)),
            jnp.sum(heads_delta, axis=(0, 1)),
            jnp.sum(cotangent, axis=(0, 1)),
            jnp.sum(up_delta, axis=(0, 1)),
            jnp.sum(nest_blocks[0] * nest_blocks[0]),
            jnp.sum(nest_blocks[1] * nest_blocks[1]),
            jnp.sum(nest_blocks[2] * nest_blocks[2]),
            jnp.sum(nest_blocks[3] * nest_blocks[3]),
        ),
        ("ctx", "fsdp"),
    )
    gathered = (
        lax.all_gather(nest_blocks[0], "fsdp", axis=0, tiled=True),
        lax.all_gather(nest_blocks[1], "fsdp", axis=0, tiled=True),
        lax.all_gather(nest_blocks[2], "fsdp", axis=0, tiled=True),
        lax.all_gather(nest_blocks[3], "fsdp", axis=0, tiled=True),
    )
    widths = [piece.shape[1] for piece in gathered]
    widest = max(widths)
    owners = [which * shard_count // 4 for which in range(4)]
    selected = jnp.zeros((width, widest), single)
    square_sum = jnp.zeros((), single)
    for which in range(4):
        chosen = (shard_place == owners[which]).astype(single)
        selected = selected + chosen * jnp.pad(
            gathered[which], ((0, 0), (0, widest - widths[which]))
        )
        square_sum = square_sum + chosen * sums[7 + which]
    ortho = (selected / (jnp.sqrt(square_sum) + 1e-07)).astype(half)
    for turn in range(NS_ITERS):
        partial_value = jnp.einsum("rw,sw->rs", ortho, ortho, preferred_element_type=single)
        gram = lax.psum(partial_value.astype(jnp.bfloat16), "ctx").astype(jnp.float32).astype(half)
        mix = (
            schulz_coeffs[1] * gram.astype(single)
            + schulz_coeffs[2] * jnp.dot(gram, gram, preferred_element_type=single)
        ).astype(half)
        ortho = (
            schulz_coeffs[0] * ortho.astype(single)
            + jnp.dot(mix, ortho, preferred_element_type=single)
        ).astype(half)
    shard_rows = width // shard_count
    updated = []
    for which in range(4):
        received = broadcast(ortho, "fsdp", owners[which])
        piece = lax.dynamic_slice(
            received, (shard_place * shard_rows, 0), (shard_rows, widths[which])
        )
        total_cols = weights_all[which].shape[1]
        current = lax.dynamic_slice_in_dim(
            weights_all[which], ctx_place * widths[which], widths[which], 1
        )
        updated.append(current - step_rates[which] * math.sqrt(total_cols) * piece.astype(single))
    new_weights = (
        lax.all_gather(updated[0], "ctx", axis=1, tiled=True),
        lax.all_gather(updated[1], "ctx", axis=1, tiled=True),
        lax.all_gather(updated[2], "ctx", axis=1, tiled=True),
        lax.all_gather(updated[3], "ctx", axis=1, tiled=True),
    )
    vector_values = (
        gain_first,
        shift_first,
        gain_second,
        shift_second,
        heads_bias,
        output_bias,
        up_bias,
        down_bias,
    )
    vector_grads = (sums[0], sums[1], sums[2], sums[3], sums[4], sums[5], sums[6], sums[5])
    grad_shards = []
    new_shards = []
    for which in range(8):
        size_here = vector_values[which].shape[0]
        whole_grad = vector_grads[which]
        shard = lax.dynamic_slice_in_dim(whole_grad, shard_place * size_here, size_here)
        grad_shards.append(shard)
        new_shards.append(
            vector_values[which]
            - vector_rate * shard * lax.rsqrt(jnp.mean(whole_grad * whole_grad) + norm_eps)
        )
    return (
        block_out,
        input_grad,
        grad_shards[0],
        grad_shards[1],
        grad_shards[2],
        grad_shards[3],
        full_grads[0],
        grad_shards[4],
        full_grads[1],
        grad_shards[5],
        full_grads[2],
        grad_shards[6],
        full_grads[3],
        grad_shards[7],
        new_shards[0],
        new_shards[1],
        new_shards[2],
        new_shards[3],
        new_weights[0],
        new_shards[4],
        new_weights[1],
        new_shards[5],
        new_weights[2],
        new_shards[6],
        new_weights[3],
        new_shards[7],
        new_moments[0],
        new_moments[1],
        new_moments[2],
        new_moments[3],
    )


Y_PLACES = 2
Z_PLACES = 4
CTX = Y_PLACES * Z_PLACES
SHARDS = 4


def swap(x, axis, offset):
    count = lax.axis_size(axis)
    return lax.ppermute(x, axis, [(i, i ^ offset) for i in range(count)])


def pick(x, index, dim=0):
    return lax.dynamic_index_in_dim(x, index, dim, keepdims=False)


def in_order(pieces, place):
    stacked = jnp.stack(pieces)
    return jnp.stack([pick(stacked, place ^ i) for i in range(len(pieces))])


def spread(x, place):
    return [pick(x, place)] + [swap(pick(x, place ^ k), "fsdp", k) for k in range(1, SHARDS)]


def gather_ctx(x):
    along = [x] + [swap(x, "ctx", 2 * k) for k in range(1, Z_PLACES)]
    pieces = []
    for piece in along:
        pieces += [piece, swap(piece, "ctx", 1)]
    return pieces


def scatter_ctx(x, ctx_place, dim):
    single, half = jnp.float32, jnp.bfloat16
    y, z = ctx_place % Y_PLACES, ctx_place // Y_PLACES
    x = x.reshape(x.shape[:dim] + (Z_PLACES, Y_PLACES) + x.shape[dim + 1 :])
    sent = swap(pick(x, 1 - y, dim + 1).astype(half), "ctx", 1)
    kept = pick(x, y, dim + 1) + sent.astype(single)
    total = pick(kept, z, dim)
    for k in range(1, Z_PLACES):
        total = total + swap(pick(kept, z ^ k, dim).astype(half), "ctx", 2 * k).astype(single)
    return total


def attention_kernel(recv_ref, place_row_ref, place_col_ref, place_half_ref, out_ref):
    single, half = jnp.float32, jnp.bfloat16
    scale = 1.0 / math.sqrt(HD)
    rows = 128
    length = CTX * rows
    place_row = place_row_ref[...]

    def run(query, keys, values, outer, places, step):
        key_sum = jnp.zeros((length, HD), single)
        value_sum = jnp.zeros((length, HD), single)
        mixed_all, query_all = [], []
        for at in range(0, query.shape[0], step):
            one = query[at : at + step]
            back = outer[at : at + step]
            score = (
                lax.dot_general(one, keys, (((1,), (1,)), ((), ())), preferred_element_type=single)
                * scale
            )
            allowed = place_row <= places[at : at + step]
            score = jnp.where(allowed, score, neg_large)
            peak = jnp.max(score, axis=-1, keepdims=True)
            weights = jnp.where(allowed, jnp.exp(score - peak), 0.0)
            total = jnp.sum(weights, axis=-1, keepdims=True)
            prob = weights * (1.0 / total)
            prob_half = prob.astype(half)
            mixed = jnp.dot(prob_half, values, preferred_element_type=single).astype(half)
            delta = jnp.sum(
                back.astype(single) * mixed.astype(single), axis=-1, keepdims=True
            )
            prob_grad = lax.dot_general(
                back, values, (((1,), (1,)), ((), ())), preferred_element_type=single
            )
            score_delta = (prob * (prob_grad - delta)).astype(half)
            query_grad = jnp.dot(score_delta, keys, preferred_element_type=single) * scale
            key_sum += lax.dot_general(
                score_delta, one, (((0,), (0,)), ((), ())), preferred_element_type=single
            )
            value_sum += lax.dot_general(
                prob_half, back, (((0,), (0,)), ((), ())), preferred_element_type=single
            )
            mixed_all.append(mixed)
            query_all.append(query_grad.astype(half))
        return (
            jnp.concatenate(mixed_all, axis=0),
            jnp.concatenate(query_all, axis=0),
            (key_sum * scale).astype(half),
            value_sum.astype(half),
        )

    first = recv_ref[:, 0:128, :].reshape(length, 128)
    second = recv_ref[:, 128:256, :].reshape(length, 128)
    mixed, query_grad, key_grad, value_grad = run(
        first[:, :HD], first[:, HD:], second[:, :HD], second[:, HD:], place_col_ref[...], 256
    )
    out_ref[:, 0:128, :] = jnp.concatenate([mixed, query_grad], axis=1).reshape(CTX, rows, 128)
    out_ref[:, 128:256, :] = jnp.concatenate([key_grad, value_grad], axis=1).reshape(
        CTX, rows, 128
    )
    third = recv_ref[:, 256:384, :].reshape(length, 128)
    fourth = recv_ref[:, 384:448, :].reshape(length // 2, 128)
    mixed, query_grad, key_grad, value_grad = run(
        fourth[:, :HD], third[:, :HD], third[:, HD:], fourth[:, HD:], place_half_ref[...], 256
    )
    out_ref[:, 256:384, :] = jnp.concatenate([key_grad, value_grad], axis=1).reshape(
        CTX, rows, 128
    )
    out_ref[:, 384:448, :] = jnp.concatenate([mixed, query_grad], axis=1).reshape(
        CTX, rows // 2, 128
    )


def attention(recv, places, y):
    length = places.shape[0]
    halves = pick(places.reshape(CTX, Y_PLACES, length // CTX // Y_PLACES), y, 1).reshape(-1)
    return pl.pallas_call(
        attention_kernel,
        out_shape=jax.ShapeDtypeStruct(recv.shape, recv.dtype),
        compiler_params=pltpu.CompilerParams(vmem_limit_bytes=48 * 1024 * 1024),
        cost_estimate=pl.CostEstimate(
            flops=7 * 2 * 1536 * 1024 * 128, bytes_accessed=2 * recv.size * 2, transcendentals=1536 * 1024
        ),
        name="attention",
    )(recv, places[None, :], places[:, None], halves[:, None])


def moment_kernel(where_ref, grads_ref, *refs):
    at = 0
    for which in range(4):
        moment_ref, grad_out, moment_out = refs[which], refs[4 + which], refs[8 + which]
        cols = moment_ref.shape[1]
        grad = grads_ref[0, :, at : at + cols].astype(jnp.float32)
        grad_out[...] = grad
        moment_out[...] = mom_rate * moment_ref[...] + grad
        at += cols


def write_moments(grads, moments, ctx_place):
    rows = moments[0].shape[0] // CTX
    blocks = [pl.BlockSpec((rows, m.shape[1]), lambda i, where: (i, 0)) for m in moments]
    shapes = [jax.ShapeDtypeStruct(m.shape, m.dtype) for m in moments]
    out = pl.pallas_call(
        moment_kernel,
        grid_spec=pltpu.PrefetchScalarGridSpec(
            num_scalar_prefetch=1,
            grid=(CTX,),
            in_specs=[
                pl.BlockSpec((1,) + grads.shape[1:], lambda i, where: (i ^ where[0], 0, 0))
            ]
            + blocks,
            out_specs=blocks + blocks,
        ),
        out_shape=shapes + shapes,
        compiler_params=pltpu.CompilerParams(vmem_limit_bytes=32 * 1024 * 1024),
        name="moments",
    )(ctx_place.reshape(1), grads, *moments)
    return out[:4], out[4:]


def weight_kernel(where_ref, *refs):
    for which in range(4):
        ortho_ref, weight_ref, out_ref = refs[which], refs[4 + which], refs[8 + which]
        cols = weight_ref.shape[1]
        rate = step_rates[which] * math.sqrt(cols)
        out_ref[...] = weight_ref[...] - rate * ortho_ref[0, 0, :, :cols].astype(jnp.float32)


def write_weights(ortho, weights, ctx_place, shard_place):
    rows = weights[0].shape[0] // CTX
    blocks = [pl.BlockSpec((rows, w.shape[1]), lambda i, where: (i, 0)) for w in weights]

    def source(which):
        return pl.BlockSpec(
            (1, 1) + ortho.shape[2:], lambda i, where: (where[1] ^ which, i ^ where[0], 0, 0)
        )

    return pl.pallas_call(
        weight_kernel,
        grid_spec=pltpu.PrefetchScalarGridSpec(
            num_scalar_prefetch=1,
            grid=(CTX,),
            in_specs=[source(which) for which in range(4)] + blocks,
            out_specs=blocks,
        ),
        out_shape=[jax.ShapeDtypeStruct(w.shape, w.dtype) for w in weights],
        compiler_params=pltpu.CompilerParams(vmem_limit_bytes=32 * 1024 * 1024),
        name="weights",
    )(jnp.stack([ctx_place, shard_place]), ortho, ortho, ortho, ortho, *weights)


def local_fast(
    residual_in,
    cotangent,
    group_order,
    gain_first,
    shift_first,
    gain_second,
    shift_second,
    heads_weight,
    heads_bias,
    output_weight,
    output_bias,
    up_weight,
    up_bias,
    down_weight,
    down_bias,
    heads_moment,
    output_moment,
    up_moment,
    down_moment,
):
    single = jnp.float32
    half = jnp.bfloat16
    ctx_place = lax.axis_index("ctx")
    shard_place = lax.axis_index("fsdp")
    y, z = ctx_place % Y_PLACES, ctx_place // Y_PLACES
    seqs, rows, width = residual_in.shape
    length = rows * CTX
    group = rows // 2
    part = width // SHARDS
    hidden = up_weight.shape[1]
    hidden_part = hidden // SHARDS
    strip = part // CTX

    small = jnp.zeros((16, width), half)
    small = small.at[0].set(
        jnp.concatenate([gain_first, shift_first, gain_second, shift_second]).astype(half)
    )
    small = small.at[1, : 2 * part].set(jnp.concatenate([output_bias, down_bias]).astype(half))
    small = small.at[2, : 3 * part].set(heads_bias.astype(half))
    packed = jnp.concatenate([residual_in[0], cotangent[0].astype(half), small], axis=0)
    packs = [packed] + [swap(packed, "fsdp", k) for k in range(1, SHARDS)]
    heads_split = jnp.moveaxis(
        heads_weight.astype(half).reshape(part, 3, SHARDS, part), 2, 0
    ).reshape(SHARDS, part, 3 * part)
    heads_block = in_order(spread(heads_split, shard_place), shard_place).reshape(width, 3 * part)
    up_split = jnp.moveaxis(up_weight.astype(half).reshape(part, SHARDS, hidden_part), 1, 0)
    down_split = jnp.moveaxis(down_weight.astype(half).reshape(part, SHARDS, hidden_part), 1, 0)
    mlp_split = jnp.concatenate([up_split, down_split], axis=-1)
    mlp_block = in_order(spread(mlp_split, shard_place), shard_place).reshape(
        width, 2 * hidden_part
    )
    up_block, down_block = mlp_block[:, :hidden_part], mlp_block[:, hidden_part:]
    output_block = output_weight.astype(half)

    tokens = jnp.stack([p[:rows] for p in packs])
    grad_half = jnp.stack([p[rows : 2 * rows] for p in packs]).reshape(SHARDS * rows, width)
    vectors = in_order([p[2 * rows :] for p in packs], shard_place).astype(single)
    gain_one, shift_one, gain_two, shift_two = [
        vectors[:, 0, i * part : (i + 1) * part].reshape(width) for i in range(4)
    ]
    output_shift, down_shift = [
        vectors[:, 1, i * part : (i + 1) * part].reshape(width) for i in range(2)
    ]
    heads_shift = pick(
        vectors[:, 2, : 3 * part].reshape(3, SHARDS, part), shard_place, 1
    ).reshape(3 * part)
    up_shift = up_bias.astype(half).astype(single)

    inputs = tokens.astype(single).reshape(SHARDS * rows, width)
    average = jnp.mean(inputs, axis=-1, keepdims=True)
    centred = inputs - average
    variance = jnp.mean(centred * centred, axis=-1, keepdims=True)
    inverse = lax.rsqrt(variance + norm_eps)
    normed = centred * inverse
    first_in = (normed * gain_one + shift_one).astype(half)
    second_in = (normed * gain_two + shift_two).astype(half)

    projected = jnp.dot(first_in, heads_block, preferred_element_type=single) + heads_shift
    places = slot_places(group_order, 0, length, group)
    query_places = slot_places(group_order, ctx_place * rows, rows, group)
    cosine, sine = rotary_tables(query_places)
    rest = HD - ROT
    turn_cos = jnp.concatenate([cosine, cosine, jnp.ones((rows, rest), single)], axis=1)
    turn_sin = jnp.concatenate([sine, sine, jnp.zeros((rows, rest), single)], axis=1)
    turn_cos = jnp.tile(turn_cos, (SHARDS, 2 * part // HD))
    turn_sin = jnp.tile(turn_sin, (SHARDS, 2 * part // HD))
    lane = jnp.arange(2 * part)
    inside = lane % HD
    other = jnp.where(inside < ROT // 2, lane + ROT // 2, lane - ROT // 2)
    sign = jnp.where(inside < ROT // 2, -1.0, 1.0) * (inside < ROT)
    partner = jnp.where(lane[:, None] == other[None, :], sign[None, :], 0.0).astype(single)

    def turned(x, direction):
        moved = jnp.dot(x, partner, precision=lax.Precision.HIGHEST, preferred_element_type=single)
        return x * turn_cos + direction * (moved * turn_sin)

    turned_half = turned(projected[:, : 2 * part], 1.0).astype(half)
    attn_delta = lax.dot_general(
        grad_half, output_block, (((1,), (1,)), ((), ())), preferred_element_type=single
    ).astype(half)
    query = turned_half[:, :part].reshape(SHARDS, rows, part)
    keys = turned_half[:, part:].reshape(SHARDS, rows, part)
    values = projected[:, 2 * part :].astype(half).reshape(SHARDS, rows, part)
    outer = attn_delta.reshape(SHARDS, rows, part)

    def beside(a, b, head):
        cut = slice(head * HD, (head + 1) * HD)
        return jnp.concatenate([a[..., cut], b[..., cut]], axis=-1)

    shared_rows = beside(query, outer, 2).reshape(SHARDS, Y_PLACES, rows // 2, 2 * HD)
    shared_keys = beside(keys, values, 2)
    payload = jnp.stack(
        [
            jnp.concatenate(
                [
                    beside(query, keys, head),
                    beside(values, outer, head),
                    shared_keys,
                    shared_rows[:, head],
                ],
                axis=1,
            )
            for head in range(Y_PLACES)
        ],
        axis=1,
    ).reshape(CTX, 3 * rows + rows // 2, 2 * HD)
    sent = lax.all_to_all(payload, "ctx", 0, 0)
    done = attention(sent, places, y)
    back = lax.all_to_all(done, "ctx", 0, 0).reshape(
        Z_PLACES, Y_PLACES, 3 * rows + rows // 2, 2 * HD
    )

    up_pre = jnp.dot(second_in, up_block, preferred_element_type=single) + up_shift
    active = gelu_value(up_pre).astype(half)
    up_delta = jnp.dot(grad_half, down_block, preferred_element_type=single) * gelu_slope(up_pre)
    up_half = up_delta.astype(half)

    def over_tokens(a, b):
        return lax.dot_general(a, b, (((0,), (0,)), ((), ())), preferred_element_type=single)

    def over_columns(a, b):
        return lax.dot_general(a, b, (((1,), (1,)), ((), ())), preferred_element_type=single)

    up_local = over_tokens(second_in, up_half).reshape(SHARDS, CTX, strip, hidden_part)
    down_local = over_tokens(grad_half, active).reshape(SHARDS, CTX, strip, hidden_part)
    up_strip = scatter_ctx(up_local, ctx_place, 1)
    down_strip = scatter_ctx(down_local, ctx_place, 1)
    mlp_part = over_columns(active, down_block)
    second_part = over_columns(up_half, up_block)

    early, late = back[..., :HD], back[..., HD:]
    attn = jnp.concatenate(
        [early[:, 0, :rows], early[:, 1, :rows], early[:, :, 3 * rows :].reshape(SHARDS, rows, HD)],
        axis=-1,
    ).reshape(SHARDS * rows, part)
    query_grad = jnp.concatenate(
        [late[:, 0, :rows], late[:, 1, :rows], late[:, :, 3 * rows :].reshape(SHARDS, rows, HD)],
        axis=-1,
    ).astype(single)
    wide = back[:, :, rows : 3 * rows].astype(single)
    shared = wide[:, 0, rows:] + wide[:, 1, rows:]
    key_grad = jnp.concatenate(
        [wide[:, 0, :rows, :HD], wide[:, 1, :rows, :HD], shared[..., :HD]], axis=-1
    )
    value_grad = jnp.concatenate(
        [wide[:, 0, :rows, HD:], wide[:, 1, :rows, HD:], shared[..., HD:]], axis=-1
    )
    turned_grad = turned(
        jnp.concatenate([query_grad, key_grad], axis=-1).reshape(SHARDS * rows, 2 * part), -1.0
    )
    heads_delta = jnp.concatenate([turned_grad, value_grad.reshape(SHARDS * rows, part)], axis=-1)
    heads_half = heads_delta.astype(half)
    heads_local = over_tokens(first_in, heads_half).reshape(SHARDS, CTX, strip, 3 * part)
    output_local = over_tokens(attn, grad_half).reshape(CTX, strip, width)
    heads_strip = scatter_ctx(heads_local, ctx_place, 1)
    output_strip = scatter_ctx(output_local, ctx_place, 0)
    output_part = jnp.dot(attn, output_block, preferred_element_type=single)
    first_part = over_columns(heads_half, heads_block)

    def home(x):
        x = x.reshape(SHARDS, rows, width)
        total = x[0]
        for k in range(1, SHARDS):
            total = total + swap(x[k].astype(half), "fsdp", k).astype(single)
        return total

    mine = inputs[:rows]
    block_out = (mine + (home(output_part + mlp_part) + output_shift + down_shift)).astype(half)
    second_delta = home(second_part)
    first_delta = home(first_part)
    my_normed, my_inverse = normed[:rows], inverse[:rows]
    input_grad = (
        cotangent[0]
        + norm_back(first_delta, my_normed, my_inverse, gain_one)
        + norm_back(second_delta, my_normed, my_inverse, gain_two)
    )

    strips = jnp.concatenate([heads_strip, up_strip, down_strip], axis=-1).astype(half)
    whole = in_order(spread(strips, shard_place), shard_place)
    heads_grad = jnp.moveaxis(
        whole[..., : 3 * part].reshape(SHARDS, strip, 3, part), 0, 2
    ).reshape(strip, 3 * width)
    up_grad = jnp.moveaxis(whole[..., 3 * part : 3 * part + hidden_part], 0, 1).reshape(
        strip, hidden
    )
    down_grad = jnp.moveaxis(whole[..., 3 * part + hidden_part :], 0, 1).reshape(strip, hidden)
    strip_grads = (heads_grad, output_strip.astype(half), up_grad, down_grad)
    moments_all = (heads_moment, output_moment, up_moment, down_moment)
    weights_all = (heads_weight, output_weight, up_weight, down_weight)
    nests = []
    for which in range(4):
        grad = strip_grads[which].astype(single)
        moment = mom_rate * lax.dynamic_slice_in_dim(
            moments_all[which], ctx_place * strip, strip, 0
        ) + grad
        nest = (grad + mom_rate * moment).astype(half)
        nests.append(jnp.pad(nest, ((0, 0), (0, hidden - nest.shape[1]))))
    owned = jnp.stack(spread(jnp.stack(nests), shard_place))
    nest = jnp.stack(gather_ctx(owned)).reshape(width, hidden)
    grads_all = jnp.stack(gather_ctx(jnp.concatenate(strip_grads, axis=-1)))
    full_grads, new_moments = write_moments(grads_all, moments_all, ctx_place)

    wide_nest = nest.astype(single)
    size = jnp.sqrt(jnp.sum(wide_nest * wide_nest))
    ortho = (wide_nest / (size + 1e-07)).astype(half)
    for turn in range(NS_ITERS):
        gram = over_columns(ortho, ortho).astype(half)
        mix = (
            schulz_coeffs[1] * gram.astype(single)
            + schulz_coeffs[2] * jnp.dot(gram, gram, preferred_element_type=single)
        ).astype(half)
        ortho = (
            schulz_coeffs[0] * ortho.astype(single)
            + jnp.dot(mix, ortho, preferred_element_type=single)
        ).astype(half)
    ortho = ortho.reshape(CTX, SHARDS, strip, hidden)
    arrived = jnp.stack(
        [ortho[:, 0]] + [swap(ortho[:, k], "fsdp", k) for k in range(1, SHARDS)]
    )
    new_weights = write_weights(arrived, weights_all, ctx_place, shard_place)

    heads_sum = jnp.sum(heads_delta, axis=0).reshape(3, 1, part)
    heads_sum = lax.dynamic_update_slice(
        jnp.zeros((3, SHARDS, part), single), heads_sum, (0, shard_place, 0)
    ).reshape(3 * width)
    up_sum = lax.dynamic_update_slice(
        jnp.zeros((hidden,), single), jnp.sum(up_delta, axis=0), (shard_place * hidden_part,)
    )
    sums = lax.psum(
        jnp.concatenate(
            [
                jnp.sum(first_delta * my_normed, axis=0),
                jnp.sum(first_delta, axis=0),
                jnp.sum(second_delta * my_normed, axis=0),
                jnp.sum(second_delta, axis=0),
                jnp.sum(cotangent[0], axis=0),
                heads_sum,
                up_sum,
            ]
        ),
        ("ctx", "fsdp"),
    )
    pieces = [sums[i * width : (i + 1) * width] for i in range(5)]
    heads_total = sums[5 * width : 8 * width]
    up_total = sums[8 * width :]
    vector_values = (
        gain_first,
        shift_first,
        gain_second,
        shift_second,
        heads_bias,
        output_bias,
        up_bias,
        down_bias,
    )
    vector_grads = (
        pieces[0],
        pieces[1],
        pieces[2],
        pieces[3],
        heads_total,
        pieces[4],
        up_total,
        pieces[4],
    )
    grad_shards = []
    new_shards = []
    for which in range(8):
        size_here = vector_values[which].shape[0]
        whole_grad = vector_grads[which]
        shard = lax.dynamic_slice_in_dim(whole_grad, shard_place * size_here, size_here)
        grad_shards.append(shard)
        new_shards.append(
            vector_values[which]
            - vector_rate * shard * lax.rsqrt(jnp.mean(whole_grad * whole_grad) + norm_eps)
        )
    return (
        block_out[None],
        input_grad[None],
        grad_shards[0],
        grad_shards[1],
        grad_shards[2],
        grad_shards[3],
        full_grads[0],
        grad_shards[4],
        full_grads[1],
        grad_shards[5],
        full_grads[2],
        grad_shards[6],
        full_grads[3],
        grad_shards[7],
        new_shards[0],
        new_shards[1],
        new_shards[2],
        new_shards[3],
        new_weights[0],
        new_shards[4],
        new_weights[1],
        new_shards[5],
        new_weights[2],
        new_shards[6],
        new_weights[3],
        new_shards[7],
        new_moments[0],
        new_moments[1],
        new_moments[2],
        new_moments[3],
    )


def solution(mesh):
    in_specs = (
        P("fsdp", "ctx", None),
        P("fsdp", "ctx", None),
        P(),
        P("fsdp"),
        P("fsdp"),
        P("fsdp"),
        P("fsdp"),
        P("fsdp", None),
        P("fsdp"),
        P("fsdp", None),
        P("fsdp"),
        P("fsdp", None),
        P("fsdp"),
        P("fsdp", None),
        P("fsdp"),
        P("fsdp", None),
        P("fsdp", None),
        P("fsdp", None),
        P("fsdp", None),
    )
    out_specs = (
        P("fsdp", "ctx", None),
        P("fsdp", "ctx", None),
        P("fsdp"),
        P("fsdp"),
        P("fsdp"),
        P("fsdp"),
        P("fsdp", None),
        P("fsdp"),
        P("fsdp", None),
        P("fsdp"),
        P("fsdp", None),
        P("fsdp"),
        P("fsdp", None),
        P("fsdp"),
        P("fsdp"),
        P("fsdp"),
        P("fsdp"),
        P("fsdp"),
        P("fsdp", None),
        P("fsdp"),
        P("fsdp", None),
        P("fsdp"),
        P("fsdp", None),
        P("fsdp"),
        P("fsdp", None),
        P("fsdp"),
        P("fsdp", None),
        P("fsdp", None),
        P("fsdp", None),
        P("fsdp", None),
    )
    sizes = dict(mesh.shape)
    fits = sizes["ctx"] == 8 and sizes["fsdp"] == 4
    chosen = local_fast if fits else local_general
    return jax.shard_map(chosen, mesh=mesh, in_specs=in_specs, out_specs=out_specs, check_vma=False)
```

```python
import math

import jax
import jax.numpy as jnp
from jax import lax
from jax.experimental import pallas as pl
from jax.experimental.pallas import tpu as pltpu
from jax.sharding import PartitionSpec as P

HEADS = 12
HD = 64
ROT = 16
NS_ITERS = 5


mom_rate = 0.95
schulz_coeffs = (3.4445, -4.775, 2.0315)
step_rates = (0.04, 0.3, 0.04, 0.04)
vector_rate = 0.3
norm_eps = 1e-05
neg_large = -1e30


def broadcast(x, axis, root):
    mine = lax.axis_index(axis) == root
    return lax.psum(jnp.where(mine, x, jnp.zeros_like(x)), axis)


def layer_norm(inputs, gain, shift):
    average = jnp.mean(inputs, axis=-1, keepdims=True)
    centred = inputs - average
    variance = jnp.mean(centred * centred, axis=-1, keepdims=True)
    inverse = lax.rsqrt(variance + norm_eps)
    normed = centred * inverse
    return (normed, inverse, normed * gain + shift)


def norm_back(delta, normed, inverse, gain):
    scaled = delta * gain
    first = jnp.mean(scaled, axis=-1, keepdims=True)
    second = jnp.mean(scaled * normed, axis=-1, keepdims=True)
    return inverse * (scaled - first - normed * second)


def gelu_value(pre):
    return 0.5 * pre * (1.0 + lax.erf(pre / math.sqrt(2.0)))


def gelu_slope(pre):
    return 0.5 * (1.0 + lax.erf(pre / math.sqrt(2.0))) + pre * jnp.exp(
        -0.5 * pre * pre
    ) / math.sqrt(2.0 * math.pi)


def slot_places(group_order, first_row, count, group):
    positions = first_row + jnp.arange(count, dtype=jnp.int32)
    slots = positions // group
    table = jnp.arange(group_order.shape[0], dtype=jnp.int32)
    picked = jnp.sum(jnp.where(slots[:, None] == table[None, :], group_order[None, :], 0), axis=1)
    return picked * group + positions % group


def rotary_tables(places):
    halfway = ROT // 2
    rates = 10000.0 ** (-2.0 * jnp.arange(halfway, dtype=jnp.float32) / ROT)
    angle = places.astype(jnp.float32)[:, None] * rates[None, :]
    return (jnp.cos(angle), jnp.sin(angle))


def rotate(heads, cosine, sine, sign):
    halfway = ROT // 2
    first = heads[..., :halfway]
    second = heads[..., halfway:ROT]
    cosine = cosine[:, None, :]
    sine = sign * sine[:, None, :]
    return jnp.concatenate(
        [first * cosine - second * sine, second * cosine + first * sine, heads[..., ROT:]], axis=-1
    )


def local_general(
    residual_in,
    cotangent,
    group_order,
    gain_first,
    shift_first,
    gain_second,
    shift_second,
    heads_weight,
    heads_bias,
    output_weight,
    output_bias,
    up_weight,
    up_bias,
    down_weight,
    down_bias,
    heads_moment,
    output_moment,
    up_moment,
    down_moment,
):
    single = jnp.float32
    half = jnp.bfloat16
    ctx_count = lax.axis_size("ctx")
    shard_count = lax.axis_size("fsdp")
    ctx_place = lax.axis_index("ctx")
    shard_place = lax.axis_index("fsdp")
    seqs, rows, width = residual_in.shape
    length = rows * ctx_count
    group = rows // 2
    scale = 1.0 / math.sqrt(HD)
    query_places = slot_places(group_order, ctx_place * rows, rows, group)
    key_places = slot_places(group_order, 0, length, group)
    copies = (
        lax.all_gather(heads_weight.astype(half), "fsdp", axis=0, tiled=True),
        lax.all_gather(output_weight.astype(half), "fsdp", axis=0, tiled=True),
        lax.all_gather(up_weight.astype(half), "fsdp", axis=0, tiled=True),
        lax.all_gather(down_weight.astype(half), "fsdp", axis=0, tiled=True),
        lax.all_gather(gain_first.astype(half), "fsdp", axis=0, tiled=True),
        lax.all_gather(shift_first.astype(half), "fsdp", axis=0, tiled=True),
        lax.all_gather(gain_second.astype(half), "fsdp", axis=0, tiled=True),
        lax.all_gather(shift_second.astype(half), "fsdp", axis=0, tiled=True),
        lax.all_gather(heads_bias.astype(half), "fsdp", axis=0, tiled=True),
        lax.all_gather(output_bias.astype(half), "fsdp", axis=0, tiled=True),
        lax.all_gather(up_bias.astype(half), "fsdp", axis=0, tiled=True),
        lax.all_gather(down_bias.astype(half), "fsdp", axis=0, tiled=True),
    )
    heads_copy, output_copy, up_copy, down_copy = (copies[0], copies[1], copies[2], copies[3])
    gain_one, shift_one, gain_two, shift_two, heads_shift, output_shift, up_shift, down_shift = [
        piece.astype(single) for piece in copies[4:]
    ]
    inputs = residual_in.astype(single)
    first_hat, first_inv, first_norm = layer_norm(inputs, gain_one, shift_one)
    second_hat, second_inv, second_norm = layer_norm(inputs, gain_two, shift_two)
    first_in = first_norm.astype(half)
    second_in = second_norm.astype(half)
    projected = (
        jnp.einsum("std,de->ste", first_in, heads_copy, preferred_element_type=single) + heads_shift
    )
    cosine, sine = rotary_tables(query_places)
    split = projected.reshape(seqs, rows, 3, HEADS, HD)
    query = rotate(split[:, :, 0], cosine, sine, 1.0).astype(half)
    keys = rotate(split[:, :, 1], cosine, sine, 1.0).astype(half).reshape(seqs, rows, width)
    values = split[:, :, 2].astype(half).reshape(seqs, rows, width)
    peak = jnp.full((seqs, HEADS, rows), neg_large, single)
    key_piece = lax.all_gather(keys, "ctx", axis=1, tiled=True)
    value_piece = lax.all_gather(values, "ctx", axis=1, tiled=True)
    count = key_piece.shape[1]
    places = slot_places(group_order, jnp.int32(0), count, group)
    key_heads = key_piece.reshape(seqs, count, HEADS, HD)
    value_heads = value_piece.reshape(seqs, count, HEADS, HD)
    score = jnp.einsum("sqhd,skhd->shqk", query, key_heads, preferred_element_type=single) * scale
    allowed = (places[None, :] <= query_places[:, None])[None, None]
    new_peak = jnp.maximum(peak, jnp.max(jnp.where(allowed, score, neg_large), axis=-1))
    weights = jnp.where(allowed, jnp.exp(score - new_peak[..., None]), 0.0)
    total = jnp.sum(weights, axis=-1)
    mixed = jnp.einsum(
        "shqk,skhd->shqd", weights.astype(half), value_heads, preferred_element_type=single
    )
    state = (new_peak, total, mixed)
    peak, total, mixed = state
    lse = peak + jnp.log(total)
    attn = (
        jnp.transpose(mixed / total[..., None], (0, 2, 1, 3))
        .reshape(seqs, rows, width)
        .astype(half)
    )
    output_part = (
        jnp.einsum("std,de->ste", attn, output_copy, preferred_element_type=single) + output_shift
    )
    up_pre = jnp.einsum("std,df->stf", second_in, up_copy, preferred_element_type=single) + up_shift
    active = gelu_value(up_pre).astype(half)
    mlp_part = (
        jnp.einsum("stf,df->std", active, down_copy, preferred_element_type=single) + down_shift
    )
    block_out = (inputs + output_part + mlp_part).astype(half)
    grad_half = cotangent.astype(half)
    down_local = jnp.einsum("std,stf->df", grad_half, active, preferred_element_type=single)
    up_delta = jnp.einsum(
        "std,df->stf", grad_half, down_copy, preferred_element_type=single
    ) * gelu_slope(up_pre)
    up_half = up_delta.astype(half)
    up_local = jnp.einsum("std,stf->df", second_in, up_half, preferred_element_type=single)
    second_delta = jnp.einsum("stf,df->std", up_half, up_copy, preferred_element_type=single)
    output_local = jnp.einsum("std,ste->de", attn, grad_half, preferred_element_type=single)
    attn_delta = jnp.einsum(
        "ste,de->std", grad_half, output_copy, preferred_element_type=single
    ).astype(half)
    attn_heads = attn_delta.reshape(seqs, rows, HEADS, HD)
    delta = jnp.transpose(
        jnp.sum(
            attn_heads.astype(single) * attn.reshape(seqs, rows, HEADS, HD).astype(single), axis=-1
        ),
        (0, 2, 1),
    )
    every_key, every_value = (
        lax.all_gather(keys, "ctx", axis=1, tiled=True),
        lax.all_gather(values, "ctx", axis=1, tiled=True),
    )
    block = math.gcd(length, 512)
    count = length // block
    key_blocks = jnp.moveaxis(every_key.reshape(seqs, count, block, HEADS, HD), 1, 0)
    value_blocks = jnp.moveaxis(every_value.reshape(seqs, count, block, HEADS, HD), 1, 0)
    place_blocks = key_places.reshape(count, block)

    def back_block(query_grad, data):
        key_block, value_block, place_block = data
        score = (
            jnp.einsum("sqhd,skhd->shqk", query, key_block, preferred_element_type=single) * scale
        )
        allowed = (place_block[None, :] <= query_places[:, None])[None, None]
        prob = jnp.where(allowed, jnp.exp(score - lse[..., None]), 0.0)
        prob_half = prob.astype(half)
        prob_grad = jnp.einsum(
            "sqhd,skhd->shqk", attn_heads, value_block, preferred_element_type=single
        )
        score_delta = (prob * (prob_grad - delta[..., None])).astype(half)
        query_grad = (
            query_grad
            + jnp.einsum("shqk,skhd->sqhd", score_delta, key_block, preferred_element_type=single)
            * scale
        )
        key_grad = (
            jnp.einsum("shqk,sqhd->skhd", score_delta, query, preferred_element_type=single) * scale
        )
        value_grad = jnp.einsum(
            "shqk,sqhd->skhd", prob_half, attn_heads, preferred_element_type=single
        )
        joined = jnp.concatenate(
            [key_grad.reshape(seqs, block, width), value_grad.reshape(seqs, block, width)], axis=-1
        )
        return (query_grad, joined)

    query_grad, stacked = lax.scan(
        back_block,
        jnp.zeros((seqs, rows, HEADS, HD), single),
        (key_blocks, value_blocks, place_blocks),
    )
    key_grads = jnp.moveaxis(stacked, 0, 1).reshape(seqs, length, 2 * width)
    home = lax.psum_scatter(key_grads, "ctx", scatter_dimension=1, tiled=True)
    key_delta = rotate(home[..., :width].reshape(seqs, rows, HEADS, HD), cosine, sine, -1.0)
    query_delta = rotate(query_grad, cosine, sine, -1.0)
    heads_delta = jnp.concatenate(
        [
            query_delta.reshape(seqs, rows, width),
            key_delta.reshape(seqs, rows, width),
            home[..., width:],
        ],
        axis=-1,
    )
    heads_half = heads_delta.astype(half)
    heads_local = jnp.einsum("std,ste->de", first_in, heads_half, preferred_element_type=single)
    first_delta = jnp.einsum("ste,de->std", heads_half, heads_copy, preferred_element_type=single)
    input_grad = (
        cotangent
        + norm_back(first_delta, first_hat, first_inv, gain_one)
        + norm_back(second_delta, second_hat, second_inv, gain_two)
    )
    columns = (
        lax.psum_scatter(heads_local, "ctx", scatter_dimension=1, tiled=True),
        lax.psum_scatter(output_local, "ctx", scatter_dimension=1, tiled=True),
        lax.psum_scatter(up_local, "ctx", scatter_dimension=1, tiled=True),
        lax.psum_scatter(down_local, "ctx", scatter_dimension=1, tiled=True),
    )
    parts = (
        lax.psum_scatter(columns[0], "fsdp", scatter_dimension=0, tiled=True),
        lax.psum_scatter(columns[1], "fsdp", scatter_dimension=0, tiled=True),
        lax.psum_scatter(columns[2], "fsdp", scatter_dimension=0, tiled=True),
        lax.psum_scatter(columns[3], "fsdp", scatter_dimension=0, tiled=True),
    )
    full_grads = (
        lax.all_gather(parts[0], "ctx", axis=1, tiled=True),
        lax.all_gather(parts[1], "ctx", axis=1, tiled=True),
        lax.all_gather(parts[2], "ctx", axis=1, tiled=True),
        lax.all_gather(parts[3], "ctx", axis=1, tiled=True),
    )
    weights_all = (heads_weight, output_weight, up_weight, down_weight)
    moments_all = (heads_moment, output_moment, up_moment, down_moment)
    new_moments = []
    nest_blocks = []
    for which in range(4):
        moment = mom_rate * moments_all[which] + full_grads[which]
        nest = full_grads[which] + mom_rate * moment
        cols = nest.shape[1] // ctx_count
        new_moments.append(moment)
        nest_blocks.append(lax.dynamic_slice_in_dim(nest, ctx_place * cols, cols, 1))
    sums = lax.psum(
        (
            jnp.sum(first_delta * first_hat, axis=(0, 1)),
            jnp.sum(first_delta, axis=(0, 1)),
            jnp.sum(second_delta * second_hat, axis=(0, 1)),
            jnp.sum(second_delta, axis=(0, 1)),
            jnp.sum(heads_delta, axis=(0, 1)),
            jnp.sum(cotangent, axis=(0, 1)),
            jnp.sum(up_delta, axis=(0, 1)),
            jnp.sum(nest_blocks[0] * nest_blocks[0]),
            jnp.sum(nest_blocks[1] * nest_blocks[1]),
            jnp.sum(nest_blocks[2] * nest_blocks[2]),
            jnp.sum(nest_blocks[3] * nest_blocks[3]),
        ),
        ("ctx", "fsdp"),
    )
    gathered = (
        lax.all_gather(nest_blocks[0], "fsdp", axis=0, tiled=True),
        lax.all_gather(nest_blocks[1], "fsdp", axis=0, tiled=True),
        lax.all_gather(nest_blocks[2], "fsdp", axis=0, tiled=True),
        lax.all_gather(nest_blocks[3], "fsdp", axis=0, tiled=True),
    )
    widths = [piece.shape[1] for piece in gathered]
    widest = max(widths)
    owners = [which * shard_count // 4 for which in range(4)]
    selected = jnp.zeros((width, widest), single)
    square_sum = jnp.zeros((), single)
    for which in range(4):
        chosen = (shard_place == owners[which]).astype(single)
        selected = selected + chosen * jnp.pad(
            gathered[which], ((0, 0), (0, widest - widths[which]))
        )
        square_sum = square_sum + chosen * sums[7 + which]
    ortho = (selected / (jnp.sqrt(square_sum) + 1e-07)).astype(half)
    for turn in range(NS_ITERS):
        partial_value = jnp.einsum("rw,sw->rs", ortho, ortho, preferred_element_type=single)
        gram = lax.psum(partial_value.astype(jnp.bfloat16), "ctx").astype(jnp.float32).astype(half)
        mix = (
            schulz_coeffs[1] * gram.astype(single)
            + schulz_coeffs[2] * jnp.dot(gram, gram, preferred_element_type=single)
        ).astype(half)
        ortho = (
            schulz_coeffs[0] * ortho.astype(single)
            + jnp.dot(mix, ortho, preferred_element_type=single)
        ).astype(half)
    shard_rows = width // shard_count
    updated = []
    for which in range(4):
        received = broadcast(ortho, "fsdp", owners[which])
        piece = lax.dynamic_slice(
            received, (shard_place * shard_rows, 0), (shard_rows, widths[which])
        )
        total_cols = weights_all[which].shape[1]
        current = lax.dynamic_slice_in_dim(
            weights_all[which], ctx_place * widths[which], widths[which], 1
        )
        updated.append(current - step_rates[which] * math.sqrt(total_cols) * piece.astype(single))
    new_weights = (
        lax.all_gather(updated[0], "ctx", axis=1, tiled=True),
        lax.all_gather(updated[1], "ctx", axis=1, tiled=True),
        lax.all_gather(updated[2], "ctx", axis=1, tiled=True),
        lax.all_gather(updated[3], "ctx", axis=1, tiled=True),
    )
    vector_values = (
        gain_first,
        shift_first,
        gain_second,
        shift_second,
        heads_bias,
        output_bias,
        up_bias,
        down_bias,
    )
    vector_grads = (sums[0], sums[1], sums[2], sums[3], sums[4], sums[5], sums[6], sums[5])
    grad_shards = []
    new_shards = []
    for which in range(8):
        size_here = vector_values[which].shape[0]
        whole_grad = vector_grads[which]
        shard = lax.dynamic_slice_in_dim(whole_grad, shard_place * size_here, size_here)
        grad_shards.append(shard)
        new_shards.append(
            vector_values[which]
            - vector_rate * shard * lax.rsqrt(jnp.mean(whole_grad * whole_grad) + norm_eps)
        )
    return (
        block_out,
        input_grad,
        grad_shards[0],
        grad_shards[1],
        grad_shards[2],
        grad_shards[3],
        full_grads[0],
        grad_shards[4],
        full_grads[1],
        grad_shards[5],
        full_grads[2],
        grad_shards[6],
        full_grads[3],
        grad_shards[7],
        new_shards[0],
        new_shards[1],
        new_shards[2],
        new_shards[3],
        new_weights[0],
        new_shards[4],
        new_weights[1],
        new_shards[5],
        new_weights[2],
        new_shards[6],
        new_weights[3],
        new_shards[7],
        new_moments[0],
        new_moments[1],
        new_moments[2],
        new_moments[3],
    )


Y_PLACES = 2
Z_PLACES = 4
CTX = Y_PLACES * Z_PLACES
SHARDS = 4


OWNERS = (0, 2, 1, 3)


def swap(x, axis, offset):
    count = lax.axis_size(axis)
    return lax.ppermute(x, axis, [(i, i ^ offset) for i in range(count)])


def exchange(x, axis="fsdp"):
    return lax.all_to_all(x, axis, 0, 0)


def pick(x, index, dim=0):
    return lax.dynamic_index_in_dim(x, index, dim, keepdims=False)


def gather_z(x):
    return [x] + [swap(x, "ctx", Y_PLACES * k) for k in range(1, Z_PLACES)]


def gather_y(along):
    pieces = []
    for piece in along:
        pieces += [piece, swap(piece, "ctx", 1)]
    return pieces


def call(kernel, outs, args, prefetch, name, cost, scratch=(), earlier=()):
    whole = pl.BlockSpec(memory_space=pltpu.VMEM)
    count = 1 + len(args)

    def body(*refs):
        kernel(*refs[:count], *refs[count + len(earlier) :])

    return pl.pallas_call(
        body,
        in_specs=[pl.BlockSpec(memory_space=pltpu.SMEM)]
        + [whole] * len(args)
        + [pl.BlockSpec(memory_space=pl.ANY)] * len(earlier),
        out_specs=[whole] * len(outs),
        out_shape=[jax.ShapeDtypeStruct(shape, dtype) for shape, dtype in outs],
        scratch_shapes=list(scratch),
        compiler_params=pltpu.CompilerParams(vmem_limit_bytes=50 * 1024 * 1024),
        cost_estimate=pl.CostEstimate(
            flops=0, bytes_accessed=int(cost * 3.6e6), transcendentals=0
        ),
        name=name,
    )(prefetch, *args, *earlier)


NT = (((1,), (1,)), ((), ()))
TN = (((0,), (0,)), ((), ()))


def pack_kernel(where_ref, residual_ref, grad_ref, *refs):
    half = jnp.bfloat16
    vectors, out_ref = refs[:7], refs[7]
    place = where_ref[2]
    rows, width = residual_ref.shape

    def share(ref):
        size = ref.shape[1]
        lane = lax.broadcasted_iota(jnp.int32, (1, SHARDS * size), 1)
        mine = jnp.logical_and(lane >= place * size, lane < (place + 1) * size)
        return jnp.where(mine, jnp.concatenate([ref[...]] * SHARDS, axis=1), 0.0)

    heads = share(vectors[6])
    out_ref[:rows] = residual_ref[...]
    out_ref[rows : 2 * rows] = grad_ref[...].astype(half)
    small = [share(v) for v in vectors[:6]]
    small += [heads[:, t * width : (t + 1) * width] for t in range(3)]
    small.append(jnp.zeros((16 - len(small), width), jnp.float32))
    out_ref[2 * rows :] = jnp.concatenate(small, axis=0).astype(half)


def heads_split_kernel(where_ref, weight_ref, out_ref):
    part, width = weight_ref.shape[0], weight_ref.shape[1] // 3
    for dest in range(SHARDS):
        out_ref[dest] = jnp.concatenate(
            [
                weight_ref[:, t * width + dest * part : t * width + (dest + 1) * part]
                for t in range(3)
            ],
            axis=1,
        ).astype(jnp.bfloat16)


def mlp_split_kernel(where_ref, up_ref, down_ref, moments_ref, *outs):
    place = where_ref[2]
    part, cols = up_ref.shape[0], up_ref.shape[1] // SHARDS
    for k in range(SHARDS):
        cut = pl.ds(pl.multiple_of((place ^ k) * cols, cols), cols)
        outs[k][:part, :cols] = up_ref[:, cut].astype(jnp.bfloat16)
        outs[k][:part, cols:] = down_ref[:, cut].astype(jnp.bfloat16)
        moment = moments_ref[place ^ k]
        outs[k][part:] = jnp.concatenate(
            [moment[:, : 2 * cols], moment[:, 2 * cols :]], axis=0
        ).astype(jnp.bfloat16)


def turn(x, cos_ref, high_ref, low_ref, direction):
    lanes = x.shape[1]
    moved = pltpu.roll(x, ROT // 2, 1) * high_ref[...] + pltpu.roll(
        x, lanes - ROT // 2, 1
    ) * low_ref[...]
    return x * cos_ref[...] + direction * moved


def pre_kernel(where_ref, *refs):
    single, half = jnp.float32, jnp.bfloat16
    packs, block_ref = refs[:4], refs[4]
    output_ref, cos_ref, high_ref, low_ref = refs[5:9]
    first_ref, second_ref, grad_ref, payload_ref, normed_ref, inverse_ref = refs[9:]
    place = where_ref[2]
    part = output_ref.shape[0]
    rows = normed_ref.shape[0]
    vectors = sum(p[2 * rows :].astype(single) for p in packs)
    for r in range(SHARDS):
        x = packs[r][:rows].astype(single)
        average = jnp.mean(x, axis=-1, keepdims=True)
        centred = x - average
        variance = jnp.mean(centred * centred, axis=-1, keepdims=True)
        inverse = lax.rsqrt(variance + norm_eps)
        normed = centred * inverse
        if r == 0:
            normed_ref[...] = normed
            inverse_ref[...] = jnp.broadcast_to(inverse, inverse_ref.shape)
        cut = slice(r * rows, (r + 1) * rows)
        first_ref[cut] = (normed * vectors[0:1] + vectors[1:2]).astype(half)
        second_ref[cut] = (normed * vectors[2:3] + vectors[3:4]).astype(half)
        grad_ref[cut] = packs[r][rows : 2 * rows]
    shift = jnp.concatenate(
        [
            sum(
                jnp.where(place == j, vectors[6 + t : 7 + t, j * part : (j + 1) * part], 0.0)
                for j in range(SHARDS)
            )
            for t in range(3)
        ],
        axis=1,
    )
    projected = jnp.dot(first_ref[...], block_ref[...], preferred_element_type=single) + shift
    outer = lax.dot_general(
        grad_ref[...], output_ref[...], NT, preferred_element_type=single
    ).astype(half)
    for r in range(SHARDS):
        cut = slice(r * rows, (r + 1) * rows)
        turned = turn(projected[cut, : 2 * part], cos_ref, high_ref, low_ref, 1.0).astype(half)
        values = projected[cut, 2 * part :].astype(half)
        back = outer[cut]

        def head(x, h):
            return x[:, h * HD : (h + 1) * HD]

        last = 3 * Z_PLACES // 4 - 1
        shared = jnp.concatenate([head(turned, 3 + last), head(values, last)], axis=1)
        query = jnp.concatenate([head(turned, last), head(back, last)], axis=1)
        for y in range(Y_PLACES):
            at = r * Y_PLACES + y
            payload_ref[at, :rows] = jnp.concatenate([head(turned, y), head(turned, 3 + y)], axis=1)
            payload_ref[at, rows : 2 * rows] = jnp.concatenate(
                [head(values, y), head(back, y)], axis=1
            )
            payload_ref[at, 2 * rows : 3 * rows] = shared
            payload_ref[at, 3 * rows :] = query[y * rows // 2 : (y + 1) * rows // 2]


def write_strips(grad_ref, send_ref, keep_ref, y):
    strip = send_ref.shape[2]
    for f in range(SHARDS):
        for z in range(Z_PLACES):
            start = (f * CTX + z * Y_PLACES) * strip
            mine = pl.multiple_of(start + y * strip, 8)
            other = pl.multiple_of(start + (1 - y) * strip, 8)
            keep_ref[f, z] = grad_ref[pl.ds(mine, strip), :]
            send_ref[f, z] = grad_ref[pl.ds(other, strip), :].astype(jnp.bfloat16)


def mlp_kernel(where_ref, *refs):
    single, half = jnp.float32, jnp.bfloat16
    second_ref, grad_ref, shift_ref = refs[:3]
    pieces = refs[3:7]
    send_ref, keep_ref, out_ref, sum_ref, back_ref, block_ref, local_ref = refs[7:]
    y, place = where_ref[1], where_ref[2]
    cols = shift_ref.shape[1]
    part = block_ref.shape[0] // SHARDS
    for k in range(SHARDS):
        block_ref[pl.ds(pl.multiple_of((place ^ k) * part, part), part), :] = pieces[k][:part]
    second, grad = second_ref[...], grad_ref[...]
    up = block_ref[:, :cols]
    down = block_ref[:, cols:]
    pre = jnp.dot(second, up, preferred_element_type=single) + shift_ref[...]
    cdf = 0.5 * (1.0 + lax.erf(pre * (1.0 / math.sqrt(2.0))))
    active = (pre * cdf).astype(half)
    slope = cdf + pre * jnp.exp(-0.5 * pre * pre) * (1.0 / math.sqrt(2.0 * math.pi))
    delta = jnp.dot(grad, down, preferred_element_type=single) * slope
    sum_ref[...] = jnp.sum(delta, axis=0, keepdims=True)
    delta_half = delta.astype(half)
    local_ref[:, :cols] = lax.dot_general(second, delta_half, TN, preferred_element_type=single)
    local_ref[:, cols:] = lax.dot_general(grad, active, TN, preferred_element_type=single)
    write_strips(local_ref, send_ref, keep_ref, y)
    out_ref[...] = lax.dot_general(active, down, NT, preferred_element_type=single)
    back_ref[...] = lax.dot_general(delta_half, up, NT, preferred_element_type=single)


def post_kernel(where_ref, *refs):
    single, half = jnp.float32, jnp.bfloat16
    back_ref, first_ref, grad_ref, block_ref, output_ref, mlp_ref, second_ref = refs[:7]
    cos_ref, high_ref, low_ref = refs[7:10]
    send_ref, keep_ref, sum_ref, mine_ref, home_ref = refs[10:15]
    attn_ref, heads_ref, local_ref = refs[15:]
    y, place = where_ref[1], where_ref[2]
    part, width = output_ref.shape
    rows = mine_ref.shape[0] // 3
    sums = jnp.zeros((1, 3 * part), single)
    for r in range(SHARDS):
        cut = slice(r * rows, (r + 1) * rows)
        early = [back_ref[r * Y_PLACES + i, :rows] for i in range(Y_PLACES)]
        early.append(
            jnp.concatenate([back_ref[r * Y_PLACES + i, 3 * rows :] for i in range(Y_PLACES)], axis=0)
        )
        late = [back_ref[r * Y_PLACES + i, rows : 2 * rows].astype(single) for i in range(Y_PLACES)]
        late.append(
            sum(back_ref[r * Y_PLACES + i, 2 * rows : 3 * rows].astype(single) for i in range(Y_PLACES))
        )
        attn_ref[cut] = jnp.concatenate([x[:, :HD] for x in early], axis=1)
        turned = turn(
            jnp.concatenate(
                [x[:, HD:].astype(single) for x in early] + [x[:, :HD] for x in late], axis=1
            ),
            cos_ref,
            high_ref,
            low_ref,
            -1.0,
        )
        whole = jnp.concatenate([turned] + [x[:, HD:] for x in late], axis=1)
        sums += jnp.sum(whole, axis=0, keepdims=True)
        heads_ref[cut] = whole.astype(half)
    sum_ref[...] = sums
    local_ref[:, : 3 * part] = lax.dot_general(
        first_ref[...], heads_ref[...], TN, preferred_element_type=single
    )
    output_local = lax.dot_general(
        attn_ref[...], grad_ref[...], TN, preferred_element_type=single
    )
    for j in range(SHARDS):
        local_ref[j * part : (j + 1) * part, 3 * part :] = output_local[:, j * part : (j + 1) * part]
    write_strips(local_ref, send_ref, keep_ref, y)
    out = jnp.dot(attn_ref[...], output_ref[...], preferred_element_type=single) + mlp_ref[...]
    first = lax.dot_general(heads_ref[...], block_ref[...], NT, preferred_element_type=single)
    for i, value in enumerate((out, first, second_ref[...])):
        cut = slice(i * rows, (i + 1) * rows)
        mine_ref[cut] = value[:rows]
        home_ref[place, cut] = jnp.zeros((rows, width), half)
        for k in range(1, SHARDS):
            home_ref[place ^ k, cut] = value[k * rows : (k + 1) * rows].astype(half)


def along_z_kernel(where_ref, keep_ref, came_ref, own_ref, *sends):
    z = where_ref[0]
    own_ref[...] = keep_ref[:, z] + came_ref[:, z].astype(jnp.float32)
    for k in range(1, Z_PLACES):
        sends[k - 1][...] = (keep_ref[:, z ^ k] + came_ref[:, z ^ k].astype(jnp.float32)).astype(
            jnp.bfloat16
        )


def scatter_ctx(send, keep, where, name, *earlier):
    single, half = jnp.float32, jnp.bfloat16
    came = swap(send, "ctx", 1)
    shape = (keep.shape[0],) + keep.shape[2:]
    own, *sends = call(
        along_z_kernel,
        [(shape, single)] + [(shape, half)] * (Z_PLACES - 1),
        [keep, came],
        where,
        name,
        0.1,
        earlier=earlier,
    )
    return came, [own] + [swap(sends[k - 1], "ctx", 2 * k) for k in range(1, Z_PLACES)]


def strip_sum(parts, index):
    return parts[0][index] + sum(p[index].astype(jnp.float32) for p in parts[1:])


def strip_kernel(where_ref, *refs):
    half = jnp.bfloat16
    heads, mlp = refs[:4], refs[4:8]
    strips_ref, owners_ref, output_ref = refs[8:]
    size = owners_ref.shape[3]
    cols = 3 * size // 4
    for j in range(SHARDS):
        total = strip_sum(heads, j)
        both = strip_sum(mlp, j).astype(half)
        strips_ref[j, :, : 2 * size] = both
        strips_ref[j, :, 2 * size :] = total[:, :cols].astype(half)
        output_ref[:, j * size // SHARDS : (j + 1) * size // SHARDS] = total[:, cols:]
        owners_ref[OWNERS[0], j] = total.astype(half)
        owners_ref[OWNERS[2], j] = both[:, :size]
        owners_ref[OWNERS[3], j] = both[:, size:]
    owners_ref[OWNERS[1], 0] = output_ref[...].astype(half)
    owners_ref[OWNERS[1], 1:] = jnp.zeros(owners_ref.shape[1:], half)[1:]


def owned_kernel(where_ref, grads_ref, strips_ref, *refs):
    single = jnp.float32
    moments, out_ref, strips_out = refs[:4], refs[4], refs[5]
    strips_out[...] = strips_ref[...]
    place = where_ref[2]
    size = grads_ref.shape[3]
    part = size // SHARDS

    def write(f, owner, grad):
        cols, strip = grad.shape[1], grad.shape[0]
        both = moments[f ^ owner][part:].astype(single)
        moment = jnp.concatenate([both[:strip], both[strip:]], axis=1)[:, :cols]
        nest = grad + mom_rate * (mom_rate * moment + grad)
        out_ref[f, :, :cols] = nest.astype(out_ref.dtype)
        if cols < out_ref.shape[2]:
            rest = (out_ref.shape[1], out_ref.shape[2] - cols)
            out_ref[f, :, cols:] = jnp.zeros(rest, out_ref.dtype)

    @pl.when(place == OWNERS[0])
    def _():
        for f in range(SHARDS):
            pieces = [
                grads_ref[j, f][:, t * part : (t + 1) * part].astype(single)
                for t in range(3)
                for j in range(SHARDS)
            ]
            write(f, OWNERS[0], jnp.concatenate(pieces, axis=1))

    @pl.when(place == OWNERS[1])
    def _():
        for f in range(SHARDS):
            write(f, OWNERS[1], grads_ref[f, 0].astype(single))

    for owner in OWNERS[2:]:

        @pl.when(place == owner)
        def _():
            for f in range(SHARDS):
                pieces = [grads_ref[j, f].astype(single) for j in range(SHARDS)]
                write(f, owner, jnp.concatenate(pieces, axis=1))


def grads_kernel(where_ref, strips_ref, output_ref, out_ref):
    size = output_ref.shape[1]
    part = size // SHARDS
    pieces = [
        strips_ref[f][:, 2 * size + t * part : 2 * size + (t + 1) * part].astype(jnp.float32)
        for t in range(3)
        for f in range(SHARDS)
    ]
    out_ref[...] = jnp.concatenate(
        pieces
        + [output_ref[...]]
        + [
            strips_ref[f][:, i * size : (i + 1) * size].astype(jnp.float32)
            for i in range(2)
            for f in range(SHARDS)
        ],
        axis=1,
    ).astype(jnp.bfloat16)


NEWTON_SIZE = 256
NEWTON_CHUNK = 768


def newton_mixing(x_ref, gram_ref, mix_ref):
    single, half = jnp.float32, jnp.bfloat16
    blocks = x_ref.shape[0] // NEWTON_SIZE
    cuts = [slice(i * NEWTON_SIZE, (i + 1) * NEWTON_SIZE) for i in range(blocks)]
    pairs = [(cuts[i], cuts[j]) for i in range(blocks) for j in range(i, blocks)]
    for here, there in pairs:
        gram = lax.dot_general(x_ref[here], x_ref[there], NT, preferred_element_type=single)
        gram_ref[here, there] = gram.astype(half)
        if here != there:
            gram_ref[there, here] = jnp.transpose(gram).astype(half)
    for here, there in pairs:
        square = jnp.dot(gram_ref[here], gram_ref[:, there], preferred_element_type=single)
        mix = schulz_coeffs[1] * gram_ref[here, there].astype(single) + schulz_coeffs[2] * square
        mix_ref[here, there] = mix.astype(half)
        if here != there:
            mix_ref[there, here] = jnp.transpose(mix).astype(half)


def newton_applied(x_ref, mix_ref, at):
    x = x_ref[:, at : at + NEWTON_CHUNK]
    return schulz_coeffs[0] * x.astype(jnp.float32) + jnp.dot(
        mix_ref[...], x, preferred_element_type=jnp.float32
    )


def newton_kernel(where_ref, *refs):
    single, half = jnp.float32, jnp.bfloat16
    pieces, x_ref, gram_ref, mix_ref = refs[:CTX], *refs[CTX:]
    cols = x_ref.shape[1]
    tall = SHARDS * pieces[0].shape[1]
    total = jnp.zeros((1, 1), single)
    for piece in pieces:
        value = piece[...].astype(single)
        total += jnp.sum(jnp.sum(value * value, axis=0), keepdims=True)
    factor = 1.0 / (jnp.sqrt(total) + 1e-07)
    for c in range(CTX):
        value = pieces[c][...].astype(single).reshape(tall, cols)
        x_ref[c * tall : (c + 1) * tall] = (value * factor).astype(half)

    @pl.loop(0, NS_ITERS - 1)
    def _(step):
        newton_mixing(x_ref, gram_ref, mix_ref)
        for at in range(0, cols, NEWTON_CHUNK):
            x_ref[:, at : at + NEWTON_CHUNK] = newton_applied(x_ref, mix_ref, at).astype(half)


def last_newton_kernel(where_ref, x_ref, sums_ref, out_ref, sums_out, gram_ref, mix_ref):
    sums_out[...] = sums_ref[...]
    newton_mixing(x_ref, gram_ref, mix_ref)
    strip = out_ref.shape[2]
    for at in range(0, x_ref.shape[1], NEWTON_CHUNK):
        x = newton_applied(x_ref, mix_ref, at)
        for c in range(CTX):
            for k in range(SHARDS):
                start = (c * SHARDS + k) * strip
                out_ref[k, c, :, at : at + NEWTON_CHUNK] = x[start : start + strip].astype(
                    jnp.bfloat16
                )


def newton(pieces, sums, where, earlier, between):
    strip, cols = pieces[0].shape[1:]
    n = CTX * SHARDS * strip
    half = jnp.bfloat16
    scratch = [pltpu.VMEM((n, n), half), pltpu.VMEM((n, n), half)]
    [x] = call(
        newton_kernel, [((n, cols), half)], list(pieces), where, "newton", 36.0, scratch, earlier
    )
    return call(
        last_newton_kernel,
        [((SHARDS, CTX, strip, cols), half), (sums.shape, sums.dtype)],
        [x, sums],
        where,
        "last_newton",
        9.0,
        scratch,
        between,
    )


def attention_kernel(where_ref, recv_ref, place_row_ref, place_col_ref, place_half_ref, out_ref):
    single, half = jnp.float32, jnp.bfloat16
    scale = 1.0 / math.sqrt(HD)
    rows = 128
    length = CTX * rows
    place_row = place_row_ref[...]

    def run(query, keys, values, outer, places, step):
        key_sum = jnp.zeros((length, HD), single)
        value_sum = jnp.zeros((length, HD), single)
        mixed_all, query_all = [], []
        for at in range(0, query.shape[0], step):
            one = query[at : at + step]
            back = outer[at : at + step]
            score = (
                lax.dot_general(one, keys, (((1,), (1,)), ((), ())), preferred_element_type=single)
                * scale
            )
            allowed = place_row <= places[at : at + step]
            score = jnp.where(allowed, score, neg_large)
            peak = jnp.max(score, axis=-1, keepdims=True)
            weights = jnp.where(allowed, jnp.exp(score - peak), 0.0)
            total = jnp.sum(weights, axis=-1, keepdims=True)
            prob = weights * (1.0 / total)
            prob_half = prob.astype(half)
            mixed = jnp.dot(prob_half, values, preferred_element_type=single).astype(half)
            delta = jnp.sum(
                back.astype(single) * mixed.astype(single), axis=-1, keepdims=True
            )
            prob_grad = lax.dot_general(
                back, values, (((1,), (1,)), ((), ())), preferred_element_type=single
            )
            score_delta = (prob * (prob_grad - delta)).astype(half)
            query_grad = jnp.dot(score_delta, keys, preferred_element_type=single) * scale
            key_sum += lax.dot_general(
                score_delta, one, (((0,), (0,)), ((), ())), preferred_element_type=single
            )
            value_sum += lax.dot_general(
                prob_half, back, (((0,), (0,)), ((), ())), preferred_element_type=single
            )
            mixed_all.append(mixed)
            query_all.append(query_grad.astype(half))
        return (
            jnp.concatenate(mixed_all, axis=0),
            jnp.concatenate(query_all, axis=0),
            (key_sum * scale).astype(half),
            value_sum.astype(half),
        )

    first = recv_ref[:, 0:128, :].reshape(length, 128)
    second = recv_ref[:, 128:256, :].reshape(length, 128)
    mixed, query_grad, key_grad, value_grad = run(
        first[:, :HD], first[:, HD:], second[:, :HD], second[:, HD:], place_col_ref[...], 256
    )
    out_ref[:, 0:128, :] = jnp.concatenate([mixed, query_grad], axis=1).reshape(CTX, rows, 128)
    out_ref[:, 128:256, :] = jnp.concatenate([key_grad, value_grad], axis=1).reshape(
        CTX, rows, 128
    )
    third = recv_ref[:, 256:384, :].reshape(length, 128)
    fourth = recv_ref[:, 384:448, :].reshape(length // 2, 128)
    mixed, query_grad, key_grad, value_grad = run(
        fourth[:, :HD], third[:, :HD], third[:, HD:], fourth[:, HD:], place_half_ref[...], 256
    )
    out_ref[:, 256:384, :] = jnp.concatenate([key_grad, value_grad], axis=1).reshape(
        CTX, rows, 128
    )
    out_ref[:, 384:448, :] = jnp.concatenate([mixed, query_grad], axis=1).reshape(
        CTX, rows // 2, 128
    )


def attention(recv, places, where, y, earlier):
    length = places.shape[0]
    halves = pick(places.reshape(CTX, Y_PLACES, length // CTX // Y_PLACES), y, 1).reshape(-1)
    [out] = call(
        attention_kernel,
        [(recv.shape, recv.dtype)],
        [recv, places[None, :], places[:, None], halves[:, None]],
        where,
        "attention",
        0.1,
        earlier=earlier,
    )
    return out


def moment_kernel(where_ref, grads_ref, *refs):
    at = 0
    for which in range(4):
        moment_ref, grad_out, moment_out = refs[which], refs[4 + which], refs[8 + which]
        cols = moment_ref.shape[1]
        grad = grads_ref[0, :, at : at + cols].astype(jnp.float32)
        grad_out[...] = grad
        moment_out[...] = mom_rate * moment_ref[...] + grad
        at += cols


def write_moments(grads, moments, ctx_place):
    rows = moments[0].shape[0] // CTX
    blocks = [pl.BlockSpec((rows, m.shape[1]), lambda i, where: (i, 0)) for m in moments]
    shapes = [jax.ShapeDtypeStruct(m.shape, m.dtype) for m in moments]
    out = pl.pallas_call(
        moment_kernel,
        grid_spec=pltpu.PrefetchScalarGridSpec(
            num_scalar_prefetch=1,
            grid=(CTX,),
            in_specs=[
                pl.BlockSpec((1,) + grads.shape[1:], lambda i, where: (i ^ where[0], 0, 0))
            ]
            + blocks,
            out_specs=blocks + blocks,
        ),
        out_shape=shapes + shapes,
        compiler_params=pltpu.CompilerParams(vmem_limit_bytes=32 * 1024 * 1024),
        cost_estimate=pl.CostEstimate(
            flops=0, bytes_accessed=int(100 * 3.6e6), transcendentals=0
        ),
        name="moments",
    )(ctx_place.reshape(1), grads, *moments)
    return out[:4], out[4:]


def weight_kernel(where_ref, *refs):
    for which in range(4):
        ortho_ref, weight_ref, out_ref = refs[which], refs[4 + which], refs[8 + which]
        cols = weight_ref.shape[1]
        rate = step_rates[which] * math.sqrt(cols)
        out_ref[...] = weight_ref[...] - rate * ortho_ref[0, 0, :, :cols].astype(jnp.float32)


def write_weights(ortho, weights, ctx_place):
    rows = weights[0].shape[0] // CTX
    blocks = [pl.BlockSpec((rows, w.shape[1]), lambda i, where: (i, 0)) for w in weights]

    def source(owner):
        return pl.BlockSpec(
            (1, 1) + ortho.shape[2:], lambda i, where: (owner, i ^ where[0], 0, 0)
        )

    return pl.pallas_call(
        weight_kernel,
        grid_spec=pltpu.PrefetchScalarGridSpec(
            num_scalar_prefetch=1,
            grid=(CTX,),
            in_specs=[source(owner) for owner in OWNERS] + blocks,
            out_specs=blocks,
        ),
        out_shape=[jax.ShapeDtypeStruct(w.shape, w.dtype) for w in weights],
        compiler_params=pltpu.CompilerParams(vmem_limit_bytes=32 * 1024 * 1024),
        name="weights",
    )(ctx_place.reshape(1), *[ortho] * 4, *weights)


def local_fast(
    residual_in,
    cotangent,
    group_order,
    gain_first,
    shift_first,
    gain_second,
    shift_second,
    heads_weight,
    heads_bias,
    output_weight,
    output_bias,
    up_weight,
    up_bias,
    down_weight,
    down_bias,
    heads_moment,
    output_moment,
    up_moment,
    down_moment,
):
    single = jnp.float32
    half = jnp.bfloat16
    ctx_place = lax.axis_index("ctx")
    shard_place = lax.axis_index("fsdp")
    y, z = ctx_place % Y_PLACES, ctx_place // Y_PLACES
    seqs, rows, width = residual_in.shape
    length = rows * CTX
    group = rows // 2
    part = width // SHARDS
    hidden = up_weight.shape[1]
    hidden_part = hidden // SHARDS
    strip = part // CTX

    where = jnp.stack([z, y, shard_place, ctx_place]).astype(jnp.int32)

    [packed] = call(
        pack_kernel,
        [((2 * rows + 16, width), half)],
        [residual_in[0], cotangent[0]]
        + [
            v[None]
            for v in (
                gain_first,
                shift_first,
                gain_second,
                shift_second,
                output_bias,
                down_bias,
                heads_bias,
            )
        ],
        where,
        "pack",
        0.1,
    )
    packs = [packed] + [swap(packed, "fsdp", k) for k in (1, 2)]
    packs.append(swap(packs[2], "fsdp", 1))
    [heads_split] = call(
        heads_split_kernel, [((SHARDS, part, 3 * part), half)], [heads_weight], where, "heads_split", 0.1
    )
    heads_block = exchange(heads_split).reshape(width, 3 * part)
    moments_all = (heads_moment, output_moment, up_moment, down_moment)
    weights_all = (heads_weight, output_weight, up_weight, down_weight)
    strip_moments = [None] * SHARDS
    for which in range(4):
        moment = lax.dynamic_slice_in_dim(moments_all[which], ctx_place * strip, strip, 0)
        strip_moments[OWNERS[which]] = jnp.pad(moment, ((0, 0), (0, hidden - moment.shape[1])))
    mlp_split = call(
        mlp_split_kernel,
        [((part + 2 * strip, 2 * hidden_part), half)] * SHARDS,
        [up_weight, down_weight, jnp.stack(strip_moments)],
        where,
        "mlp_split",
        0.1,
        earlier=[heads_block],
    )
    mlp_pieces = [mlp_split[0]] + [swap(mlp_split[k], "fsdp", k) for k in range(1, SHARDS)]
    output_block = output_weight.astype(half)
    vectors = sum(p[2 * rows :].astype(single) for p in packs)

    places = slot_places(group_order, 0, length, group)
    query_places = slot_places(group_order, ctx_place * rows, rows, group)
    cosine, sine = rotary_tables(query_places)
    none, rest = jnp.zeros((rows, ROT // 2), single), jnp.zeros((rows, HD - ROT), single)
    turn_cos, turn_high, turn_low = [
        jnp.tile(jnp.concatenate(t, axis=1), (1, 2 * part // HD))
        for t in ([cosine, cosine, rest + 1.0], [none, sine, rest], [-sine, none, rest])
    ]

    first_in, second_in, grad_half, payload, my_normed, inverse = call(
        pre_kernel,
        [
            ((SHARDS * rows, width), half),
            ((SHARDS * rows, width), half),
            ((SHARDS * rows, width), half),
            ((CTX, 3 * rows + rows // 2, 2 * HD), half),
            ((rows, width), single),
            ((rows, 128), single),
        ],
        list(packs) + [heads_block, output_block, turn_cos, turn_high, turn_low],
        where,
        "pre",
        0.1,
    )
    my_inverse = inverse[:, :1]
    sent = exchange(payload, "ctx")
    done = attention(sent, places, where, y, mlp_pieces[2:3])
    back = exchange(done, "ctx")

    mlp_send, mlp_keep, mlp_part, up_sum, second_part = call(
        mlp_kernel,
        [
            ((SHARDS, Z_PLACES, strip, 2 * hidden_part), half),
            ((SHARDS, Z_PLACES, strip, 2 * hidden_part), single),
            ((SHARDS * rows, width), single),
            ((1, hidden_part), single),
            ((SHARDS * rows, width), single),
        ],
        [second_in, grad_half, up_bias.astype(half).astype(single)[None]] + mlp_pieces,
        where,
        "mlp",
        0.1,
        [
            pltpu.VMEM((width, 2 * hidden_part), half),
            pltpu.VMEM((width, 2 * hidden_part), single),
        ],
    )
    mlp_came, mlp_sums = scatter_ctx(mlp_send, mlp_keep, where, "mlp_z")

    send, keep, heads_sum, mine, home = call(
        post_kernel,
        [
            ((SHARDS, Z_PLACES, strip, width), half),
            ((SHARDS, Z_PLACES, strip, width), single),
            ((1, 3 * part), single),
            ((3 * rows, width), single),
            ((SHARDS, 3 * rows, width), half),
        ],
        [back, first_in, grad_half, heads_block, output_block, mlp_part, second_part]
        + [turn_cos, turn_high, turn_low],
        where,
        "post",
        0.1,
        [
            pltpu.VMEM((SHARDS * rows, part), half),
            pltpu.VMEM((SHARDS * rows, 3 * part), half),
            pltpu.VMEM((width, width), single),
        ],
        [mlp_sums[0]],
    )
    _, heads_sums = scatter_ctx(send, keep, where, "heads_z")
    home = exchange(home)
    total = mine + jnp.sum(home.astype(single), axis=0)
    block_out = (
        residual_in[0].astype(single) + (total[:rows] + vectors[4] + vectors[5])
    ).astype(half)
    first_delta, second_delta = total[rows : 2 * rows], total[2 * rows :]
    input_grad = (
        cotangent[0]
        + norm_back(first_delta, my_normed, my_inverse, vectors[0])
        + norm_back(second_delta, my_normed, my_inverse, vectors[2])
    )

    heads_sum = lax.dynamic_update_slice(
        jnp.zeros((3, SHARDS, part), single),
        heads_sum.reshape(3, 1, part),
        (0, shard_place, 0),
    ).reshape(3 * width)
    up_sum = lax.dynamic_update_slice(
        jnp.zeros((hidden,), single), up_sum[0], (shard_place * hidden_part,)
    )
    sums = jnp.concatenate(
        [
            jnp.sum(first_delta * my_normed, axis=0),
            jnp.sum(first_delta, axis=0),
            jnp.sum(second_delta * my_normed, axis=0),
            jnp.sum(second_delta, axis=0),
            jnp.sum(cotangent[0], axis=0),
            heads_sum,
            up_sum,
        ]
    ).reshape(-1, 128)
    sums = sums + sum(swap(sums, "fsdp", k) for k in range(1, SHARDS))

    strips, owned, output_strip = call(
        strip_kernel,
        [
            ((SHARDS, strip, 2 * hidden_part + 3 * part), half),
            ((SHARDS, SHARDS, strip, width), half),
            ((strip, width), single),
        ],
        heads_sums + mlp_sums,
        where,
        "strip",
        0.1,
        earlier=[home],
    )
    owned, strips = call(
        owned_kernel,
        [((SHARDS, strip, hidden), half), (strips.shape, half)],
        [exchange(owned), strips] + mlp_pieces,
        where,
        "owned",
        0.1,
    )
    pieces = gather_y(gather_z(owned))
    [grads] = call(
        grads_kernel,
        [((strip, 4 * width + 2 * hidden), half)],
        [exchange(strips), output_strip],
        where,
        "grads",
        0.1,
        earlier=pieces[1:],
    )
    grads_along = gather_z(grads)

    sums = sums + swap(sums, "ctx", 1)
    ortho, sums = newton(pieces, sums, where, [grads], grads_along[1:])
    sums = sums + sum(swap(sums, "ctx", Y_PLACES * k) for k in range(1, Z_PLACES))
    sums = sums.reshape(-1)
    arrived = exchange(ortho)
    new_weights = write_weights(arrived, weights_all, ctx_place)
    full_grads, new_moments = write_moments(
        jnp.stack(gather_y(grads_along)), moments_all, ctx_place
    )
    pieces = [sums[i * width : (i + 1) * width] for i in range(5)]
    heads_total = sums[5 * width : 8 * width]
    up_total = sums[8 * width :]
    vector_values = (
        gain_first,
        shift_first,
        gain_second,
        shift_second,
        heads_bias,
        output_bias,
        up_bias,
        down_bias,
    )
    vector_grads = (
        pieces[0],
        pieces[1],
        pieces[2],
        pieces[3],
        heads_total,
        pieces[4],
        up_total,
        pieces[4],
    )
    grad_shards = []
    new_shards = []
    for which in range(8):
        size_here = vector_values[which].shape[0]
        whole_grad = vector_grads[which]
        shard = lax.dynamic_slice_in_dim(whole_grad, shard_place * size_here, size_here)
        grad_shards.append(shard)
        new_shards.append(
            vector_values[which]
            - vector_rate * shard * lax.rsqrt(jnp.mean(whole_grad * whole_grad) + norm_eps)
        )
    return (
        block_out[None],
        input_grad[None],
        grad_shards[0],
        grad_shards[1],
        grad_shards[2],
        grad_shards[3],
        full_grads[0],
        grad_shards[4],
        full_grads[1],
        grad_shards[5],
        full_grads[2],
        grad_shards[6],
        full_grads[3],
        grad_shards[7],
        new_shards[0],
        new_shards[1],
        new_shards[2],
        new_shards[3],
        new_weights[0],
        new_shards[4],
        new_weights[1],
        new_shards[5],
        new_weights[2],
        new_shards[6],
        new_weights[3],
        new_shards[7],
        new_moments[0],
        new_moments[1],
        new_moments[2],
        new_moments[3],
    )


def solution(mesh):
    in_specs = (
        P("fsdp", "ctx", None),
        P("fsdp", "ctx", None),
        P(),
        P("fsdp"),
        P("fsdp"),
        P("fsdp"),
        P("fsdp"),
        P("fsdp", None),
        P("fsdp"),
        P("fsdp", None),
        P("fsdp"),
        P("fsdp", None),
        P("fsdp"),
        P("fsdp", None),
        P("fsdp"),
        P("fsdp", None),
        P("fsdp", None),
        P("fsdp", None),
        P("fsdp", None),
    )
    out_specs = (
        P("fsdp", "ctx", None),
        P("fsdp", "ctx", None),
        P("fsdp"),
        P("fsdp"),
        P("fsdp"),
        P("fsdp"),
        P("fsdp", None),
        P("fsdp"),
        P("fsdp", None),
        P("fsdp"),
        P("fsdp", None),
        P("fsdp"),
        P("fsdp", None),
        P("fsdp"),
        P("fsdp"),
        P("fsdp"),
        P("fsdp"),
        P("fsdp"),
        P("fsdp", None),
        P("fsdp"),
        P("fsdp", None),
        P("fsdp"),
        P("fsdp", None),
        P("fsdp"),
        P("fsdp", None),
        P("fsdp"),
        P("fsdp", None),
        P("fsdp", None),
        P("fsdp", None),
        P("fsdp", None),
    )
    sizes = dict(mesh.shape)
    fits = sizes["ctx"] == 8 and sizes["fsdp"] == 4
    chosen = local_fast if fits else local_general
    return jax.shard_map(chosen, mesh=mesh, in_specs=in_specs, out_specs=out_specs, check_vma=False)
```

```python
import math

import jax
import jax.numpy as jnp
from jax import lax
from jax.experimental import pallas as pl
from jax.experimental.pallas import tpu as pltpu
from jax.sharding import PartitionSpec as P

HEADS = 12
HD = 64
ROT = 16
NS_ITERS = 5


mom_rate = 0.95
schulz_coeffs = (3.4445, -4.775, 2.0315)
step_rates = (0.04, 0.3, 0.04, 0.04)
vector_rate = 0.3
norm_eps = 1e-05
neg_large = -1e30


def broadcast(x, axis, root):
    mine = lax.axis_index(axis) == root
    return lax.psum(jnp.where(mine, x, jnp.zeros_like(x)), axis)


def layer_norm(inputs, gain, shift):
    average = jnp.mean(inputs, axis=-1, keepdims=True)
    centred = inputs - average
    variance = jnp.mean(centred * centred, axis=-1, keepdims=True)
    inverse = lax.rsqrt(variance + norm_eps)
    normed = centred * inverse
    return (normed, inverse, normed * gain + shift)


def norm_back(delta, normed, inverse, gain):
    scaled = delta * gain
    first = jnp.mean(scaled, axis=-1, keepdims=True)
    second = jnp.mean(scaled * normed, axis=-1, keepdims=True)
    return inverse * (scaled - first - normed * second)


def gelu_value(pre):
    return 0.5 * pre * (1.0 + lax.erf(pre / math.sqrt(2.0)))


def gelu_slope(pre):
    return 0.5 * (1.0 + lax.erf(pre / math.sqrt(2.0))) + pre * jnp.exp(
        -0.5 * pre * pre
    ) / math.sqrt(2.0 * math.pi)


def slot_places(group_order, first_row, count, group):
    positions = first_row + jnp.arange(count, dtype=jnp.int32)
    slots = positions // group
    table = jnp.arange(group_order.shape[0], dtype=jnp.int32)
    picked = jnp.sum(jnp.where(slots[:, None] == table[None, :], group_order[None, :], 0), axis=1)
    return picked * group + positions % group


def rotary_tables(places):
    halfway = ROT // 2
    rates = 10000.0 ** (-2.0 * jnp.arange(halfway, dtype=jnp.float32) / ROT)
    angle = places.astype(jnp.float32)[:, None] * rates[None, :]
    return (jnp.cos(angle), jnp.sin(angle))


def rotate(heads, cosine, sine, sign):
    halfway = ROT // 2
    first = heads[..., :halfway]
    second = heads[..., halfway:ROT]
    cosine = cosine[:, None, :]
    sine = sign * sine[:, None, :]
    return jnp.concatenate(
        [first * cosine - second * sine, second * cosine + first * sine, heads[..., ROT:]], axis=-1
    )


def local_general(
    residual_in,
    cotangent,
    group_order,
    gain_first,
    shift_first,
    gain_second,
    shift_second,
    heads_weight,
    heads_bias,
    output_weight,
    output_bias,
    up_weight,
    up_bias,
    down_weight,
    down_bias,
    heads_moment,
    output_moment,
    up_moment,
    down_moment,
):
    single = jnp.float32
    half = jnp.bfloat16
    ctx_count = lax.axis_size("ctx")
    shard_count = lax.axis_size("fsdp")
    ctx_place = lax.axis_index("ctx")
    shard_place = lax.axis_index("fsdp")
    seqs, rows, width = residual_in.shape
    length = rows * ctx_count
    group = rows // 2
    scale = 1.0 / math.sqrt(HD)
    query_places = slot_places(group_order, ctx_place * rows, rows, group)
    key_places = slot_places(group_order, 0, length, group)
    copies = (
        lax.all_gather(heads_weight.astype(half), "fsdp", axis=0, tiled=True),
        lax.all_gather(output_weight.astype(half), "fsdp", axis=0, tiled=True),
        lax.all_gather(up_weight.astype(half), "fsdp", axis=0, tiled=True),
        lax.all_gather(down_weight.astype(half), "fsdp", axis=0, tiled=True),
        lax.all_gather(gain_first.astype(half), "fsdp", axis=0, tiled=True),
        lax.all_gather(shift_first.astype(half), "fsdp", axis=0, tiled=True),
        lax.all_gather(gain_second.astype(half), "fsdp", axis=0, tiled=True),
        lax.all_gather(shift_second.astype(half), "fsdp", axis=0, tiled=True),
        lax.all_gather(heads_bias.astype(half), "fsdp", axis=0, tiled=True),
        lax.all_gather(output_bias.astype(half), "fsdp", axis=0, tiled=True),
        lax.all_gather(up_bias.astype(half), "fsdp", axis=0, tiled=True),
        lax.all_gather(down_bias.astype(half), "fsdp", axis=0, tiled=True),
    )
    heads_copy, output_copy, up_copy, down_copy = (copies[0], copies[1], copies[2], copies[3])
    gain_one, shift_one, gain_two, shift_two, heads_shift, output_shift, up_shift, down_shift = [
        piece.astype(single) for piece in copies[4:]
    ]
    inputs = residual_in.astype(single)
    first_hat, first_inv, first_norm = layer_norm(inputs, gain_one, shift_one)
    second_hat, second_inv, second_norm = layer_norm(inputs, gain_two, shift_two)
    first_in = first_norm.astype(half)
    second_in = second_norm.astype(half)
    projected = (
        jnp.einsum("std,de->ste", first_in, heads_copy, preferred_element_type=single) + heads_shift
    )
    cosine, sine = rotary_tables(query_places)
    split = projected.reshape(seqs, rows, 3, HEADS, HD)
    query = rotate(split[:, :, 0], cosine, sine, 1.0).astype(half)
    keys = rotate(split[:, :, 1], cosine, sine, 1.0).astype(half).reshape(seqs, rows, width)
    values = split[:, :, 2].astype(half).reshape(seqs, rows, width)
    peak = jnp.full((seqs, HEADS, rows), neg_large, single)
    key_piece = lax.all_gather(keys, "ctx", axis=1, tiled=True)
    value_piece = lax.all_gather(values, "ctx", axis=1, tiled=True)
    count = key_piece.shape[1]
    places = slot_places(group_order, jnp.int32(0), count, group)
    key_heads = key_piece.reshape(seqs, count, HEADS, HD)
    value_heads = value_piece.reshape(seqs, count, HEADS, HD)
    score = jnp.einsum("sqhd,skhd->shqk", query, key_heads, preferred_element_type=single) * scale
    allowed = (places[None, :] <= query_places[:, None])[None, None]
    new_peak = jnp.maximum(peak, jnp.max(jnp.where(allowed, score, neg_large), axis=-1))
    weights = jnp.where(allowed, jnp.exp(score - new_peak[..., None]), 0.0)
    total = jnp.sum(weights, axis=-1)
    mixed = jnp.einsum(
        "shqk,skhd->shqd", weights.astype(half), value_heads, preferred_element_type=single
    )
    state = (new_peak, total, mixed)
    peak, total, mixed = state
    lse = peak + jnp.log(total)
    attn = (
        jnp.transpose(mixed / total[..., None], (0, 2, 1, 3))
        .reshape(seqs, rows, width)
        .astype(half)
    )
    output_part = (
        jnp.einsum("std,de->ste", attn, output_copy, preferred_element_type=single) + output_shift
    )
    up_pre = jnp.einsum("std,df->stf", second_in, up_copy, preferred_element_type=single) + up_shift
    active = gelu_value(up_pre).astype(half)
    mlp_part = (
        jnp.einsum("stf,df->std", active, down_copy, preferred_element_type=single) + down_shift
    )
    block_out = (inputs + output_part + mlp_part).astype(half)
    grad_half = cotangent.astype(half)
    down_local = jnp.einsum("std,stf->df", grad_half, active, preferred_element_type=single)
    up_delta = jnp.einsum(
        "std,df->stf", grad_half, down_copy, preferred_element_type=single
    ) * gelu_slope(up_pre)
    up_half = up_delta.astype(half)
    up_local = jnp.einsum("std,stf->df", second_in, up_half, preferred_element_type=single)
    second_delta = jnp.einsum("stf,df->std", up_half, up_copy, preferred_element_type=single)
    output_local = jnp.einsum("std,ste->de", attn, grad_half, preferred_element_type=single)
    attn_delta = jnp.einsum(
        "ste,de->std", grad_half, output_copy, preferred_element_type=single
    ).astype(half)
    attn_heads = attn_delta.reshape(seqs, rows, HEADS, HD)
    delta = jnp.transpose(
        jnp.sum(
            attn_heads.astype(single) * attn.reshape(seqs, rows, HEADS, HD).astype(single), axis=-1
        ),
        (0, 2, 1),
    )
    every_key, every_value = (
        lax.all_gather(keys, "ctx", axis=1, tiled=True),
        lax.all_gather(values, "ctx", axis=1, tiled=True),
    )
    block = math.gcd(length, 512)
    count = length // block
    key_blocks = jnp.moveaxis(every_key.reshape(seqs, count, block, HEADS, HD), 1, 0)
    value_blocks = jnp.moveaxis(every_value.reshape(seqs, count, block, HEADS, HD), 1, 0)
    place_blocks = key_places.reshape(count, block)

    def back_block(query_grad, data):
        key_block, value_block, place_block = data
        score = (
            jnp.einsum("sqhd,skhd->shqk", query, key_block, preferred_element_type=single) * scale
        )
        allowed = (place_block[None, :] <= query_places[:, None])[None, None]
        prob = jnp.where(allowed, jnp.exp(score - lse[..., None]), 0.0)
        prob_half = prob.astype(half)
        prob_grad = jnp.einsum(
            "sqhd,skhd->shqk", attn_heads, value_block, preferred_element_type=single
        )
        score_delta = (prob * (prob_grad - delta[..., None])).astype(half)
        query_grad = (
            query_grad
            + jnp.einsum("shqk,skhd->sqhd", score_delta, key_block, preferred_element_type=single)
            * scale
        )
        key_grad = (
            jnp.einsum("shqk,sqhd->skhd", score_delta, query, preferred_element_type=single) * scale
        )
        value_grad = jnp.einsum(
            "shqk,sqhd->skhd", prob_half, attn_heads, preferred_element_type=single
        )
        joined = jnp.concatenate(
            [key_grad.reshape(seqs, block, width), value_grad.reshape(seqs, block, width)], axis=-1
        )
        return (query_grad, joined)

    query_grad, stacked = lax.scan(
        back_block,
        jnp.zeros((seqs, rows, HEADS, HD), single),
        (key_blocks, value_blocks, place_blocks),
    )
    key_grads = jnp.moveaxis(stacked, 0, 1).reshape(seqs, length, 2 * width)
    home = lax.psum_scatter(key_grads, "ctx", scatter_dimension=1, tiled=True)
    key_delta = rotate(home[..., :width].reshape(seqs, rows, HEADS, HD), cosine, sine, -1.0)
    query_delta = rotate(query_grad, cosine, sine, -1.0)
    heads_delta = jnp.concatenate(
        [
            query_delta.reshape(seqs, rows, width),
            key_delta.reshape(seqs, rows, width),
            home[..., width:],
        ],
        axis=-1,
    )
    heads_half = heads_delta.astype(half)
    heads_local = jnp.einsum("std,ste->de", first_in, heads_half, preferred_element_type=single)
    first_delta = jnp.einsum("ste,de->std", heads_half, heads_copy, preferred_element_type=single)
    input_grad = (
        cotangent
        + norm_back(first_delta, first_hat, first_inv, gain_one)
        + norm_back(second_delta, second_hat, second_inv, gain_two)
    )
    columns = (
        lax.psum_scatter(heads_local, "ctx", scatter_dimension=1, tiled=True),
        lax.psum_scatter(output_local, "ctx", scatter_dimension=1, tiled=True),
        lax.psum_scatter(up_local, "ctx", scatter_dimension=1, tiled=True),
        lax.psum_scatter(down_local, "ctx", scatter_dimension=1, tiled=True),
    )
    parts = (
        lax.psum_scatter(columns[0], "fsdp", scatter_dimension=0, tiled=True),
        lax.psum_scatter(columns[1], "fsdp", scatter_dimension=0, tiled=True),
        lax.psum_scatter(columns[2], "fsdp", scatter_dimension=0, tiled=True),
        lax.psum_scatter(columns[3], "fsdp", scatter_dimension=0, tiled=True),
    )
    full_grads = (
        lax.all_gather(parts[0], "ctx", axis=1, tiled=True),
        lax.all_gather(parts[1], "ctx", axis=1, tiled=True),
        lax.all_gather(parts[2], "ctx", axis=1, tiled=True),
        lax.all_gather(parts[3], "ctx", axis=1, tiled=True),
    )
    weights_all = (heads_weight, output_weight, up_weight, down_weight)
    moments_all = (heads_moment, output_moment, up_moment, down_moment)
    new_moments = []
    nest_blocks = []
    for which in range(4):
        moment = mom_rate * moments_all[which] + full_grads[which]
        nest = full_grads[which] + mom_rate * moment
        cols = nest.shape[1] // ctx_count
        new_moments.append(moment)
        nest_blocks.append(lax.dynamic_slice_in_dim(nest, ctx_place * cols, cols, 1))
    sums = lax.psum(
        (
            jnp.sum(first_delta * first_hat, axis=(0, 1)),
            jnp.sum(first_delta, axis=(0, 1)),
            jnp.sum(second_delta * second_hat, axis=(0, 1)),
            jnp.sum(second_delta, axis=(0, 1)),
            jnp.sum(heads_delta, axis=(0, 1)),
            jnp.sum(cotangent, axis=(0, 1)),
            jnp.sum(up_delta, axis=(0, 1)),
            jnp.sum(nest_blocks[0] * nest_blocks[0]),
            jnp.sum(nest_blocks[1] * nest_blocks[1]),
            jnp.sum(nest_blocks[2] * nest_blocks[2]),
            jnp.sum(nest_blocks[3] * nest_blocks[3]),
        ),
        ("ctx", "fsdp"),
    )
    gathered = (
        lax.all_gather(nest_blocks[0], "fsdp", axis=0, tiled=True),
        lax.all_gather(nest_blocks[1], "fsdp", axis=0, tiled=True),
        lax.all_gather(nest_blocks[2], "fsdp", axis=0, tiled=True),
        lax.all_gather(nest_blocks[3], "fsdp", axis=0, tiled=True),
    )
    widths = [piece.shape[1] for piece in gathered]
    widest = max(widths)
    owners = [which * shard_count // 4 for which in range(4)]
    selected = jnp.zeros((width, widest), single)
    square_sum = jnp.zeros((), single)
    for which in range(4):
        chosen = (shard_place == owners[which]).astype(single)
        selected = selected + chosen * jnp.pad(
            gathered[which], ((0, 0), (0, widest - widths[which]))
        )
        square_sum = square_sum + chosen * sums[7 + which]
    ortho = (selected / (jnp.sqrt(square_sum) + 1e-07)).astype(half)
    for turn in range(NS_ITERS):
        partial_value = jnp.einsum("rw,sw->rs", ortho, ortho, preferred_element_type=single)
        gram = lax.psum(partial_value.astype(jnp.bfloat16), "ctx").astype(jnp.float32).astype(half)
        mix = (
            schulz_coeffs[1] * gram.astype(single)
            + schulz_coeffs[2] * jnp.dot(gram, gram, preferred_element_type=single)
        ).astype(half)
        ortho = (
            schulz_coeffs[0] * ortho.astype(single)
            + jnp.dot(mix, ortho, preferred_element_type=single)
        ).astype(half)
    shard_rows = width // shard_count
    updated = []
    for which in range(4):
        received = broadcast(ortho, "fsdp", owners[which])
        piece = lax.dynamic_slice(
            received, (shard_place * shard_rows, 0), (shard_rows, widths[which])
        )
        total_cols = weights_all[which].shape[1]
        current = lax.dynamic_slice_in_dim(
            weights_all[which], ctx_place * widths[which], widths[which], 1
        )
        updated.append(current - step_rates[which] * math.sqrt(total_cols) * piece.astype(single))
    new_weights = (
        lax.all_gather(updated[0], "ctx", axis=1, tiled=True),
        lax.all_gather(updated[1], "ctx", axis=1, tiled=True),
        lax.all_gather(updated[2], "ctx", axis=1, tiled=True),
        lax.all_gather(updated[3], "ctx", axis=1, tiled=True),
    )
    vector_values = (
        gain_first,
        shift_first,
        gain_second,
        shift_second,
        heads_bias,
        output_bias,
        up_bias,
        down_bias,
    )
    vector_grads = (sums[0], sums[1], sums[2], sums[3], sums[4], sums[5], sums[6], sums[5])
    grad_shards = []
    new_shards = []
    for which in range(8):
        size_here = vector_values[which].shape[0]
        whole_grad = vector_grads[which]
        shard = lax.dynamic_slice_in_dim(whole_grad, shard_place * size_here, size_here)
        grad_shards.append(shard)
        new_shards.append(
            vector_values[which]
            - vector_rate * shard * lax.rsqrt(jnp.mean(whole_grad * whole_grad) + norm_eps)
        )
    return (
        block_out,
        input_grad,
        grad_shards[0],
        grad_shards[1],
        grad_shards[2],
        grad_shards[3],
        full_grads[0],
        grad_shards[4],
        full_grads[1],
        grad_shards[5],
        full_grads[2],
        grad_shards[6],
        full_grads[3],
        grad_shards[7],
        new_shards[0],
        new_shards[1],
        new_shards[2],
        new_shards[3],
        new_weights[0],
        new_shards[4],
        new_weights[1],
        new_shards[5],
        new_weights[2],
        new_shards[6],
        new_weights[3],
        new_shards[7],
        new_moments[0],
        new_moments[1],
        new_moments[2],
        new_moments[3],
    )


Y_PLACES = 2
Z_PLACES = 4
CTX = Y_PLACES * Z_PLACES
SHARDS = 4


OWNERS = (0, 2, 1, 3)


def swap(x, axis, offset):
    count = lax.axis_size(axis)
    return lax.ppermute(x, axis, [(i, i ^ offset) for i in range(count)])


def exchange(x, axis="fsdp"):
    return lax.all_to_all(x, axis, 0, 0)


def pick(x, index, dim=0):
    return lax.dynamic_index_in_dim(x, index, dim, keepdims=False)


def gather_z(x):
    return [x] + [swap(x, "ctx", Y_PLACES * k) for k in range(1, Z_PLACES)]


def gather_y(along):
    pieces = []
    for piece in along:
        pieces += [piece, swap(piece, "ctx", 1)]
    return pieces


def call(kernel, outs, args, prefetch, name, cost, scratch=(), earlier=()):
    whole = pl.BlockSpec(memory_space=pltpu.VMEM)
    count = 1 + len(args)

    def body(*refs):
        kernel(*refs[:count], *refs[count + len(earlier) :])

    return pl.pallas_call(
        body,
        in_specs=[pl.BlockSpec(memory_space=pltpu.SMEM)]
        + [whole] * len(args)
        + [pl.BlockSpec(memory_space=pl.ANY)] * len(earlier),
        out_specs=[whole] * len(outs),
        out_shape=[jax.ShapeDtypeStruct(shape, dtype) for shape, dtype in outs],
        scratch_shapes=list(scratch),
        compiler_params=pltpu.CompilerParams(vmem_limit_bytes=50 * 1024 * 1024),
        cost_estimate=pl.CostEstimate(
            flops=0, bytes_accessed=int(cost * 3.6e6), transcendentals=0
        ),
        name=name,
    )(prefetch, *args, *earlier)


NT = (((1,), (1,)), ((), ()))
TN = (((0,), (0,)), ((), ()))


def pack_kernel(where_ref, residual_ref, grad_ref, *refs):
    half = jnp.bfloat16
    vectors_ref, out_ref = refs
    place = where_ref[2]
    rows, width = residual_ref.shape
    part = width // SHARDS

    def share(start, size):
        lane = lax.broadcasted_iota(jnp.int32, (1, SHARDS * size), 1)
        mine = jnp.logical_and(lane >= place * size, lane < (place + 1) * size)
        piece = vectors_ref[:, start : start + size]
        return jnp.where(mine, jnp.concatenate([piece] * SHARDS, axis=1), 0.0)

    heads = share(6 * part, 3 * part)
    out_ref[:rows] = residual_ref[...]
    out_ref[rows : 2 * rows] = grad_ref[...].astype(half)
    small = [share(i * part, part) for i in range(6)]
    small += [heads[:, t * width : (t + 1) * width] for t in range(3)]
    small.append(jnp.zeros((16 - len(small), width), jnp.float32))
    out_ref[2 * rows :] = jnp.concatenate(small, axis=0).astype(half)


def heads_split_kernel(where_ref, weight_ref, out_ref):
    part, width = weight_ref.shape[0], weight_ref.shape[1] // 3
    for dest in range(SHARDS):
        out_ref[dest] = jnp.concatenate(
            [
                weight_ref[:, t * width + dest * part : t * width + (dest + 1) * part]
                for t in range(3)
            ],
            axis=1,
        ).astype(jnp.bfloat16)


def mlp_split_kernel(where_ref, up_ref, down_ref, moments_ref, *outs):
    place = where_ref[2]
    part, cols = up_ref.shape[0], up_ref.shape[1] // SHARDS
    for k in range(SHARDS):
        cut = pl.ds(pl.multiple_of((place ^ k) * cols, cols), cols)
        outs[k][:part, :cols] = up_ref[:, cut].astype(jnp.bfloat16)
        outs[k][:part, cols:] = down_ref[:, cut].astype(jnp.bfloat16)
        moment = moments_ref[place ^ k]
        outs[k][part:] = jnp.concatenate(
            [moment[:, : 2 * cols], moment[:, 2 * cols :]], axis=0
        ).astype(jnp.bfloat16)


def turn(x, cos_ref, high_ref, low_ref, direction):
    lanes = x.shape[1]
    moved = pltpu.roll(x, ROT // 2, 1) * high_ref[...] + pltpu.roll(
        x, lanes - ROT // 2, 1
    ) * low_ref[...]
    return x * cos_ref[...] + direction * moved


def pre_kernel(where_ref, *refs):
    single, half = jnp.float32, jnp.bfloat16
    packs, block_ref = refs[:4], refs[4]
    output_ref, cos_ref, high_ref, low_ref = refs[5:9]
    first_ref, second_ref, grad_ref, payload_ref, normed_ref, inverse_ref = refs[9:]
    place = where_ref[2]
    part = output_ref.shape[0]
    rows = normed_ref.shape[0]
    vectors = sum(p[2 * rows :].astype(single) for p in packs)
    for r in range(SHARDS):
        x = packs[r][:rows].astype(single)
        average = jnp.mean(x, axis=-1, keepdims=True)
        centred = x - average
        variance = jnp.mean(centred * centred, axis=-1, keepdims=True)
        inverse = lax.rsqrt(variance + norm_eps)
        normed = centred * inverse
        if r == 0:
            normed_ref[...] = normed
            inverse_ref[...] = jnp.broadcast_to(inverse, inverse_ref.shape)
        cut = slice(r * rows, (r + 1) * rows)
        first_ref[cut] = (normed * vectors[0:1] + vectors[1:2]).astype(half)
        second_ref[cut] = (normed * vectors[2:3] + vectors[3:4]).astype(half)
        grad_ref[cut] = packs[r][rows : 2 * rows]
    shift = jnp.concatenate(
        [
            sum(
                jnp.where(place == j, vectors[6 + t : 7 + t, j * part : (j + 1) * part], 0.0)
                for j in range(SHARDS)
            )
            for t in range(3)
        ],
        axis=1,
    )
    projected = jnp.dot(first_ref[...], block_ref[...], preferred_element_type=single) + shift
    outer = lax.dot_general(
        grad_ref[...], output_ref[...], NT, preferred_element_type=single
    ).astype(half)
    for r in range(SHARDS):
        cut = slice(r * rows, (r + 1) * rows)
        turned = turn(projected[cut, : 2 * part], cos_ref, high_ref, low_ref, 1.0).astype(half)
        values = projected[cut, 2 * part :].astype(half)
        back = outer[cut]

        def head(x, h):
            return x[:, h * HD : (h + 1) * HD]

        last = 3 * Z_PLACES // 4 - 1
        shared = jnp.concatenate([head(turned, 3 + last), head(values, last)], axis=1)
        query = jnp.concatenate([head(turned, last), head(back, last)], axis=1)
        for y in range(Y_PLACES):
            at = r * Y_PLACES + y
            payload_ref[at, :rows] = jnp.concatenate([head(turned, y), head(turned, 3 + y)], axis=1)
            payload_ref[at, rows : 2 * rows] = jnp.concatenate(
                [head(values, y), head(back, y)], axis=1
            )
            payload_ref[at, 2 * rows : 3 * rows] = shared
            payload_ref[at, 3 * rows :] = query[y * rows // 2 : (y + 1) * rows // 2]


def write_strips(grad_ref, send_ref, keep_ref, y):
    strip = send_ref.shape[2]
    for f in range(SHARDS):
        for z in range(Z_PLACES):
            start = (f * CTX + z * Y_PLACES) * strip
            mine = pl.multiple_of(start + y * strip, 8)
            other = pl.multiple_of(start + (1 - y) * strip, 8)
            keep_ref[f, z] = grad_ref[pl.ds(mine, strip), :]
            send_ref[f, z] = grad_ref[pl.ds(other, strip), :].astype(jnp.bfloat16)


def mlp_kernel(where_ref, *refs):
    single, half = jnp.float32, jnp.bfloat16
    second_ref, grad_ref, shift_ref = refs[:3]
    pieces = refs[3:7]
    send_ref, keep_ref, out_ref, sum_ref, back_ref, block_ref, local_ref = refs[7:]
    y, place = where_ref[1], where_ref[2]
    cols = shift_ref.shape[1]
    part = block_ref.shape[0] // SHARDS
    for k in range(SHARDS):
        block_ref[pl.ds(pl.multiple_of((place ^ k) * part, part), part), :] = pieces[k][:part]
    second, grad = second_ref[...], grad_ref[...]
    up = block_ref[:, :cols]
    down = block_ref[:, cols:]
    pre = jnp.dot(second, up, preferred_element_type=single) + shift_ref[...]
    cdf = 0.5 * (1.0 + lax.erf(pre * (1.0 / math.sqrt(2.0))))
    active = (pre * cdf).astype(half)
    slope = cdf + pre * jnp.exp(-0.5 * pre * pre) * (1.0 / math.sqrt(2.0 * math.pi))
    delta = jnp.dot(grad, down, preferred_element_type=single) * slope
    sum_ref[...] = jnp.sum(delta, axis=0, keepdims=True)
    delta_half = delta.astype(half)
    local_ref[:, :cols] = lax.dot_general(second, delta_half, TN, preferred_element_type=single)
    local_ref[:, cols:] = lax.dot_general(grad, active, TN, preferred_element_type=single)
    write_strips(local_ref, send_ref, keep_ref, y)
    out_ref[...] = lax.dot_general(active, down, NT, preferred_element_type=single)
    back_ref[...] = lax.dot_general(delta_half, up, NT, preferred_element_type=single)


def post_kernel(where_ref, *refs):
    single, half = jnp.float32, jnp.bfloat16
    back_ref, first_ref, grad_ref, block_ref, output_ref, mlp_ref, second_ref = refs[:7]
    cos_ref, high_ref, low_ref = refs[7:10]
    send_ref, keep_ref, sum_ref, mine_ref, home_ref = refs[10:15]
    attn_ref, heads_ref, local_ref = refs[15:]
    y, place = where_ref[1], where_ref[2]
    part, width = output_ref.shape
    rows = mine_ref.shape[0] // 3
    sums = jnp.zeros((1, 3 * part), single)
    for r in range(SHARDS):
        cut = slice(r * rows, (r + 1) * rows)
        early = [back_ref[r * Y_PLACES + i, :rows] for i in range(Y_PLACES)]
        early.append(
            jnp.concatenate([back_ref[r * Y_PLACES + i, 3 * rows :] for i in range(Y_PLACES)], axis=0)
        )
        late = [back_ref[r * Y_PLACES + i, rows : 2 * rows].astype(single) for i in range(Y_PLACES)]
        late.append(
            sum(back_ref[r * Y_PLACES + i, 2 * rows : 3 * rows].astype(single) for i in range(Y_PLACES))
        )
        attn_ref[cut] = jnp.concatenate([x[:, :HD] for x in early], axis=1)
        turned = turn(
            jnp.concatenate(
                [x[:, HD:].astype(single) for x in early] + [x[:, :HD] for x in late], axis=1
            ),
            cos_ref,
            high_ref,
            low_ref,
            -1.0,
        )
        whole = jnp.concatenate([turned] + [x[:, HD:] for x in late], axis=1)
        sums += jnp.sum(whole, axis=0, keepdims=True)
        heads_ref[cut] = whole.astype(half)
    sum_ref[...] = sums
    local_ref[:, : 3 * part] = lax.dot_general(
        first_ref[...], heads_ref[...], TN, preferred_element_type=single
    )
    output_local = lax.dot_general(
        attn_ref[...], grad_ref[...], TN, preferred_element_type=single
    )
    for j in range(SHARDS):
        local_ref[j * part : (j + 1) * part, 3 * part :] = output_local[:, j * part : (j + 1) * part]
    write_strips(local_ref, send_ref, keep_ref, y)
    out = jnp.dot(attn_ref[...], output_ref[...], preferred_element_type=single) + mlp_ref[...]
    first = lax.dot_general(heads_ref[...], block_ref[...], NT, preferred_element_type=single)
    for i, value in enumerate((out, first, second_ref[...])):
        cut = slice(i * rows, (i + 1) * rows)
        mine_ref[cut] = value[:rows]
        home_ref[place, cut] = jnp.zeros((rows, width), half)
        for k in range(1, SHARDS):
            home_ref[place ^ k, cut] = value[k * rows : (k + 1) * rows].astype(half)


def along_z_kernel(where_ref, keep_ref, came_ref, own_ref, *sends):
    z = where_ref[0]
    own_ref[...] = keep_ref[:, z] + came_ref[:, z].astype(jnp.float32)
    for k in range(1, Z_PLACES):
        sends[k - 1][...] = (keep_ref[:, z ^ k] + came_ref[:, z ^ k].astype(jnp.float32)).astype(
            jnp.bfloat16
        )


def scatter_ctx(send, keep, where, name, *earlier):
    single, half = jnp.float32, jnp.bfloat16
    came = swap(send, "ctx", 1)
    shape = (keep.shape[0],) + keep.shape[2:]
    own, *sends = call(
        along_z_kernel,
        [(shape, single)] + [(shape, half)] * (Z_PLACES - 1),
        [keep, came],
        where,
        name,
        0.1,
        earlier=earlier,
    )
    return came, [own] + [swap(sends[k - 1], "ctx", 2 * k) for k in range(1, Z_PLACES)]


def strip_sum(parts, index):
    return parts[0][index] + sum(p[index].astype(jnp.float32) for p in parts[1:])


def strip_kernel(where_ref, *refs):
    half = jnp.bfloat16
    heads, mlp = refs[:4], refs[4:8]
    strips_ref, owners_ref, output_ref = refs[8:]
    size = owners_ref.shape[3]
    cols = 3 * size // 4
    for j in range(SHARDS):
        total = strip_sum(heads, j)
        both = strip_sum(mlp, j).astype(half)
        strips_ref[j, :, : 2 * size] = both
        strips_ref[j, :, 2 * size :] = total[:, :cols].astype(half)
        output_ref[:, j * size // SHARDS : (j + 1) * size // SHARDS] = total[:, cols:]
        owners_ref[OWNERS[0], j] = total.astype(half)
        owners_ref[OWNERS[2], j] = both[:, :size]
        owners_ref[OWNERS[3], j] = both[:, size:]
    owners_ref[OWNERS[1], 0] = output_ref[...].astype(half)
    owners_ref[OWNERS[1], 1:] = jnp.zeros(owners_ref.shape[1:], half)[1:]


def owned_kernel(where_ref, grads_ref, strips_ref, *refs):
    single = jnp.float32
    moments, out_ref, strips_out = refs[:4], refs[4], refs[5]
    strips_out[...] = strips_ref[...]
    place = where_ref[2]
    size = grads_ref.shape[3]
    part = size // SHARDS

    def write(f, owner, grad):
        cols, strip = grad.shape[1], grad.shape[0]
        both = moments[f ^ owner][part:].astype(single)
        moment = jnp.concatenate([both[:strip], both[strip:]], axis=1)[:, :cols]
        nest = grad + mom_rate * (mom_rate * moment + grad)
        out_ref[f, :, :cols] = nest.astype(out_ref.dtype)
        if cols < out_ref.shape[2]:
            rest = (out_ref.shape[1], out_ref.shape[2] - cols)
            out_ref[f, :, cols:] = jnp.zeros(rest, out_ref.dtype)

    @pl.when(place == OWNERS[0])
    def _():
        for f in range(SHARDS):
            pieces = [
                grads_ref[j, f][:, t * part : (t + 1) * part].astype(single)
                for t in range(3)
                for j in range(SHARDS)
            ]
            write(f, OWNERS[0], jnp.concatenate(pieces, axis=1))

    @pl.when(place == OWNERS[1])
    def _():
        for f in range(SHARDS):
            write(f, OWNERS[1], grads_ref[f, 0].astype(single))

    for owner in OWNERS[2:]:

        @pl.when(place == owner)
        def _():
            for f in range(SHARDS):
                pieces = [grads_ref[j, f].astype(single) for j in range(SHARDS)]
                write(f, owner, jnp.concatenate(pieces, axis=1))


def copy_kernel(where_ref, x_ref, out_ref):
    out_ref[...] = x_ref[...]


def grads_kernel(where_ref, strips_ref, output_ref, sums_ref, out_ref, sums_out):
    sums_out[...] = sums_ref[...]
    size = output_ref.shape[1]
    part = size // SHARDS
    pieces = [
        strips_ref[f][:, 2 * size + t * part : 2 * size + (t + 1) * part].astype(jnp.float32)
        for t in range(3)
        for f in range(SHARDS)
    ]
    out_ref[...] = jnp.concatenate(
        pieces
        + [output_ref[...]]
        + [
            strips_ref[f][:, i * size : (i + 1) * size].astype(jnp.float32)
            for i in range(2)
            for f in range(SHARDS)
        ],
        axis=1,
    ).astype(jnp.bfloat16)


NEWTON_SIZE = 256
NEWTON_CHUNK = 768


def newton_mixing(x_ref, gram_ref, mix_ref):
    single, half = jnp.float32, jnp.bfloat16
    blocks = x_ref.shape[0] // NEWTON_SIZE
    cuts = [slice(i * NEWTON_SIZE, (i + 1) * NEWTON_SIZE) for i in range(blocks)]
    pairs = [(cuts[i], cuts[j]) for i in range(blocks) for j in range(i, blocks)]
    for here, there in pairs:
        gram = lax.dot_general(x_ref[here], x_ref[there], NT, preferred_element_type=single)
        gram_ref[here, there] = gram.astype(half)
        if here != there:
            gram_ref[there, here] = jnp.transpose(gram).astype(half)
    for here, there in pairs:
        square = jnp.dot(gram_ref[here], gram_ref[:, there], preferred_element_type=single)
        mix = schulz_coeffs[1] * gram_ref[here, there].astype(single) + schulz_coeffs[2] * square
        mix_ref[here, there] = mix.astype(half)
        if here != there:
            mix_ref[there, here] = jnp.transpose(mix).astype(half)


def newton_applied(x_ref, mix_ref, at):
    x = x_ref[:, at : at + NEWTON_CHUNK]
    return schulz_coeffs[0] * x.astype(jnp.float32) + jnp.dot(
        mix_ref[...], x, preferred_element_type=jnp.float32
    )


def newton_kernel(where_ref, *refs):
    single, half = jnp.float32, jnp.bfloat16
    pieces, x_ref, gram_ref, mix_ref = refs[:CTX], *refs[CTX:]
    cols = x_ref.shape[1]
    tall = SHARDS * pieces[0].shape[1]
    total = jnp.zeros((1, 1), single)
    for piece in pieces:
        value = piece[...].astype(single)
        total += jnp.sum(jnp.sum(value * value, axis=0), keepdims=True)
    factor = 1.0 / (jnp.sqrt(total) + 1e-07)
    for c in range(CTX):
        value = pieces[c][...].astype(single).reshape(tall, cols)
        x_ref[c * tall : (c + 1) * tall] = (value * factor).astype(half)

    @pl.loop(0, NS_ITERS - 1)
    def _(step):
        newton_mixing(x_ref, gram_ref, mix_ref)
        for at in range(0, cols, NEWTON_CHUNK):
            x_ref[:, at : at + NEWTON_CHUNK] = newton_applied(x_ref, mix_ref, at).astype(half)


def last_newton_kernel(where_ref, x_ref, sums_ref, out_ref, sums_out, gram_ref, mix_ref):
    sums_out[...] = sums_ref[...]
    newton_mixing(x_ref, gram_ref, mix_ref)
    strip = out_ref.shape[2]
    for at in range(0, x_ref.shape[1], NEWTON_CHUNK):
        x = newton_applied(x_ref, mix_ref, at)
        for c in range(CTX):
            for k in range(SHARDS):
                start = (c * SHARDS + k) * strip
                out_ref[k, c, :, at : at + NEWTON_CHUNK] = x[start : start + strip].astype(
                    jnp.bfloat16
                )


def newton(pieces, sums, where, earlier, between):
    strip, cols = pieces[0].shape[1:]
    n = CTX * SHARDS * strip
    half = jnp.bfloat16
    scratch = [pltpu.VMEM((n, n), half), pltpu.VMEM((n, n), half)]
    [x] = call(
        newton_kernel, [((n, cols), half)], list(pieces), where, "newton", 36.0, scratch, earlier
    )
    return call(
        last_newton_kernel,
        [((SHARDS, CTX, strip, cols), half), (sums.shape, sums.dtype)],
        [x, sums],
        where,
        "last_newton",
        9.0,
        scratch,
        between,
    )


def attention_kernel(where_ref, recv_ref, place_row_ref, place_col_ref, place_half_ref, out_ref):
    single, half = jnp.float32, jnp.bfloat16
    scale = 1.0 / math.sqrt(HD)
    rows = 128
    length = CTX * rows
    place_row = place_row_ref[...]

    def run(query, keys, values, outer, places, step):
        key_sum = jnp.zeros((length, HD), single)
        value_sum = jnp.zeros((length, HD), single)
        mixed_all, query_all = [], []
        for at in range(0, query.shape[0], step):
            one = query[at : at + step]
            back = outer[at : at + step]
            score = (
                lax.dot_general(one, keys, (((1,), (1,)), ((), ())), preferred_element_type=single)
                * scale
            )
            allowed = place_row <= places[at : at + step]
            score = jnp.where(allowed, score, neg_large)
            peak = jnp.max(score, axis=-1, keepdims=True)
            weights = jnp.where(allowed, jnp.exp(score - peak), 0.0)
            total = jnp.sum(weights, axis=-1, keepdims=True)
            prob = weights * (1.0 / total)
            prob_half = prob.astype(half)
            mixed = jnp.dot(prob_half, values, preferred_element_type=single).astype(half)
            delta = jnp.sum(
                back.astype(single) * mixed.astype(single), axis=-1, keepdims=True
            )
            prob_grad = lax.dot_general(
                back, values, (((1,), (1,)), ((), ())), preferred_element_type=single
            )
            score_delta = (prob * (prob_grad - delta)).astype(half)
            query_grad = jnp.dot(score_delta, keys, preferred_element_type=single) * scale
            key_sum += lax.dot_general(
                score_delta, one, (((0,), (0,)), ((), ())), preferred_element_type=single
            )
            value_sum += lax.dot_general(
                prob_half, back, (((0,), (0,)), ((), ())), preferred_element_type=single
            )
            mixed_all.append(mixed)
            query_all.append(query_grad.astype(half))
        return (
            jnp.concatenate(mixed_all, axis=0),
            jnp.concatenate(query_all, axis=0),
            (key_sum * scale).astype(half),
            value_sum.astype(half),
        )

    first = recv_ref[:, 0:128, :].reshape(length, 128)
    second = recv_ref[:, 128:256, :].reshape(length, 128)
    mixed, query_grad, key_grad, value_grad = run(
        first[:, :HD], first[:, HD:], second[:, :HD], second[:, HD:], place_col_ref[...], 256
    )
    out_ref[:, 0:128, :] = jnp.concatenate([mixed, query_grad], axis=1).reshape(CTX, rows, 128)
    out_ref[:, 128:256, :] = jnp.concatenate([key_grad, value_grad], axis=1).reshape(
        CTX, rows, 128
    )
    third = recv_ref[:, 256:384, :].reshape(length, 128)
    fourth = recv_ref[:, 384:448, :].reshape(length // 2, 128)
    mixed, query_grad, key_grad, value_grad = run(
        fourth[:, :HD], third[:, :HD], third[:, HD:], fourth[:, HD:], place_half_ref[...], 256
    )
    out_ref[:, 256:384, :] = jnp.concatenate([key_grad, value_grad], axis=1).reshape(
        CTX, rows, 128
    )
    out_ref[:, 384:448, :] = jnp.concatenate([mixed, query_grad], axis=1).reshape(
        CTX, rows // 2, 128
    )


def attention(recv, places, where, y, earlier):
    length = places.shape[0]
    halves = pick(places.reshape(CTX, Y_PLACES, length // CTX // Y_PLACES), y, 1).reshape(-1)
    [out] = call(
        attention_kernel,
        [(recv.shape, recv.dtype)],
        [recv, places[None, :], places[:, None], halves[:, None]],
        where,
        "attention",
        0.1,
        earlier=earlier,
    )
    return out


def moment_kernel(where_ref, grads_ref, *refs):
    at = 0
    for which in range(4):
        moment_ref, grad_out, moment_out = refs[which], refs[4 + which], refs[8 + which]
        cols = moment_ref.shape[1]
        grad = grads_ref[0, :, at : at + cols].astype(jnp.float32)
        grad_out[...] = grad
        moment_out[...] = mom_rate * moment_ref[...] + grad
        at += cols


def write_moments(grads, moments, ctx_place):
    rows = moments[0].shape[0] // CTX
    blocks = [pl.BlockSpec((rows, m.shape[1]), lambda i, where: (i, 0)) for m in moments]
    shapes = [jax.ShapeDtypeStruct(m.shape, m.dtype) for m in moments]
    out = pl.pallas_call(
        moment_kernel,
        grid_spec=pltpu.PrefetchScalarGridSpec(
            num_scalar_prefetch=1,
            grid=(CTX,),
            in_specs=[
                pl.BlockSpec((1,) + grads.shape[1:], lambda i, where: (i ^ where[0], 0, 0))
            ]
            + blocks,
            out_specs=blocks + blocks,
        ),
        out_shape=shapes + shapes,
        compiler_params=pltpu.CompilerParams(vmem_limit_bytes=60 * 1024 * 1024),
        cost_estimate=pl.CostEstimate(
            flops=0, bytes_accessed=int(100 * 3.6e6), transcendentals=0
        ),
        name="moments",
    )(ctx_place.reshape(1), grads, *moments)
    return out[:4], out[4:]


def weight_kernel(where_ref, *refs):
    for which in range(4):
        ortho_ref, weight_ref, out_ref = refs[which], refs[4 + which], refs[8 + which]
        cols = weight_ref.shape[1]
        rate = step_rates[which] * math.sqrt(cols)
        out_ref[...] = weight_ref[...] - rate * ortho_ref[0, 0, :, :cols].astype(jnp.float32)


def write_weights(ortho, weights, ctx_place):
    rows = weights[0].shape[0] // CTX
    blocks = [pl.BlockSpec((rows, w.shape[1]), lambda i, where: (i, 0)) for w in weights]

    def source(owner):
        return pl.BlockSpec(
            (1, 1) + ortho.shape[2:], lambda i, where: (owner, i ^ where[0], 0, 0)
        )

    return pl.pallas_call(
        weight_kernel,
        grid_spec=pltpu.PrefetchScalarGridSpec(
            num_scalar_prefetch=1,
            grid=(CTX,),
            in_specs=[source(owner) for owner in OWNERS] + blocks,
            out_specs=blocks,
        ),
        out_shape=[jax.ShapeDtypeStruct(w.shape, w.dtype) for w in weights],
        compiler_params=pltpu.CompilerParams(vmem_limit_bytes=60 * 1024 * 1024),
        name="weights",
    )(ctx_place.reshape(1), *[ortho] * 4, *weights)


def local_fast(
    residual_in,
    cotangent,
    group_order,
    gain_first,
    shift_first,
    gain_second,
    shift_second,
    heads_weight,
    heads_bias,
    output_weight,
    output_bias,
    up_weight,
    up_bias,
    down_weight,
    down_bias,
    heads_moment,
    output_moment,
    up_moment,
    down_moment,
):
    single = jnp.float32
    half = jnp.bfloat16
    ctx_place = lax.axis_index("ctx")
    shard_place = lax.axis_index("fsdp")
    y, z = ctx_place % Y_PLACES, ctx_place // Y_PLACES
    seqs, rows, width = residual_in.shape
    length = rows * CTX
    group = rows // 2
    part = width // SHARDS
    hidden = up_weight.shape[1]
    hidden_part = hidden // SHARDS
    strip = part // CTX

    where = jnp.stack([z, y, shard_place, ctx_place]).astype(jnp.int32)

    [packed] = call(
        pack_kernel,
        [((2 * rows + 16, width), half)],
        [
            residual_in[0],
            cotangent[0],
            jnp.concatenate(
                [
                    gain_first,
                    shift_first,
                    gain_second,
                    shift_second,
                    output_bias,
                    down_bias,
                    heads_bias,
                ]
            )[None],
        ],
        where,
        "pack",
        0.1,
    )
    packs = [packed] + [swap(packed, "fsdp", k) for k in (1, 2)]
    packs.append(swap(packs[2], "fsdp", 1))
    [heads_split] = call(
        heads_split_kernel, [((SHARDS, part, 3 * part), half)], [heads_weight], where, "heads_split", 0.1
    )
    heads_block = exchange(heads_split).reshape(width, 3 * part)
    moments_all = (heads_moment, output_moment, up_moment, down_moment)
    weights_all = (heads_weight, output_weight, up_weight, down_weight)
    strip_moments = [None] * SHARDS
    for which in range(4):
        moment = lax.dynamic_slice_in_dim(moments_all[which], ctx_place * strip, strip, 0)
        strip_moments[OWNERS[which]] = jnp.pad(moment, ((0, 0), (0, hidden - moment.shape[1])))
    mlp_split = call(
        mlp_split_kernel,
        [((part + 2 * strip, 2 * hidden_part), half)] * SHARDS,
        [up_weight, down_weight, jnp.stack(strip_moments)],
        where,
        "mlp_split",
        0.1,
        earlier=[packs[3]],
    )
    mlp_pieces = [mlp_split[0]] + [swap(mlp_split[k], "fsdp", k) for k in range(1, SHARDS)]
    output_block = output_weight.astype(half)
    vectors = sum(p[2 * rows :].astype(single) for p in packs)

    places = slot_places(group_order, 0, length, group)
    query_places = slot_places(group_order, ctx_place * rows, rows, group)
    cosine, sine = rotary_tables(query_places)
    none, rest = jnp.zeros((rows, ROT // 2), single), jnp.zeros((rows, HD - ROT), single)
    turn_cos, turn_high, turn_low = [
        jnp.tile(jnp.concatenate(t, axis=1), (1, 2 * part // HD))
        for t in ([cosine, cosine, rest + 1.0], [none, sine, rest], [-sine, none, rest])
    ]

    first_in, second_in, grad_half, payload, my_normed, inverse = call(
        pre_kernel,
        [
            ((SHARDS * rows, width), half),
            ((SHARDS * rows, width), half),
            ((SHARDS * rows, width), half),
            ((CTX, 3 * rows + rows // 2, 2 * HD), half),
            ((rows, width), single),
            ((rows, 128), single),
        ],
        list(packs) + [heads_block, output_block, turn_cos, turn_high, turn_low],
        where,
        "pre",
        0.1,
    )
    my_inverse = inverse[:, :1]
    sent = exchange(payload, "ctx")
    done = attention(sent, places, where, y, mlp_pieces[2:3])
    back = exchange(done, "ctx")

    mlp_send, mlp_keep, mlp_part, up_sum, second_part = call(
        mlp_kernel,
        [
            ((SHARDS, Z_PLACES, strip, 2 * hidden_part), half),
            ((SHARDS, Z_PLACES, strip, 2 * hidden_part), single),
            ((SHARDS * rows, width), single),
            ((1, hidden_part), single),
            ((SHARDS * rows, width), single),
        ],
        [second_in, grad_half, up_bias.astype(half).astype(single)[None]] + mlp_pieces,
        where,
        "mlp",
        0.1,
        [
            pltpu.VMEM((width, 2 * hidden_part), half),
            pltpu.VMEM((width, 2 * hidden_part), single),
        ],
    )
    mlp_came, mlp_sums = scatter_ctx(mlp_send, mlp_keep, where, "mlp_z")

    send, keep, heads_sum, mine, home = call(
        post_kernel,
        [
            ((SHARDS, Z_PLACES, strip, width), half),
            ((SHARDS, Z_PLACES, strip, width), single),
            ((1, 3 * part), single),
            ((3 * rows, width), single),
            ((SHARDS, 3 * rows, width), half),
        ],
        [back, first_in, grad_half, heads_block, output_block, mlp_part, second_part]
        + [turn_cos, turn_high, turn_low],
        where,
        "post",
        0.1,
        [
            pltpu.VMEM((SHARDS * rows, part), half),
            pltpu.VMEM((SHARDS * rows, 3 * part), half),
            pltpu.VMEM((width, width), single),
        ],
        [mlp_sums[0]],
    )
    _, heads_sums = scatter_ctx(send, keep, where, "heads_z")
    home = exchange(home)
    total = mine + jnp.sum(home.astype(single), axis=0)
    block_out = (
        residual_in[0].astype(single) + (total[:rows] + vectors[4] + vectors[5])
    ).astype(half)
    first_delta, second_delta = total[rows : 2 * rows], total[2 * rows :]
    input_grad = (
        cotangent[0]
        + norm_back(first_delta, my_normed, my_inverse, vectors[0])
        + norm_back(second_delta, my_normed, my_inverse, vectors[2])
    )

    heads_sum = lax.dynamic_update_slice(
        jnp.zeros((3, SHARDS, part), single),
        heads_sum.reshape(3, 1, part),
        (0, shard_place, 0),
    ).reshape(3 * width)
    up_sum = lax.dynamic_update_slice(
        jnp.zeros((hidden,), single), up_sum[0], (shard_place * hidden_part,)
    )
    sums = jnp.concatenate(
        [
            jnp.sum(first_delta * my_normed, axis=0),
            jnp.sum(first_delta, axis=0),
            jnp.sum(second_delta * my_normed, axis=0),
            jnp.sum(second_delta, axis=0),
            jnp.sum(cotangent[0], axis=0),
            heads_sum,
            up_sum,
        ]
    ).reshape(-1, 128)
    sums = sums + sum(swap(sums, "fsdp", k) for k in range(1, SHARDS))

    strips, owned, output_strip = call(
        strip_kernel,
        [
            ((SHARDS, strip, 2 * hidden_part + 3 * part), half),
            ((SHARDS, SHARDS, strip, width), half),
            ((strip, width), single),
        ],
        heads_sums + mlp_sums,
        where,
        "strip",
        0.1,
        earlier=[home],
    )
    owned, strips = call(
        owned_kernel,
        [((SHARDS, strip, hidden), half), (strips.shape, half)],
        [exchange(owned), strips] + mlp_pieces,
        where,
        "owned",
        0.1,
    )
    along = [owned, swap(owned, "ctx", Y_PLACES), swap(owned, "ctx", 2 * Y_PLACES)]
    first, second = swap(owned, "ctx", 1), swap(along[1], "ctx", 1)
    [again] = call(
        copy_kernel, [(owned.shape, half)], [owned], where, "again", 0.1, earlier=[second, along[2]]
    )
    along.append(swap(again, "ctx", 3 * Y_PLACES))
    third, fourth = swap(along[2], "ctx", 1), swap(along[3], "ctx", 1)
    pieces = [owned, first, along[1], second, along[2], third, along[3], fourth]
    grads, sums = call(
        grads_kernel,
        [((strip, 4 * width + 2 * hidden), half), (sums.shape, single)],
        [exchange(strips), output_strip, sums],
        where,
        "grads",
        0.1,
        earlier=pieces[1:],
    )
    grads_along = gather_z(grads)

    sums = sums + swap(sums, "ctx", 1)
    ortho, sums = newton(pieces, sums, where, [grads], grads_along[1:])
    sums = sums + sum(swap(sums, "ctx", Y_PLACES * k) for k in range(1, Z_PLACES))
    sums = sums.reshape(-1)
    arrived = exchange(ortho)
    new_weights = write_weights(arrived, weights_all, ctx_place)
    full_grads, new_moments = write_moments(
        jnp.stack(gather_y(grads_along)), moments_all, ctx_place
    )
    pieces = [sums[i * width : (i + 1) * width] for i in range(5)]
    heads_total = sums[5 * width : 8 * width]
    up_total = sums[8 * width :]
    vector_values = (
        gain_first,
        shift_first,
        gain_second,
        shift_second,
        heads_bias,
        output_bias,
        up_bias,
        down_bias,
    )
    vector_grads = (
        pieces[0],
        pieces[1],
        pieces[2],
        pieces[3],
        heads_total,
        pieces[4],
        up_total,
        pieces[4],
    )
    grad_shards = []
    new_shards = []
    for which in range(8):
        size_here = vector_values[which].shape[0]
        whole_grad = vector_grads[which]
        shard = lax.dynamic_slice_in_dim(whole_grad, shard_place * size_here, size_here)
        grad_shards.append(shard)
        new_shards.append(
            vector_values[which]
            - vector_rate * shard * lax.rsqrt(jnp.mean(whole_grad * whole_grad) + norm_eps)
        )
    return (
        block_out[None],
        input_grad[None],
        grad_shards[0],
        grad_shards[1],
        grad_shards[2],
        grad_shards[3],
        full_grads[0],
        grad_shards[4],
        full_grads[1],
        grad_shards[5],
        full_grads[2],
        grad_shards[6],
        full_grads[3],
        grad_shards[7],
        new_shards[0],
        new_shards[1],
        new_shards[2],
        new_shards[3],
        new_weights[0],
        new_shards[4],
        new_weights[1],
        new_shards[5],
        new_weights[2],
        new_shards[6],
        new_weights[3],
        new_shards[7],
        new_moments[0],
        new_moments[1],
        new_moments[2],
        new_moments[3],
    )


def solution(mesh):
    in_specs = (
        P("fsdp", "ctx", None),
        P("fsdp", "ctx", None),
        P(),
        P("fsdp"),
        P("fsdp"),
        P("fsdp"),
        P("fsdp"),
        P("fsdp", None),
        P("fsdp"),
        P("fsdp", None),
        P("fsdp"),
        P("fsdp", None),
        P("fsdp"),
        P("fsdp", None),
        P("fsdp"),
        P("fsdp", None),
        P("fsdp", None),
        P("fsdp", None),
        P("fsdp", None),
    )
    out_specs = (
        P("fsdp", "ctx", None),
        P("fsdp", "ctx", None),
        P("fsdp"),
        P("fsdp"),
        P("fsdp"),
        P("fsdp"),
        P("fsdp", None),
        P("fsdp"),
        P("fsdp", None),
        P("fsdp"),
        P("fsdp", None),
        P("fsdp"),
        P("fsdp", None),
        P("fsdp"),
        P("fsdp"),
        P("fsdp"),
        P("fsdp"),
        P("fsdp"),
        P("fsdp", None),
        P("fsdp"),
        P("fsdp", None),
        P("fsdp"),
        P("fsdp", None),
        P("fsdp"),
        P("fsdp", None),
        P("fsdp"),
        P("fsdp", None),
        P("fsdp", None),
        P("fsdp", None),
        P("fsdp", None),
    )
    sizes = dict(mesh.shape)
    fits = sizes["ctx"] == 8 and sizes["fsdp"] == 4
    chosen = local_fast if fits else local_general
    return jax.shard_map(chosen, mesh=mesh, in_specs=in_specs, out_specs=out_specs, check_vma=False)
```

```python
import math

import jax
import jax.numpy as jnp
from jax import lax
from jax.experimental import pallas as pl
from jax.experimental.pallas import tpu as pltpu
from jax.sharding import PartitionSpec as P

HEADS = 12
HD = 64
ROT = 16
NS_ITERS = 5


mom_rate = 0.95
schulz_coeffs = (3.4445, -4.775, 2.0315)
step_rates = (0.04, 0.3, 0.04, 0.04)
vector_rate = 0.3
norm_eps = 1e-05
neg_large = -1e30


def broadcast(x, axis, root):
    mine = lax.axis_index(axis) == root
    return lax.psum(jnp.where(mine, x, jnp.zeros_like(x)), axis)


def layer_norm(inputs, gain, shift):
    average = jnp.mean(inputs, axis=-1, keepdims=True)
    centred = inputs - average
    variance = jnp.mean(centred * centred, axis=-1, keepdims=True)
    inverse = lax.rsqrt(variance + norm_eps)
    normed = centred * inverse
    return (normed, inverse, normed * gain + shift)


def norm_back(delta, normed, inverse, gain):
    scaled = delta * gain
    first = jnp.mean(scaled, axis=-1, keepdims=True)
    second = jnp.mean(scaled * normed, axis=-1, keepdims=True)
    return inverse * (scaled - first - normed * second)


def gelu_value(pre):
    return 0.5 * pre * (1.0 + lax.erf(pre / math.sqrt(2.0)))


def gelu_slope(pre):
    return 0.5 * (1.0 + lax.erf(pre / math.sqrt(2.0))) + pre * jnp.exp(
        -0.5 * pre * pre
    ) / math.sqrt(2.0 * math.pi)


def slot_places(group_order, first_row, count, group):
    positions = first_row + jnp.arange(count, dtype=jnp.int32)
    slots = positions // group
    table = jnp.arange(group_order.shape[0], dtype=jnp.int32)
    picked = jnp.sum(jnp.where(slots[:, None] == table[None, :], group_order[None, :], 0), axis=1)
    return picked * group + positions % group


def rotary_tables(places):
    halfway = ROT // 2
    rates = 10000.0 ** (-2.0 * jnp.arange(halfway, dtype=jnp.float32) / ROT)
    angle = places.astype(jnp.float32)[:, None] * rates[None, :]
    return (jnp.cos(angle), jnp.sin(angle))


def rotate(heads, cosine, sine, sign):
    halfway = ROT // 2
    first = heads[..., :halfway]
    second = heads[..., halfway:ROT]
    cosine = cosine[:, None, :]
    sine = sign * sine[:, None, :]
    return jnp.concatenate(
        [first * cosine - second * sine, second * cosine + first * sine, heads[..., ROT:]], axis=-1
    )


def local_general(
    residual_in,
    cotangent,
    group_order,
    gain_first,
    shift_first,
    gain_second,
    shift_second,
    heads_weight,
    heads_bias,
    output_weight,
    output_bias,
    up_weight,
    up_bias,
    down_weight,
    down_bias,
    heads_moment,
    output_moment,
    up_moment,
    down_moment,
):
    single = jnp.float32
    half = jnp.bfloat16
    ctx_count = lax.axis_size("ctx")
    shard_count = lax.axis_size("fsdp")
    ctx_place = lax.axis_index("ctx")
    shard_place = lax.axis_index("fsdp")
    seqs, rows, width = residual_in.shape
    length = rows * ctx_count
    group = rows // 2
    scale = 1.0 / math.sqrt(HD)
    query_places = slot_places(group_order, ctx_place * rows, rows, group)
    key_places = slot_places(group_order, 0, length, group)
    copies = (
        lax.all_gather(heads_weight.astype(half), "fsdp", axis=0, tiled=True),
        lax.all_gather(output_weight.astype(half), "fsdp", axis=0, tiled=True),
        lax.all_gather(up_weight.astype(half), "fsdp", axis=0, tiled=True),
        lax.all_gather(down_weight.astype(half), "fsdp", axis=0, tiled=True),
        lax.all_gather(gain_first.astype(half), "fsdp", axis=0, tiled=True),
        lax.all_gather(shift_first.astype(half), "fsdp", axis=0, tiled=True),
        lax.all_gather(gain_second.astype(half), "fsdp", axis=0, tiled=True),
        lax.all_gather(shift_second.astype(half), "fsdp", axis=0, tiled=True),
        lax.all_gather(heads_bias.astype(half), "fsdp", axis=0, tiled=True),
        lax.all_gather(output_bias.astype(half), "fsdp", axis=0, tiled=True),
        lax.all_gather(up_bias.astype(half), "fsdp", axis=0, tiled=True),
        lax.all_gather(down_bias.astype(half), "fsdp", axis=0, tiled=True),
    )
    heads_copy, output_copy, up_copy, down_copy = (copies[0], copies[1], copies[2], copies[3])
    gain_one, shift_one, gain_two, shift_two, heads_shift, output_shift, up_shift, down_shift = [
        piece.astype(single) for piece in copies[4:]
    ]
    inputs = residual_in.astype(single)
    first_hat, first_inv, first_norm = layer_norm(inputs, gain_one, shift_one)
    second_hat, second_inv, second_norm = layer_norm(inputs, gain_two, shift_two)
    first_in = first_norm.astype(half)
    second_in = second_norm.astype(half)
    projected = (
        jnp.einsum("std,de->ste", first_in, heads_copy, preferred_element_type=single) + heads_shift
    )
    cosine, sine = rotary_tables(query_places)
    split = projected.reshape(seqs, rows, 3, HEADS, HD)
    query = rotate(split[:, :, 0], cosine, sine, 1.0).astype(half)
    keys = rotate(split[:, :, 1], cosine, sine, 1.0).astype(half).reshape(seqs, rows, width)
    values = split[:, :, 2].astype(half).reshape(seqs, rows, width)
    peak = jnp.full((seqs, HEADS, rows), neg_large, single)
    key_piece = lax.all_gather(keys, "ctx", axis=1, tiled=True)
    value_piece = lax.all_gather(values, "ctx", axis=1, tiled=True)
    count = key_piece.shape[1]
    places = slot_places(group_order, jnp.int32(0), count, group)
    key_heads = key_piece.reshape(seqs, count, HEADS, HD)
    value_heads = value_piece.reshape(seqs, count, HEADS, HD)
    score = jnp.einsum("sqhd,skhd->shqk", query, key_heads, preferred_element_type=single) * scale
    allowed = (places[None, :] <= query_places[:, None])[None, None]
    new_peak = jnp.maximum(peak, jnp.max(jnp.where(allowed, score, neg_large), axis=-1))
    weights = jnp.where(allowed, jnp.exp(score - new_peak[..., None]), 0.0)
    total = jnp.sum(weights, axis=-1)
    mixed = jnp.einsum(
        "shqk,skhd->shqd", weights.astype(half), value_heads, preferred_element_type=single
    )
    state = (new_peak, total, mixed)
    peak, total, mixed = state
    lse = peak + jnp.log(total)
    attn = (
        jnp.transpose(mixed / total[..., None], (0, 2, 1, 3))
        .reshape(seqs, rows, width)
        .astype(half)
    )
    output_part = (
        jnp.einsum("std,de->ste", attn, output_copy, preferred_element_type=single) + output_shift
    )
    up_pre = jnp.einsum("std,df->stf", second_in, up_copy, preferred_element_type=single) + up_shift
    active = gelu_value(up_pre).astype(half)
    mlp_part = (
        jnp.einsum("stf,df->std", active, down_copy, preferred_element_type=single) + down_shift
    )
    block_out = (inputs + output_part + mlp_part).astype(half)
    grad_half = cotangent.astype(half)
    down_local = jnp.einsum("std,stf->df", grad_half, active, preferred_element_type=single)
    up_delta = jnp.einsum(
        "std,df->stf", grad_half, down_copy, preferred_element_type=single
    ) * gelu_slope(up_pre)
    up_half = up_delta.astype(half)
    up_local = jnp.einsum("std,stf->df", second_in, up_half, preferred_element_type=single)
    second_delta = jnp.einsum("stf,df->std", up_half, up_copy, preferred_element_type=single)
    output_local = jnp.einsum("std,ste->de", attn, grad_half, preferred_element_type=single)
    attn_delta = jnp.einsum(
        "ste,de->std", grad_half, output_copy, preferred_element_type=single
    ).astype(half)
    attn_heads = attn_delta.reshape(seqs, rows, HEADS, HD)
    delta = jnp.transpose(
        jnp.sum(
            attn_heads.astype(single) * attn.reshape(seqs, rows, HEADS, HD).astype(single), axis=-1
        ),
        (0, 2, 1),
    )
    every_key, every_value = (
        lax.all_gather(keys, "ctx", axis=1, tiled=True),
        lax.all_gather(values, "ctx", axis=1, tiled=True),
    )
    block = math.gcd(length, 512)
    count = length // block
    key_blocks = jnp.moveaxis(every_key.reshape(seqs, count, block, HEADS, HD), 1, 0)
    value_blocks = jnp.moveaxis(every_value.reshape(seqs, count, block, HEADS, HD), 1, 0)
    place_blocks = key_places.reshape(count, block)

    def back_block(query_grad, data):
        key_block, value_block, place_block = data
        score = (
            jnp.einsum("sqhd,skhd->shqk", query, key_block, preferred_element_type=single) * scale
        )
        allowed = (place_block[None, :] <= query_places[:, None])[None, None]
        prob = jnp.where(allowed, jnp.exp(score - lse[..., None]), 0.0)
        prob_half = prob.astype(half)
        prob_grad = jnp.einsum(
            "sqhd,skhd->shqk", attn_heads, value_block, preferred_element_type=single
        )
        score_delta = (prob * (prob_grad - delta[..., None])).astype(half)
        query_grad = (
            query_grad
            + jnp.einsum("shqk,skhd->sqhd", score_delta, key_block, preferred_element_type=single)
            * scale
        )
        key_grad = (
            jnp.einsum("shqk,sqhd->skhd", score_delta, query, preferred_element_type=single) * scale
        )
        value_grad = jnp.einsum(
            "shqk,sqhd->skhd", prob_half, attn_heads, preferred_element_type=single
        )
        joined = jnp.concatenate(
            [key_grad.reshape(seqs, block, width), value_grad.reshape(seqs, block, width)], axis=-1
        )
        return (query_grad, joined)

    query_grad, stacked = lax.scan(
        back_block,
        jnp.zeros((seqs, rows, HEADS, HD), single),
        (key_blocks, value_blocks, place_blocks),
    )
    key_grads = jnp.moveaxis(stacked, 0, 1).reshape(seqs, length, 2 * width)
    home = lax.psum_scatter(key_grads, "ctx", scatter_dimension=1, tiled=True)
    key_delta = rotate(home[..., :width].reshape(seqs, rows, HEADS, HD), cosine, sine, -1.0)
    query_delta = rotate(query_grad, cosine, sine, -1.0)
    heads_delta = jnp.concatenate(
        [
            query_delta.reshape(seqs, rows, width),
            key_delta.reshape(seqs, rows, width),
            home[..., width:],
        ],
        axis=-1,
    )
    heads_half = heads_delta.astype(half)
    heads_local = jnp.einsum("std,ste->de", first_in, heads_half, preferred_element_type=single)
    first_delta = jnp.einsum("ste,de->std", heads_half, heads_copy, preferred_element_type=single)
    input_grad = (
        cotangent
        + norm_back(first_delta, first_hat, first_inv, gain_one)
        + norm_back(second_delta, second_hat, second_inv, gain_two)
    )
    columns = (
        lax.psum_scatter(heads_local, "ctx", scatter_dimension=1, tiled=True),
        lax.psum_scatter(output_local, "ctx", scatter_dimension=1, tiled=True),
        lax.psum_scatter(up_local, "ctx", scatter_dimension=1, tiled=True),
        lax.psum_scatter(down_local, "ctx", scatter_dimension=1, tiled=True),
    )
    parts = (
        lax.psum_scatter(columns[0], "fsdp", scatter_dimension=0, tiled=True),
        lax.psum_scatter(columns[1], "fsdp", scatter_dimension=0, tiled=True),
        lax.psum_scatter(columns[2], "fsdp", scatter_dimension=0, tiled=True),
        lax.psum_scatter(columns[3], "fsdp", scatter_dimension=0, tiled=True),
    )
    full_grads = (
        lax.all_gather(parts[0], "ctx", axis=1, tiled=True),
        lax.all_gather(parts[1], "ctx", axis=1, tiled=True),
        lax.all_gather(parts[2], "ctx", axis=1, tiled=True),
        lax.all_gather(parts[3], "ctx", axis=1, tiled=True),
    )
    weights_all = (heads_weight, output_weight, up_weight, down_weight)
    moments_all = (heads_moment, output_moment, up_moment, down_moment)
    new_moments = []
    nest_blocks = []
    for which in range(4):
        moment = mom_rate * moments_all[which] + full_grads[which]
        nest = full_grads[which] + mom_rate * moment
        cols = nest.shape[1] // ctx_count
        new_moments.append(moment)
        nest_blocks.append(lax.dynamic_slice_in_dim(nest, ctx_place * cols, cols, 1))
    sums = lax.psum(
        (
            jnp.sum(first_delta * first_hat, axis=(0, 1)),
            jnp.sum(first_delta, axis=(0, 1)),
            jnp.sum(second_delta * second_hat, axis=(0, 1)),
            jnp.sum(second_delta, axis=(0, 1)),
            jnp.sum(heads_delta, axis=(0, 1)),
            jnp.sum(cotangent, axis=(0, 1)),
            jnp.sum(up_delta, axis=(0, 1)),
            jnp.sum(nest_blocks[0] * nest_blocks[0]),
            jnp.sum(nest_blocks[1] * nest_blocks[1]),
            jnp.sum(nest_blocks[2] * nest_blocks[2]),
            jnp.sum(nest_blocks[3] * nest_blocks[3]),
        ),
        ("ctx", "fsdp"),
    )
    gathered = (
        lax.all_gather(nest_blocks[0], "fsdp", axis=0, tiled=True),
        lax.all_gather(nest_blocks[1], "fsdp", axis=0, tiled=True),
        lax.all_gather(nest_blocks[2], "fsdp", axis=0, tiled=True),
        lax.all_gather(nest_blocks[3], "fsdp", axis=0, tiled=True),
    )
    widths = [piece.shape[1] for piece in gathered]
    widest = max(widths)
    owners = [which * shard_count // 4 for which in range(4)]
    selected = jnp.zeros((width, widest), single)
    square_sum = jnp.zeros((), single)
    for which in range(4):
        chosen = (shard_place == owners[which]).astype(single)
        selected = selected + chosen * jnp.pad(
            gathered[which], ((0, 0), (0, widest - widths[which]))
        )
        square_sum = square_sum + chosen * sums[7 + which]
    ortho = (selected / (jnp.sqrt(square_sum) + 1e-07)).astype(half)
    for turn in range(NS_ITERS):
        partial_value = jnp.einsum("rw,sw->rs", ortho, ortho, preferred_element_type=single)
        gram = lax.psum(partial_value.astype(jnp.bfloat16), "ctx").astype(jnp.float32).astype(half)
        mix = (
            schulz_coeffs[1] * gram.astype(single)
            + schulz_coeffs[2] * jnp.dot(gram, gram, preferred_element_type=single)
        ).astype(half)
        ortho = (
            schulz_coeffs[0] * ortho.astype(single)
            + jnp.dot(mix, ortho, preferred_element_type=single)
        ).astype(half)
    shard_rows = width // shard_count
    updated = []
    for which in range(4):
        received = broadcast(ortho, "fsdp", owners[which])
        piece = lax.dynamic_slice(
            received, (shard_place * shard_rows, 0), (shard_rows, widths[which])
        )
        total_cols = weights_all[which].shape[1]
        current = lax.dynamic_slice_in_dim(
            weights_all[which], ctx_place * widths[which], widths[which], 1
        )
        updated.append(current - step_rates[which] * math.sqrt(total_cols) * piece.astype(single))
    new_weights = (
        lax.all_gather(updated[0], "ctx", axis=1, tiled=True),
        lax.all_gather(updated[1], "ctx", axis=1, tiled=True),
        lax.all_gather(updated[2], "ctx", axis=1, tiled=True),
        lax.all_gather(updated[3], "ctx", axis=1, tiled=True),
    )
    vector_values = (
        gain_first,
        shift_first,
        gain_second,
        shift_second,
        heads_bias,
        output_bias,
        up_bias,
        down_bias,
    )
    vector_grads = (sums[0], sums[1], sums[2], sums[3], sums[4], sums[5], sums[6], sums[5])
    grad_shards = []
    new_shards = []
    for which in range(8):
        size_here = vector_values[which].shape[0]
        whole_grad = vector_grads[which]
        shard = lax.dynamic_slice_in_dim(whole_grad, shard_place * size_here, size_here)
        grad_shards.append(shard)
        new_shards.append(
            vector_values[which]
            - vector_rate * shard * lax.rsqrt(jnp.mean(whole_grad * whole_grad) + norm_eps)
        )
    return (
        block_out,
        input_grad,
        grad_shards[0],
        grad_shards[1],
        grad_shards[2],
        grad_shards[3],
        full_grads[0],
        grad_shards[4],
        full_grads[1],
        grad_shards[5],
        full_grads[2],
        grad_shards[6],
        full_grads[3],
        grad_shards[7],
        new_shards[0],
        new_shards[1],
        new_shards[2],
        new_shards[3],
        new_weights[0],
        new_shards[4],
        new_weights[1],
        new_shards[5],
        new_weights[2],
        new_shards[6],
        new_weights[3],
        new_shards[7],
        new_moments[0],
        new_moments[1],
        new_moments[2],
        new_moments[3],
    )


Y_PLACES = 2
Z_PLACES = 4
CTX = Y_PLACES * Z_PLACES
SHARDS = 4


OWNERS = (0, 2, 1, 3)


def swap(x, axis, offset):
    count = lax.axis_size(axis)
    return lax.ppermute(x, axis, [(i, i ^ offset) for i in range(count)])


def exchange(x, axis="fsdp"):
    return lax.all_to_all(x, axis, 0, 0)


def pick(x, index, dim=0):
    return lax.dynamic_index_in_dim(x, index, dim, keepdims=False)


def gather_z(x):
    return [x] + [swap(x, "ctx", Y_PLACES * k) for k in range(1, Z_PLACES)]


def gather_y(along):
    pieces = []
    for piece in along:
        pieces += [piece, swap(piece, "ctx", 1)]
    return pieces


def call(kernel, outs, args, prefetch, name, cost, scratch=(), earlier=()):
    whole = pl.BlockSpec(memory_space=pltpu.VMEM)
    count = 1 + len(args)

    def body(*refs):
        kernel(*refs[:count], *refs[count + len(earlier) :])

    return pl.pallas_call(
        body,
        in_specs=[pl.BlockSpec(memory_space=pltpu.SMEM)]
        + [whole] * len(args)
        + [pl.BlockSpec(memory_space=pl.ANY)] * len(earlier),
        out_specs=[whole] * len(outs),
        out_shape=[jax.ShapeDtypeStruct(shape, dtype) for shape, dtype in outs],
        scratch_shapes=list(scratch),
        compiler_params=pltpu.CompilerParams(vmem_limit_bytes=50 * 1024 * 1024),
        cost_estimate=pl.CostEstimate(
            flops=0, bytes_accessed=int(cost * 3.6e6), transcendentals=0
        ),
        name=name,
    )(prefetch, *args, *earlier)


NT = (((1,), (1,)), ((), ()))
TN = (((0,), (0,)), ((), ()))


def pack_kernel(where_ref, residual_ref, grad_ref, *refs):
    half = jnp.bfloat16
    vectors_ref, out_ref = refs
    place = where_ref[2]
    rows, width = residual_ref.shape
    part = width // SHARDS

    def share(start, size):
        lane = lax.broadcasted_iota(jnp.int32, (1, SHARDS * size), 1)
        mine = jnp.logical_and(lane >= place * size, lane < (place + 1) * size)
        piece = vectors_ref[:, start : start + size]
        return jnp.where(mine, jnp.concatenate([piece] * SHARDS, axis=1), 0.0)

    heads = share(6 * part, 3 * part)
    out_ref[:rows] = residual_ref[...]
    out_ref[rows : 2 * rows] = grad_ref[...].astype(half)
    small = [share(i * part, part) for i in range(6)]
    small += [heads[:, t * width : (t + 1) * width] for t in range(3)]
    small.append(jnp.zeros((16 - len(small), width), jnp.float32))
    out_ref[2 * rows :] = jnp.concatenate(small, axis=0).astype(half)


def heads_split_kernel(where_ref, weight_ref, out_ref):
    part, width = weight_ref.shape[0], weight_ref.shape[1] // 3
    for dest in range(SHARDS):
        out_ref[dest] = jnp.concatenate(
            [
                weight_ref[:, t * width + dest * part : t * width + (dest + 1) * part]
                for t in range(3)
            ],
            axis=1,
        ).astype(jnp.bfloat16)


def mlp_split_kernel(where_ref, up_ref, down_ref, moments_ref, *outs):
    place = where_ref[2]
    part, cols = up_ref.shape[0], up_ref.shape[1] // SHARDS
    for k in range(SHARDS):
        cut = pl.ds(pl.multiple_of((place ^ k) * cols, cols), cols)
        outs[k][:part, :cols] = up_ref[:, cut].astype(jnp.bfloat16)
        outs[k][:part, cols:] = down_ref[:, cut].astype(jnp.bfloat16)
        moment = moments_ref[place ^ k]
        outs[k][part:] = jnp.concatenate(
            [moment[:, : 2 * cols], moment[:, 2 * cols :]], axis=0
        ).astype(jnp.bfloat16)


def turn(x, cos_ref, high_ref, low_ref, direction):
    lanes = x.shape[1]
    moved = pltpu.roll(x, ROT // 2, 1) * high_ref[...] + pltpu.roll(
        x, lanes - ROT // 2, 1
    ) * low_ref[...]
    return x * cos_ref[...] + direction * moved


def pre_kernel(where_ref, *refs):
    single, half = jnp.float32, jnp.bfloat16
    packs, block_ref = refs[:4], refs[4]
    output_ref, cos_ref, high_ref, low_ref = refs[5:9]
    first_ref, second_ref, grad_ref, payload_ref, normed_ref, inverse_ref = refs[9:]
    place = where_ref[2]
    part = output_ref.shape[0]
    rows = normed_ref.shape[0]
    vectors = sum(p[2 * rows :].astype(single) for p in packs)
    for r in range(SHARDS):
        x = packs[r][:rows].astype(single)
        average = jnp.mean(x, axis=-1, keepdims=True)
        centred = x - average
        variance = jnp.mean(centred * centred, axis=-1, keepdims=True)
        inverse = lax.rsqrt(variance + norm_eps)
        normed = centred * inverse
        if r == 0:
            normed_ref[...] = normed
            inverse_ref[...] = jnp.broadcast_to(inverse, inverse_ref.shape)
        cut = slice(r * rows, (r + 1) * rows)
        first_ref[cut] = (normed * vectors[0:1] + vectors[1:2]).astype(half)
        second_ref[cut] = (normed * vectors[2:3] + vectors[3:4]).astype(half)
        grad_ref[cut] = packs[r][rows : 2 * rows]
    shift = jnp.concatenate(
        [
            sum(
                jnp.where(place == j, vectors[6 + t : 7 + t, j * part : (j + 1) * part], 0.0)
                for j in range(SHARDS)
            )
            for t in range(3)
        ],
        axis=1,
    )
    projected = jnp.dot(first_ref[...], block_ref[...], preferred_element_type=single) + shift
    outer = lax.dot_general(
        grad_ref[...], output_ref[...], NT, preferred_element_type=single
    ).astype(half)
    for r in range(SHARDS):
        cut = slice(r * rows, (r + 1) * rows)
        turned = turn(projected[cut, : 2 * part], cos_ref, high_ref, low_ref, 1.0).astype(half)
        values = projected[cut, 2 * part :].astype(half)
        back = outer[cut]

        def head(x, h):
            return x[:, h * HD : (h + 1) * HD]

        last = 3 * Z_PLACES // 4 - 1
        shared = jnp.concatenate([head(turned, 3 + last), head(values, last)], axis=1)
        query = jnp.concatenate([head(turned, last), head(back, last)], axis=1)
        for y in range(Y_PLACES):
            at = r * Y_PLACES + y
            payload_ref[at, :rows] = jnp.concatenate([head(turned, y), head(turned, 3 + y)], axis=1)
            payload_ref[at, rows : 2 * rows] = jnp.concatenate(
                [head(values, y), head(back, y)], axis=1
            )
            payload_ref[at, 2 * rows : 3 * rows] = shared
            payload_ref[at, 3 * rows :] = query[y * rows // 2 : (y + 1) * rows // 2]


def write_strips(grad_ref, send_ref, keep_ref, y):
    strip = send_ref.shape[2]
    for f in range(SHARDS):
        for z in range(Z_PLACES):
            start = (f * CTX + z * Y_PLACES) * strip
            mine = pl.multiple_of(start + y * strip, 8)
            other = pl.multiple_of(start + (1 - y) * strip, 8)
            keep_ref[f, z] = grad_ref[pl.ds(mine, strip), :]
            send_ref[f, z] = grad_ref[pl.ds(other, strip), :].astype(jnp.bfloat16)


def mlp_kernel(where_ref, *refs):
    single, half = jnp.float32, jnp.bfloat16
    second_ref, grad_ref, shift_ref = refs[:3]
    pieces = refs[3:7]
    send_ref, keep_ref, out_ref, sum_ref, back_ref, block_ref, local_ref = refs[7:]
    y, place = where_ref[1], where_ref[2]
    cols = shift_ref.shape[1]
    part = block_ref.shape[0] // SHARDS
    for k in range(SHARDS):
        block_ref[pl.ds(pl.multiple_of((place ^ k) * part, part), part), :] = pieces[k][:part]
    second, grad = second_ref[...], grad_ref[...]
    up = block_ref[:, :cols]
    down = block_ref[:, cols:]
    pre = jnp.dot(second, up, preferred_element_type=single) + shift_ref[...]
    cdf = 0.5 * (1.0 + lax.erf(pre * (1.0 / math.sqrt(2.0))))
    active = (pre * cdf).astype(half)
    slope = cdf + pre * jnp.exp(-0.5 * pre * pre) * (1.0 / math.sqrt(2.0 * math.pi))
    delta = jnp.dot(grad, down, preferred_element_type=single) * slope
    sum_ref[...] = jnp.sum(delta, axis=0, keepdims=True)
    delta_half = delta.astype(half)
    local_ref[:, :cols] = lax.dot_general(second, delta_half, TN, preferred_element_type=single)
    local_ref[:, cols:] = lax.dot_general(grad, active, TN, preferred_element_type=single)
    write_strips(local_ref, send_ref, keep_ref, y)
    out_ref[...] = lax.dot_general(active, down, NT, preferred_element_type=single)
    back_ref[...] = lax.dot_general(delta_half, up, NT, preferred_element_type=single)


def post_kernel(where_ref, *refs):
    single, half = jnp.float32, jnp.bfloat16
    back_ref, first_ref, grad_ref, block_ref, output_ref, mlp_ref, second_ref = refs[:7]
    cos_ref, high_ref, low_ref = refs[7:10]
    send_ref, keep_ref, sum_ref, mine_ref, home_ref = refs[10:15]
    attn_ref, heads_ref, local_ref = refs[15:]
    y, place = where_ref[1], where_ref[2]
    part, width = output_ref.shape
    rows = mine_ref.shape[0] // 3
    sums = jnp.zeros((1, 3 * part), single)
    for r in range(SHARDS):
        cut = slice(r * rows, (r + 1) * rows)
        early = [back_ref[r * Y_PLACES + i, :rows] for i in range(Y_PLACES)]
        early.append(
            jnp.concatenate([back_ref[r * Y_PLACES + i, 3 * rows :] for i in range(Y_PLACES)], axis=0)
        )
        late = [back_ref[r * Y_PLACES + i, rows : 2 * rows].astype(single) for i in range(Y_PLACES)]
        late.append(
            sum(back_ref[r * Y_PLACES + i, 2 * rows : 3 * rows].astype(single) for i in range(Y_PLACES))
        )
        attn_ref[cut] = jnp.concatenate([x[:, :HD] for x in early], axis=1)
        turned = turn(
            jnp.concatenate(
                [x[:, HD:].astype(single) for x in early] + [x[:, :HD] for x in late], axis=1
            ),
            cos_ref,
            high_ref,
            low_ref,
            -1.0,
        )
        whole = jnp.concatenate([turned] + [x[:, HD:] for x in late], axis=1)
        sums += jnp.sum(whole, axis=0, keepdims=True)
        heads_ref[cut] = whole.astype(half)
    sum_ref[...] = sums
    local_ref[:, : 3 * part] = lax.dot_general(
        first_ref[...], heads_ref[...], TN, preferred_element_type=single
    )
    output_local = lax.dot_general(
        attn_ref[...], grad_ref[...], TN, preferred_element_type=single
    )
    for j in range(SHARDS):
        local_ref[j * part : (j + 1) * part, 3 * part :] = output_local[:, j * part : (j + 1) * part]
    write_strips(local_ref, send_ref, keep_ref, y)
    out = jnp.dot(attn_ref[...], output_ref[...], preferred_element_type=single) + mlp_ref[...]
    first = lax.dot_general(heads_ref[...], block_ref[...], NT, preferred_element_type=single)
    for i, value in enumerate((out, first, second_ref[...])):
        cut = slice(i * rows, (i + 1) * rows)
        mine_ref[cut] = value[:rows]
        home_ref[place, cut] = jnp.zeros((rows, width), half)
        for k in range(1, SHARDS):
            home_ref[place ^ k, cut] = value[k * rows : (k + 1) * rows].astype(half)


def along_z_kernel(where_ref, keep_ref, came_ref, own_ref, *sends):
    z = where_ref[0]
    own_ref[...] = keep_ref[:, z] + came_ref[:, z].astype(jnp.float32)
    for k in range(1, Z_PLACES):
        sends[k - 1][...] = (keep_ref[:, z ^ k] + came_ref[:, z ^ k].astype(jnp.float32)).astype(
            jnp.bfloat16
        )


def scatter_ctx(send, keep, where, name, *earlier):
    single, half = jnp.float32, jnp.bfloat16
    came = swap(send, "ctx", 1)
    shape = (keep.shape[0],) + keep.shape[2:]
    own, *sends = call(
        along_z_kernel,
        [(shape, single)] + [(shape, half)] * (Z_PLACES - 1),
        [keep, came],
        where,
        name,
        0.1,
        earlier=earlier,
    )
    return came, [own] + [swap(sends[k - 1], "ctx", 2 * k) for k in range(1, Z_PLACES)]


def strip_sum(parts, index):
    return parts[0][index] + sum(p[index].astype(jnp.float32) for p in parts[1:])


def strip_kernel(where_ref, *refs):
    half = jnp.bfloat16
    heads, mlp = refs[:4], refs[4:8]
    strips_ref, owners_ref, output_ref = refs[8:]
    size = owners_ref.shape[3]
    cols = 3 * size // 4
    for j in range(SHARDS):
        total = strip_sum(heads, j)
        both = strip_sum(mlp, j).astype(half)
        strips_ref[j, :, : 2 * size] = both
        strips_ref[j, :, 2 * size :] = total[:, :cols].astype(half)
        output_ref[:, j * size // SHARDS : (j + 1) * size // SHARDS] = total[:, cols:]
        owners_ref[OWNERS[0], j] = total.astype(half)
        owners_ref[OWNERS[2], j] = both[:, :size]
        owners_ref[OWNERS[3], j] = both[:, size:]
    owners_ref[OWNERS[1], 0] = output_ref[...].astype(half)
    owners_ref[OWNERS[1], 1:] = jnp.zeros(owners_ref.shape[1:], half)[1:]


def owned_kernel(where_ref, grads_ref, strips_ref, *refs):
    single = jnp.float32
    moments, out_ref, strips_out = refs[:4], refs[4], refs[5]
    strips_out[...] = strips_ref[...]
    place = where_ref[2]
    size = grads_ref.shape[3]
    part = size // SHARDS

    def write(f, owner, grad):
        cols, strip = grad.shape[1], grad.shape[0]
        both = moments[f ^ owner][part:].astype(single)
        moment = jnp.concatenate([both[:strip], both[strip:]], axis=1)[:, :cols]
        nest = grad + mom_rate * (mom_rate * moment + grad)
        out_ref[f, :, :cols] = nest.astype(out_ref.dtype)
        if cols < out_ref.shape[2]:
            rest = (out_ref.shape[1], out_ref.shape[2] - cols)
            out_ref[f, :, cols:] = jnp.zeros(rest, out_ref.dtype)

    @pl.when(place == OWNERS[0])
    def _():
        for f in range(SHARDS):
            pieces = [
                grads_ref[j, f][:, t * part : (t + 1) * part].astype(single)
                for t in range(3)
                for j in range(SHARDS)
            ]
            write(f, OWNERS[0], jnp.concatenate(pieces, axis=1))

    @pl.when(place == OWNERS[1])
    def _():
        for f in range(SHARDS):
            write(f, OWNERS[1], grads_ref[f, 0].astype(single))

    for owner in OWNERS[2:]:

        @pl.when(place == owner)
        def _():
            for f in range(SHARDS):
                pieces = [grads_ref[j, f].astype(single) for j in range(SHARDS)]
                write(f, owner, jnp.concatenate(pieces, axis=1))


def copy_kernel(where_ref, x_ref, out_ref):
    out_ref[...] = x_ref[...]


def grads_kernel(where_ref, strips_ref, output_ref, sums_ref, out_ref, sums_out):
    sums_out[...] = sums_ref[...]
    size = output_ref.shape[1]
    part = size // SHARDS
    pieces = [
        strips_ref[f][:, 2 * size + t * part : 2 * size + (t + 1) * part].astype(jnp.float32)
        for t in range(3)
        for f in range(SHARDS)
    ]
    out_ref[...] = jnp.concatenate(
        pieces
        + [output_ref[...]]
        + [
            strips_ref[f][:, i * size : (i + 1) * size].astype(jnp.float32)
            for i in range(2)
            for f in range(SHARDS)
        ],
        axis=1,
    ).astype(jnp.bfloat16)


NEWTON_SIZE = 256
NEWTON_CHUNK = 768


def newton_mixing(x_ref, gram_ref, mix_ref):
    single, half = jnp.float32, jnp.bfloat16
    blocks = x_ref.shape[0] // NEWTON_SIZE
    cuts = [slice(i * NEWTON_SIZE, (i + 1) * NEWTON_SIZE) for i in range(blocks)]
    pairs = [(cuts[i], cuts[j]) for i in range(blocks) for j in range(i, blocks)]
    for here, there in pairs:
        gram = lax.dot_general(x_ref[here], x_ref[there], NT, preferred_element_type=single)
        gram_ref[here, there] = gram.astype(half)
        if here != there:
            gram_ref[there, here] = jnp.transpose(gram).astype(half)
    for here, there in pairs:
        square = jnp.dot(gram_ref[here], gram_ref[:, there], preferred_element_type=single)
        mix = schulz_coeffs[1] * gram_ref[here, there].astype(single) + schulz_coeffs[2] * square
        mix_ref[here, there] = mix.astype(half)
        if here != there:
            mix_ref[there, here] = jnp.transpose(mix).astype(half)


def newton_applied(x_ref, mix_ref, at):
    x = x_ref[:, at : at + NEWTON_CHUNK]
    return schulz_coeffs[0] * x.astype(jnp.float32) + jnp.dot(
        mix_ref[...], x, preferred_element_type=jnp.float32
    )


def newton_kernel(where_ref, *refs):
    single, half = jnp.float32, jnp.bfloat16
    pieces, x_ref, gram_ref, mix_ref = refs[:CTX], *refs[CTX:]
    cols = x_ref.shape[1]
    tall = SHARDS * pieces[0].shape[1]
    total = jnp.zeros((1, 1), single)
    for piece in pieces:
        value = piece[...].astype(single)
        total += jnp.sum(jnp.sum(value * value, axis=0), keepdims=True)
    factor = 1.0 / (jnp.sqrt(total) + 1e-07)
    for c in range(CTX):
        value = pieces[c][...].astype(single).reshape(tall, cols)
        x_ref[c * tall : (c + 1) * tall] = (value * factor).astype(half)

    @pl.loop(0, NS_ITERS - 1)
    def _(step):
        newton_mixing(x_ref, gram_ref, mix_ref)
        for at in range(0, cols, NEWTON_CHUNK):
            x_ref[:, at : at + NEWTON_CHUNK] = newton_applied(x_ref, mix_ref, at).astype(half)


def last_newton_kernel(where_ref, x_ref, sums_ref, out_ref, sums_out, gram_ref, mix_ref):
    sums_out[...] = sums_ref[...]
    newton_mixing(x_ref, gram_ref, mix_ref)
    strip = out_ref.shape[2]
    for at in range(0, x_ref.shape[1], NEWTON_CHUNK):
        x = newton_applied(x_ref, mix_ref, at)
        for c in range(CTX):
            for k in range(SHARDS):
                start = (c * SHARDS + k) * strip
                out_ref[k, c, :, at : at + NEWTON_CHUNK] = x[start : start + strip].astype(
                    jnp.bfloat16
                )


def newton(pieces, sums, where, earlier, between):
    strip, cols = pieces[0].shape[1:]
    n = CTX * SHARDS * strip
    half = jnp.bfloat16
    scratch = [pltpu.VMEM((n, n), half), pltpu.VMEM((n, n), half)]
    [x] = call(
        newton_kernel, [((n, cols), half)], list(pieces), where, "newton", 36.0, scratch, earlier
    )
    return call(
        last_newton_kernel,
        [((SHARDS, CTX, strip, cols), half), (sums.shape, sums.dtype)],
        [x, sums],
        where,
        "last_newton",
        9.0,
        scratch,
        between,
    )


def attention_kernel(where_ref, recv_ref, place_row_ref, place_col_ref, place_half_ref, out_ref):
    single, half = jnp.float32, jnp.bfloat16
    scale = 1.0 / math.sqrt(HD)
    rows = 128
    length = CTX * rows
    place_row = place_row_ref[...]

    def run(query, keys, values, outer, places, step):
        key_sum = jnp.zeros((length, HD), single)
        value_sum = jnp.zeros((length, HD), single)
        mixed_all, query_all = [], []
        for at in range(0, query.shape[0], step):
            one = query[at : at + step]
            back = outer[at : at + step]
            score = (
                lax.dot_general(one, keys, (((1,), (1,)), ((), ())), preferred_element_type=single)
                * scale
            )
            allowed = place_row <= places[at : at + step]
            score = jnp.where(allowed, score, neg_large)
            peak = jnp.max(score, axis=-1, keepdims=True)
            weights = jnp.where(allowed, jnp.exp(score - peak), 0.0)
            total = jnp.sum(weights, axis=-1, keepdims=True)
            prob = weights * (1.0 / total)
            prob_half = prob.astype(half)
            mixed = jnp.dot(prob_half, values, preferred_element_type=single).astype(half)
            delta = jnp.sum(
                back.astype(single) * mixed.astype(single), axis=-1, keepdims=True
            )
            prob_grad = lax.dot_general(
                back, values, (((1,), (1,)), ((), ())), preferred_element_type=single
            )
            score_delta = (prob * (prob_grad - delta)).astype(half)
            query_grad = jnp.dot(score_delta, keys, preferred_element_type=single) * scale
            key_sum += lax.dot_general(
                score_delta, one, (((0,), (0,)), ((), ())), preferred_element_type=single
            )
            value_sum += lax.dot_general(
                prob_half, back, (((0,), (0,)), ((), ())), preferred_element_type=single
            )
            mixed_all.append(mixed)
            query_all.append(query_grad.astype(half))
        return (
            jnp.concatenate(mixed_all, axis=0),
            jnp.concatenate(query_all, axis=0),
            (key_sum * scale).astype(half),
            value_sum.astype(half),
        )

    first = recv_ref[:, 0:128, :].reshape(length, 128)
    second = recv_ref[:, 128:256, :].reshape(length, 128)
    mixed, query_grad, key_grad, value_grad = run(
        first[:, :HD], first[:, HD:], second[:, :HD], second[:, HD:], place_col_ref[...], 256
    )
    out_ref[:, 0:128, :] = jnp.concatenate([mixed, query_grad], axis=1).reshape(CTX, rows, 128)
    out_ref[:, 128:256, :] = jnp.concatenate([key_grad, value_grad], axis=1).reshape(
        CTX, rows, 128
    )
    third = recv_ref[:, 256:384, :].reshape(length, 128)
    fourth = recv_ref[:, 384:448, :].reshape(length // 2, 128)
    mixed, query_grad, key_grad, value_grad = run(
        fourth[:, :HD], third[:, :HD], third[:, HD:], fourth[:, HD:], place_half_ref[...], 256
    )
    out_ref[:, 256:384, :] = jnp.concatenate([key_grad, value_grad], axis=1).reshape(
        CTX, rows, 128
    )
    out_ref[:, 384:448, :] = jnp.concatenate([mixed, query_grad], axis=1).reshape(
        CTX, rows // 2, 128
    )


def attention(recv, places, where, y, earlier):
    length = places.shape[0]
    halves = pick(places.reshape(CTX, Y_PLACES, length // CTX // Y_PLACES), y, 1).reshape(-1)
    [out] = call(
        attention_kernel,
        [(recv.shape, recv.dtype)],
        [recv, places[None, :], places[:, None], halves[:, None]],
        where,
        "attention",
        0.1,
        earlier=earlier,
    )
    return out


def moment_kernel(where_ref, grads_ref, *refs):
    at = 0
    for which in range(4):
        moment_ref, grad_out, moment_out = refs[which], refs[4 + which], refs[8 + which]
        cols = moment_ref.shape[1]
        grad = grads_ref[0, :, at : at + cols].astype(jnp.float32)
        grad_out[...] = grad
        moment_out[...] = mom_rate * moment_ref[...] + grad
        at += cols


def write_moments(grads, moments, ctx_place):
    rows = moments[0].shape[0] // CTX
    blocks = [pl.BlockSpec((rows, m.shape[1]), lambda i, where: (i, 0)) for m in moments]
    shapes = [jax.ShapeDtypeStruct(m.shape, m.dtype) for m in moments]
    out = pl.pallas_call(
        moment_kernel,
        grid_spec=pltpu.PrefetchScalarGridSpec(
            num_scalar_prefetch=1,
            grid=(CTX,),
            in_specs=[
                pl.BlockSpec((1,) + grads.shape[1:], lambda i, where: (i ^ where[0], 0, 0))
            ]
            + blocks,
            out_specs=blocks + blocks,
        ),
        out_shape=shapes + shapes,
        compiler_params=pltpu.CompilerParams(vmem_limit_bytes=60 * 1024 * 1024),
        cost_estimate=pl.CostEstimate(
            flops=0, bytes_accessed=int(100 * 3.6e6), transcendentals=0
        ),
        name="moments",
    )(ctx_place.reshape(1), grads, *moments)
    return out[:4], out[4:]


def weight_kernel(where_ref, *refs):
    for which in range(4):
        ortho_ref, weight_ref, out_ref = refs[which], refs[4 + which], refs[8 + which]
        cols = weight_ref.shape[1]
        rate = step_rates[which] * math.sqrt(cols)
        out_ref[...] = weight_ref[...] - rate * ortho_ref[0, 0, :, :cols].astype(jnp.float32)


def write_weights(ortho, weights, ctx_place):
    rows = weights[0].shape[0] // CTX
    blocks = [pl.BlockSpec((rows, w.shape[1]), lambda i, where: (i, 0)) for w in weights]

    def source(owner):
        return pl.BlockSpec(
            (1, 1) + ortho.shape[2:], lambda i, where: (owner, i ^ where[0], 0, 0)
        )

    return pl.pallas_call(
        weight_kernel,
        grid_spec=pltpu.PrefetchScalarGridSpec(
            num_scalar_prefetch=1,
            grid=(CTX,),
            in_specs=[source(owner) for owner in OWNERS] + blocks,
            out_specs=blocks,
        ),
        out_shape=[jax.ShapeDtypeStruct(w.shape, w.dtype) for w in weights],
        compiler_params=pltpu.CompilerParams(vmem_limit_bytes=60 * 1024 * 1024),
        name="weights",
    )(ctx_place.reshape(1), *[ortho] * 4, *weights)


def local_fast(
    residual_in,
    cotangent,
    group_order,
    gain_first,
    shift_first,
    gain_second,
    shift_second,
    heads_weight,
    heads_bias,
    output_weight,
    output_bias,
    up_weight,
    up_bias,
    down_weight,
    down_bias,
    heads_moment,
    output_moment,
    up_moment,
    down_moment,
):
    single = jnp.float32
    half = jnp.bfloat16
    ctx_place = lax.axis_index("ctx")
    shard_place = lax.axis_index("fsdp")
    y, z = ctx_place % Y_PLACES, ctx_place // Y_PLACES
    seqs, rows, width = residual_in.shape
    length = rows * CTX
    group = rows // 2
    part = width // SHARDS
    hidden = up_weight.shape[1]
    hidden_part = hidden // SHARDS
    strip = part // CTX

    where = jnp.stack([z, y, shard_place, ctx_place]).astype(jnp.int32)

    [packed] = call(
        pack_kernel,
        [((2 * rows + 16, width), half)],
        [
            residual_in[0],
            cotangent[0],
            jnp.concatenate(
                [
                    gain_first,
                    shift_first,
                    gain_second,
                    shift_second,
                    output_bias,
                    down_bias,
                    heads_bias,
                ]
            )[None],
        ],
        where,
        "pack",
        0.1,
    )
    packs = [packed] + [swap(packed, "fsdp", k) for k in (1, 2)]
    packs.append(swap(packs[2], "fsdp", 1))
    [heads_split] = call(
        heads_split_kernel, [((SHARDS, part, 3 * part), half)], [heads_weight], where, "heads_split", 0.1
    )
    heads_block = exchange(heads_split).reshape(width, 3 * part)
    moments_all = (heads_moment, output_moment, up_moment, down_moment)
    weights_all = (heads_weight, output_weight, up_weight, down_weight)
    strip_moments = [None] * SHARDS
    for which in range(4):
        moment = lax.dynamic_slice_in_dim(moments_all[which], ctx_place * strip, strip, 0)
        strip_moments[OWNERS[which]] = jnp.pad(moment, ((0, 0), (0, hidden - moment.shape[1])))
    mlp_split = call(
        mlp_split_kernel,
        [((part + 2 * strip, 2 * hidden_part), half)] * SHARDS,
        [up_weight, down_weight, jnp.stack(strip_moments)],
        where,
        "mlp_split",
        0.1,
        earlier=[packs[3]],
    )
    mlp_pieces = [mlp_split[0]] + [swap(mlp_split[k], "fsdp", k) for k in range(1, SHARDS)]
    output_block = output_weight.astype(half)
    vectors = sum(p[2 * rows :].astype(single) for p in packs)

    places = slot_places(group_order, 0, length, group)
    query_places = slot_places(group_order, ctx_place * rows, rows, group)
    cosine, sine = rotary_tables(query_places)
    none, rest = jnp.zeros((rows, ROT // 2), single), jnp.zeros((rows, HD - ROT), single)
    turn_cos, turn_high, turn_low = [
        jnp.tile(jnp.concatenate(t, axis=1), (1, 2 * part // HD))
        for t in ([cosine, cosine, rest + 1.0], [none, sine, rest], [-sine, none, rest])
    ]

    first_in, second_in, grad_half, payload, my_normed, inverse = call(
        pre_kernel,
        [
            ((SHARDS * rows, width), half),
            ((SHARDS * rows, width), half),
            ((SHARDS * rows, width), half),
            ((CTX, 3 * rows + rows // 2, 2 * HD), half),
            ((rows, width), single),
            ((rows, 128), single),
        ],
        list(packs) + [heads_block, output_block, turn_cos, turn_high, turn_low],
        where,
        "pre",
        0.1,
    )
    my_inverse = inverse[:, :1]
    sent = exchange(payload, "ctx")
    done = attention(sent, places, where, y, mlp_pieces[2:3])
    back = exchange(done, "ctx")

    mlp_send, mlp_keep, mlp_part, up_sum, second_part = call(
        mlp_kernel,
        [
            ((SHARDS, Z_PLACES, strip, 2 * hidden_part), half),
            ((SHARDS, Z_PLACES, strip, 2 * hidden_part), single),
            ((SHARDS * rows, width), single),
            ((1, hidden_part), single),
            ((SHARDS * rows, width), single),
        ],
        [second_in, grad_half, up_bias.astype(half).astype(single)[None]] + mlp_pieces,
        where,
        "mlp",
        0.1,
        [
            pltpu.VMEM((width, 2 * hidden_part), half),
            pltpu.VMEM((width, 2 * hidden_part), single),
        ],
    )
    mlp_came, mlp_sums = scatter_ctx(mlp_send, mlp_keep, where, "mlp_z")

    send, keep, heads_sum, mine, home = call(
        post_kernel,
        [
            ((SHARDS, Z_PLACES, strip, width), half),
            ((SHARDS, Z_PLACES, strip, width), single),
            ((1, 3 * part), single),
            ((3 * rows, width), single),
            ((SHARDS, 3 * rows, width), half),
        ],
        [back, first_in, grad_half, heads_block, output_block, mlp_part, second_part]
        + [turn_cos, turn_high, turn_low],
        where,
        "post",
        0.1,
        [
            pltpu.VMEM((SHARDS * rows, part), half),
            pltpu.VMEM((SHARDS * rows, 3 * part), half),
            pltpu.VMEM((width, width), single),
        ],
        [mlp_came],
    )
    _, heads_sums = scatter_ctx(send, keep, where, "heads_z")
    home = exchange(home)
    total = mine + jnp.sum(home.astype(single), axis=0)
    block_out = (
        residual_in[0].astype(single) + (total[:rows] + vectors[4] + vectors[5])
    ).astype(half)
    first_delta, second_delta = total[rows : 2 * rows], total[2 * rows :]
    input_grad = (
        cotangent[0]
        + norm_back(first_delta, my_normed, my_inverse, vectors[0])
        + norm_back(second_delta, my_normed, my_inverse, vectors[2])
    )

    heads_sum = lax.dynamic_update_slice(
        jnp.zeros((3, SHARDS, part), single),
        heads_sum.reshape(3, 1, part),
        (0, shard_place, 0),
    ).reshape(3 * width)
    up_sum = lax.dynamic_update_slice(
        jnp.zeros((hidden,), single), up_sum[0], (shard_place * hidden_part,)
    )
    sums = jnp.concatenate(
        [
            jnp.sum(first_delta * my_normed, axis=0),
            jnp.sum(first_delta, axis=0),
            jnp.sum(second_delta * my_normed, axis=0),
            jnp.sum(second_delta, axis=0),
            jnp.sum(cotangent[0], axis=0),
            heads_sum,
            up_sum,
        ]
    ).reshape(-1, 128)
    sums = sums + sum(swap(sums, "fsdp", k) for k in range(1, SHARDS))

    strips, owned, output_strip = call(
        strip_kernel,
        [
            ((SHARDS, strip, 2 * hidden_part + 3 * part), half),
            ((SHARDS, SHARDS, strip, width), half),
            ((strip, width), single),
        ],
        heads_sums + mlp_sums,
        where,
        "strip",
        0.1,
        earlier=[home],
    )
    owned, strips = call(
        owned_kernel,
        [((SHARDS, strip, hidden), half), (strips.shape, half)],
        [exchange(owned), strips] + mlp_pieces,
        where,
        "owned",
        0.1,
    )
    along = [owned, swap(owned, "ctx", Y_PLACES), swap(owned, "ctx", 2 * Y_PLACES)]
    first, second = swap(owned, "ctx", 1), swap(along[1], "ctx", 1)
    [again] = call(
        copy_kernel, [(owned.shape, half)], [owned], where, "again", 0.1, earlier=[second, along[2]]
    )
    along.append(swap(again, "ctx", 3 * Y_PLACES))
    third, fourth = swap(along[2], "ctx", 1), swap(along[3], "ctx", 1)
    pieces = [owned, first, along[1], second, along[2], third, along[3], fourth]
    grads, sums = call(
        grads_kernel,
        [((strip, 4 * width + 2 * hidden), half), (sums.shape, single)],
        [exchange(strips), output_strip, sums],
        where,
        "grads",
        0.1,
        earlier=pieces[1:],
    )
    grads_along = gather_z(grads)

    sums = sums + swap(sums, "ctx", 1)
    ortho, sums = newton(pieces, sums, where, [grads], grads_along[1:])
    sums = sums + sum(swap(sums, "ctx", Y_PLACES * k) for k in range(1, Z_PLACES))
    sums = sums.reshape(-1)
    arrived = exchange(ortho)
    new_weights = write_weights(arrived, weights_all, ctx_place)
    full_grads, new_moments = write_moments(
        jnp.stack(gather_y(grads_along)), moments_all, ctx_place
    )
    pieces = [sums[i * width : (i + 1) * width] for i in range(5)]
    heads_total = sums[5 * width : 8 * width]
    up_total = sums[8 * width :]
    vector_values = (
        gain_first,
        shift_first,
        gain_second,
        shift_second,
        heads_bias,
        output_bias,
        up_bias,
        down_bias,
    )
    vector_grads = (
        pieces[0],
        pieces[1],
        pieces[2],
        pieces[3],
        heads_total,
        pieces[4],
        up_total,
        pieces[4],
    )
    grad_shards = []
    new_shards = []
    for which in range(8):
        size_here = vector_values[which].shape[0]
        whole_grad = vector_grads[which]
        shard = lax.dynamic_slice_in_dim(whole_grad, shard_place * size_here, size_here)
        grad_shards.append(shard)
        new_shards.append(
            vector_values[which]
            - vector_rate * shard * lax.rsqrt(jnp.mean(whole_grad * whole_grad) + norm_eps)
        )
    return (
        block_out[None],
        input_grad[None],
        grad_shards[0],
        grad_shards[1],
        grad_shards[2],
        grad_shards[3],
        full_grads[0],
        grad_shards[4],
        full_grads[1],
        grad_shards[5],
        full_grads[2],
        grad_shards[6],
        full_grads[3],
        grad_shards[7],
        new_shards[0],
        new_shards[1],
        new_shards[2],
        new_shards[3],
        new_weights[0],
        new_shards[4],
        new_weights[1],
        new_shards[5],
        new_weights[2],
        new_shards[6],
        new_weights[3],
        new_shards[7],
        new_moments[0],
        new_moments[1],
        new_moments[2],
        new_moments[3],
    )


def solution(mesh):
    in_specs = (
        P("fsdp", "ctx", None),
        P("fsdp", "ctx", None),
        P(),
        P("fsdp"),
        P("fsdp"),
        P("fsdp"),
        P("fsdp"),
        P("fsdp", None),
        P("fsdp"),
        P("fsdp", None),
        P("fsdp"),
        P("fsdp", None),
        P("fsdp"),
        P("fsdp", None),
        P("fsdp"),
        P("fsdp", None),
        P("fsdp", None),
        P("fsdp", None),
        P("fsdp", None),
    )
    out_specs = (
        P("fsdp", "ctx", None),
        P("fsdp", "ctx", None),
        P("fsdp"),
        P("fsdp"),
        P("fsdp"),
        P("fsdp"),
        P("fsdp", None),
        P("fsdp"),
        P("fsdp", None),
        P("fsdp"),
        P("fsdp", None),
        P("fsdp"),
        P("fsdp", None),
        P("fsdp"),
        P("fsdp"),
        P("fsdp"),
        P("fsdp"),
        P("fsdp"),
        P("fsdp", None),
        P("fsdp"),
        P("fsdp", None),
        P("fsdp"),
        P("fsdp", None),
        P("fsdp"),
        P("fsdp", None),
        P("fsdp"),
        P("fsdp", None),
        P("fsdp", None),
        P("fsdp", None),
        P("fsdp", None),
    )
    sizes = dict(mesh.shape)
    fits = sizes["ctx"] == 8 and sizes["fsdp"] == 4
    chosen = local_fast if fits else local_general
    return jax.shard_map(chosen, mesh=mesh, in_specs=in_specs, out_specs=out_specs, check_vma=False)
```
